32 devices in a mesh: dp: 4 (over y, core), fsdp: 8 (over z, x).
Axes of the slice: x: 2, y: 2, z: 4, core: 2. Of those that a mesh axis runs over, the one named last changes fastest.
Arguments:
- inputs: bfloat16 [32, 24, 28, 512], P(('dp', 'fsdp')), may hold values from -9 to 9
- heights: int32 [32], P(('dp', 'fsdp')), may hold values from 18 to 24, as said below
- widths: int32 [32], P(('dp', 'fsdp')), may hold values from 21 to 28, as said below
- conv_weights: bfloat16 [3, 4608, 512], P(None, 'fsdp', 'dp'), may hold values from -0.09375 to 0.09375
- affine_scale: float32 [3, 512], replicated, may hold values from 1 to 2.5
- affine_shift: float32 [3, 512], replicated, may hold values from -1.2 to 1.2
- tap_scales: bfloat16 [3, 512], P(None, 'fsdp'), may hold values from 0.25 to 1.75
- head_weights: bfloat16 [3, 512, 1792], P(None, 'fsdp', 'dp'), may hold values from -0.15309311 to 0.15309311
- trunk_cot: bfloat16 [32, 24, 28, 512], P(('dp', 'fsdp')), may hold values from -3 to 3
- heads_cot: bfloat16 [32, 24, 28, 1792], P(('dp', 'fsdp')), may hold values from -6 to 6
Outputs:
- trunk_out: bfloat16 [32, 24, 28, 512], P(('dp', 'fsdp'))
- heads_out: bfloat16 [32, 24, 28, 1792], P(('dp', 'fsdp'))
- input_grad: bfloat16 [32, 24, 28, 512], P(('dp', 'fsdp'))
- conv_grad: float32 [3, 4608, 512], P(None, 'fsdp', 'dp')
- scale_grad: float32 [3, 512], P(None, 'fsdp')
- head_grad: float32 [3, 512, 1792], P(None, 'fsdp', 'dp')
- rms: float32 [5], replicated
The draws below stay inside these ranges and needn't reach their ends.
Inputs may be any that keep to these rules, and one draw needn't show every extreme that they name: `heights`: some image has 24 valid rows and some 18. `widths`: some image has 28 valid columns and some 21.
All inputs are finite; a program needn't handle non-finite values.
Results may differ from the reference program's by a relative error of at most 0.015.
Values may be sent and summed in bfloat16 or wider, within the bound.
A program may use at most 192 MiB of HBM per device.

```python
import math
import jax
import jax.numpy as jnp
from jax import lax

CH = 512
LAYERS = 3
BH = 24
BW = 28
HO = 1792
IMAGES = 32
HMIN = 18
WMIN = 21


def extent_draw(key, smallest, largest):
    key_first, key_second, key_third = jax.random.split(key, 3)
    values = jax.random.randint(key_first, (IMAGES,), smallest, largest + 1)
    high_index = jax.random.randint(key_second, (), 0, IMAGES)
    other_index = (high_index + 1 + jax.random.randint(key_third, (), 0, IMAGES - 1)) % IMAGES
    return values.at[high_index].set(largest).at[other_index].set(smallest).astype(jnp.int32)


def draw_heights(key, part):
    key = jax.random.fold_in(key, 11)
    return extent_draw(key, HMIN, BH)


def draw_widths(key, part):
    key = jax.random.fold_in(key, 12)
    return extent_draw(key, WMIN, BW)


def draw_inputs(key, part):
    key = jax.random.fold_in(key, 13)
    key_first = jax.random.fold_in(key, 0)
    shape = (IMAGES, BH, BW, CH)
    base = jnp.clip(jax.random.normal(key_first, shape, jnp.float32), -5.0, 5.0)
    ramp = 0.6 + 1.2 * jnp.arange(IMAGES, dtype=jnp.float32) / max(IMAGES - 1, 1)
    return (base * ramp[:, None, None, None]).astype(jnp.bfloat16)


def draw_head_weights(key, part):
    key = jax.random.fold_in(key, 14)
    key_first, key_second = jax.random.split(key)
    shape = (LAYERS, CH, HO)
    base = jnp.clip(jax.random.normal(key_first, shape, jnp.float32), -5.0, 5.0)
    common = 0.12
    shared = jnp.clip(jax.random.normal(key_second, (LAYERS, 1, HO), jnp.float32), -4.0, 4.0)
    return ((base + common * shared) * (LAYERS * CH) ** (-0.5)).astype(jnp.bfloat16)


def raised(entries, stream_key, source, target, parts, factor):
    owner, partner = [(jnp.arange(entries.shape[position]) // (entries.shape[position] // parts)).reshape([-1 if axis == position else 1 for axis in range(entries.ndim)]) for position in (source, target)]
    chosen = jax.random.permutation(stream_key, parts)[partner]
    strong = (owner == chosen) | (owner == (partner + parts // 2) % parts)
    return jnp.where(strong, factor * entries, entries)


def level_of(rng, shape, cuts, least, high):
    factor_of, own = 1.0, jax.random.fold_in(rng, 6)
    for axis_at, blocks in cuts:
        draws = jnp.exp(jax.random.uniform(jax.random.fold_in(own, axis_at), (blocks,), jnp.float32, least / len(cuts), high / len(cuts)))
        factor_of = factor_of * jnp.repeat(draws, shape[axis_at] // blocks).reshape([-1 if axis == axis_at else 1 for axis in range(len(shape))])
    return factor_of


def bell_draw(rng, dims, deviation, reach, shards=(), kind=jnp.bfloat16):
    gain = level_of(rng, dims, shards, -0.22, 0.18) if shards else 1.0
    result = jax.random.normal(rng, dims, jnp.float32) * deviation * gain
    return jnp.minimum(jnp.maximum(result, -reach), reach).astype(kind)


def heavy_noise(rng, dims, width, most, cuts, heavy, kind=jnp.bfloat16):
    drawn = width * jax.random.normal(rng, dims, jnp.float32)
    if cuts:
        drawn = drawn * level_of(rng, dims, cuts, -0.22, 0.18)
    return jnp.clip(raised(drawn, jax.random.fold_in(rng, 3), *heavy), -most, most).astype(kind)


def setup_inputs(seed: int = 0) -> dict:
    arg_keys = jax.random.split(jax.random.key(seed), 11)
    return {
        "inputs": draw_inputs(jax.random.fold_in(arg_keys[10], 71), 0),
        "heights": draw_heights(jax.random.fold_in(arg_keys[10], 71), 0),
        "widths": draw_widths(jax.random.fold_in(arg_keys[10], 71), 0),
        "conv_weights": bell_draw(arg_keys[3], (LAYERS, 9 * CH, CH), (9 * CH) ** -0.5, 0.09375, ((1, 8), (2, 4))),
        "affine_scale": jnp.clip(jnp.exp(jax.random.uniform(arg_keys[4], (LAYERS, CH), jnp.float32, math.log(1.0), math.log(2.5))), 1.0, 2.5),
        "affine_shift": bell_draw(arg_keys[5], (LAYERS, CH), 0.3, 1.2, (), jnp.float32),
        "tap_scales": jnp.clip(1.0 + 0.15 * jax.random.normal(arg_keys[6], (LAYERS, CH), jnp.float32), 0.25, 1.75).astype(jnp.bfloat16),
        "head_weights": draw_head_weights(jax.random.fold_in(arg_keys[10], 71), 0),
        "trunk_cot": heavy_noise(arg_keys[8], (IMAGES, BH, BW, CH), 0.5, 3.0, ((0, 32),), (0, 3, 32, 2.75)),
        "heads_cot": heavy_noise(arg_keys[9], (IMAGES, BH, BW, HO), 1.0, 6.0, ((0, 32),), (0, 3, 32, 2.75)),
    }


@jax.custom_vjp
def low(v):
    return lax.optimization_barrier(v.astype(jnp.bfloat16)).astype(jnp.float32)

@jax.custom_vjp
def low_back(v):
    return v

def low_keep(v):
    return (low(v), None)

def low_pass(kept, grad):
    return (grad,)

def back_keep(v):
    return (v, None)

def back_low(kept, grad):
    return (low(grad),)
low.defvjp(low_keep, low_pass)
low_back.defvjp(back_keep, back_low)

def patches(feature):
    height = feature.shape[1]
    breadth = feature.shape[2]
    padded = jnp.pad(feature, ((0, 0), (1, 1), (1, 1), (0, 0)))
    pieces = [padded[:, down_step:down_step + height, side_step:side_step + breadth, :] for down_step in range(3) for side_step in range(3)]
    return jnp.concatenate(pieces, axis=-1)

def forward(images_float, masks, conv_mats, affine_scale, affine_shift, scale_mats, head_mats):
    feature = images_float * masks
    squares = [jnp.sum(feature * feature)]
    summed = jnp.zeros(feature.shape[:3] + (head_mats.shape[2],), jnp.float32)
    for layer_index in range(LAYERS):
        stacked = patches(low(feature))
        linear = jnp.einsum('ghwk,kc->ghwc', stacked, conv_mats[layer_index], precision=lax.Precision.HIGHEST)
        linear = low_back(linear)
        feature = masks * jax.nn.gelu(linear * affine_scale[layer_index] + affine_shift[layer_index])
        squares.append(jnp.sum(feature * feature))
        normed = feature * lax.rsqrt(lax.optimization_barrier(jnp.mean(feature * feature, axis=-1, keepdims=True)) + 1e-05) * scale_mats[layer_index]
        summed = summed + jnp.einsum('ghwc,co->ghwo', low(normed), head_mats[layer_index], precision=lax.Precision.HIGHEST)
    squares.append(jnp.sum(summed * summed))
    return ((feature, summed), jnp.stack(squares))

def reference(inputs, heights, widths, conv_weights, affine_scale, affine_shift, tap_scales, head_weights, trunk_cot, heads_cot):
    group_size = 16 if IMAGES % 16 == 0 else 1
    step_count = IMAGES // group_size
    row_ids = jnp.arange(BH, dtype=jnp.int32)
    col_ids = jnp.arange(BW, dtype=jnp.int32)
    valid = (row_ids[None, :, None] < heights[:, None, None]) & (col_ids[None, None, :] < widths[:, None, None])
    valid_mask = jnp.where(valid, 1.0, 0.0).astype(jnp.float32)[..., None]
    conv_float = conv_weights.astype(jnp.float32)
    scale_float = tap_scales.astype(jnp.float32)
    head_float = head_weights.astype(jnp.float32)

    def one_group(running, batch_slice):
        images, masks, cot_trunk, cot_heads = batch_slice

        def wrapped(images_float, conv_mats, scale_mats, head_mats):
            return forward(images_float, masks, conv_mats, affine_scale, affine_shift, scale_mats, head_mats)
        outputs, pullback, squares = jax.vjp(wrapped, images.astype(jnp.float32), conv_float, scale_float, head_float, has_aux=True)
        grad_in, grad_conv, grad_scale, grad_head = pullback((cot_trunk.astype(jnp.float32), cot_heads.astype(jnp.float32)))
        running = (running[0] + grad_conv, running[1] + grad_scale, running[2] + grad_head, running[3] + squares)
        return (running, (outputs[0].astype(jnp.bfloat16), outputs[1].astype(jnp.bfloat16), grad_in.astype(jnp.bfloat16)))
    start = (jnp.zeros((LAYERS, 9 * CH, CH), jnp.float32), jnp.zeros((LAYERS, CH), jnp.float32), jnp.zeros((LAYERS, CH, HO), jnp.float32), jnp.zeros((LAYERS + 2,), jnp.float32))
    batches = (inputs.reshape((step_count, group_size, BH, BW, CH)), valid_mask.reshape((step_count, group_size, BH, BW, 1)), trunk_cot.reshape((step_count, group_size, BH, BW, CH)), heads_cot.reshape((step_count, group_size, BH, BW, HO)))
    running, results = lax.scan(one_group, start, batches)
    conv_grad, scale_grad, head_grad, squares = running
    trunk_out = results[0].reshape((IMAGES, BH, BW, CH))
    heads_out = results[1].reshape((IMAGES, BH, BW, HO))
    input_grad = results[2].reshape((IMAGES, BH, BW, CH))
    pixels = jnp.sum(valid_mask)
    divisors = jnp.array([CH] * (LAYERS + 1) + [HO], jnp.float32)
    rms = jnp.sqrt(squares / (pixels * divisors))
    return (trunk_out, heads_out, input_grad, conv_grad, scale_grad, head_grad, rms)
```

```python
from functools import partial

import jax
import jax.numpy as jnp
from jax import lax
from jax.experimental import pallas as pl
from jax.experimental.pallas import tpu as pltpu
from jax.sharding import PartitionSpec as P

MESH = pl.DeviceIdType.MESH
F32, BF = jnp.float32, jnp.bfloat16

CONV_UNIT, HEAD_UNIT = 576, 256
UNITS = (CONV_UNIT,) * 3 + (HEAD_UNIT,) * 3
BASES = tuple(32 * sum(UNITS[:p]) for p in range(6))
ROWS = 32 * sum(UNITS)
HEAD_OF = (5, 4, 3)
SLOTS = 17
PIX, WIDE = 768, 32


ORDER = (
    ("start",),
    ("e0", 0),
    ("e0", 1),
    ("zj", 0, 1),
    ("prep_in",),
    ("ft", 0),
    ("prep_cot",),
    ("zj", 1, 1),
    ("xd", 0, 0),
    ("yd", 0, 0),
    ("zj", 0, 2),
    ("zj", 1, 2),
    ("e0", 2),
    ("xd", 0, 1),
    ("yd", 0, 1),
    ("zj", 0, 3),
    ("zj", 1, 3),
    ("zj", 2, 1),
    ("xd", 0, 2),
    ("yd", 0, 2),
    ("xd", 0, 3),
    ("zj", 2, 2),
    ("yd", 0, 3),
    ("zj", 2, 3),
    ("xf", 0, 0),
    ("yf", 0, 0),
    ("xd", 1, 0),
    ("yd", 1, 0),
    ("e0", 3),
    ("xd", 1, 1),
    ("yd", 1, 1),
    ("zj", 3, 1),
    ("zj", 3, 2),
    ("xd", 1, 2),
    ("yd", 1, 2),
    ("zj", 3, 3),
    ("xf", 0, 1),
    ("xd", 1, 3),
    ("yf", 0, 1),
    ("yd", 1, 3),
    ("e0", 4),
    ("zj", 4, 1),
    ("pw", 0),
    ("conv", 0, 0),
    ("conv", 0, 1),
    ("conv", 0, 2),
    ("act", 0),
    ("ft", 1),
    ("nt", 0),
    ("head_grads", 0, 0),
    ("head_grads", 0, 1),
    ("zj", 4, 2),
    ("xf", 1, 0),
    ("yf", 1, 0),
    ("zj", 4, 3),
    ("e0", 5),
    ("xd", 2, 0),
    ("yd", 2, 0),
    ("zj", 5, 1),
    ("xd", 2, 1),
    ("yd", 2, 1),
    ("zj", 5, 2),
    ("zj", 5, 3),
    ("xd", 2, 2),
    ("yd", 2, 2),
    ("xf", 1, 1),
    ("xd", 2, 3),
    ("yf", 1, 1),
    ("yd", 2, 3),
    ("pw", 1),
    ("conv", 1, 0),
    ("conv", 1, 1),
    ("conv", 1, 2),
    ("act", 1),
    ("ft", 2),
    ("nt", 1),
    ("head_grads", 1, 0),
    ("head_grads", 1, 1),
    ("xf", 2, 0),
    ("yf", 2, 0),
    ("xd", 3, 0),
    ("yd", 3, 0),
    ("xd", 3, 1),
    ("yd", 3, 1),
    ("xd", 3, 2),
    ("yd", 3, 2),
    ("xd", 3, 3),
    ("yd", 3, 3),
    ("xf", 3, 0),
    ("yf", 3, 0),
    ("xd", 4, 0),
    ("yd", 4, 0),
    ("xd", 4, 1),
    ("yd", 4, 1),
    ("xf", 2, 1),
    ("xd", 4, 2),
    ("yf", 2, 1),
    ("yd", 4, 2),
    ("xd", 4, 3),
    ("xf", 3, 1),
    ("yd", 4, 3),
    ("yf", 3, 1),
    ("pw", 2),
    ("conv", 2, 0),
    ("conv", 2, 1),
    ("conv", 2, 2),
    ("act", 2),
    ("nt", 2),
    ("head_grads", 2, 0),
    ("head_grads", 2, 1),
    ("trunk_cot",),
    ("xf", 4, 0),
    ("yf", 4, 0),
    ("pw", 3),
    ("dtap", 2),
    ("xd", 5, 0),
    ("yd", 5, 0),
    ("xd", 5, 1),
    ("yd", 5, 1),
    ("xd", 5, 2),
    ("yd", 5, 2),
    ("xd", 5, 3),
    ("xf", 4, 1),
    ("yd", 5, 3),
    ("yf", 4, 1),
    ("xf", 5, 0),
    ("yf", 5, 0),
    ("pw", 4),
    ("dtap", 1),
    ("xf", 5, 1),
    ("yf", 5, 1),
    ("pw", 5),
    ("dtap", 0),
    ("joined", 0),
    ("joined", 1),
    ("m0",),
    ("m1", 0),
    ("m1", 1),
    ("m1", 2),
    ("m2", 1),
    ("m2", 2),
    ("m2", 3),
    ("m3",),
    ("s1", 3),
    ("s1", 4),
    ("s1", 5),
    ("dlinear", 2),
    ("conv_back", 2, 0),
    ("conv_back", 2, 1),
    ("conv_back", 2, 2),
    ("conv_grads", 2, 0),
    ("conv_grads", 2, 1),
    ("conv_grads", 2, 2),
    ("s1", 2),
    ("s2a", 3),
    ("s2b", 3),
    ("s3a", 3),
    ("s3b", 3),
    ("zu", 3, 3),
    ("zd", 3, 0),
    ("zu", 3, 2),
    ("zd", 3, 1),
    ("fin", 3),
    ("s2a", 4),
    ("s2b", 4),
    ("s3a", 4),
    ("s3b", 4),
    ("zu", 4, 3),
    ("zd", 4, 0),
    ("zu", 4, 2),
    ("zd", 4, 1),
    ("fin", 4),
    ("s2a", 5),
    ("s2b", 5),
    ("s3a", 5),
    ("s3b", 5),
    ("zu", 5, 3),
    ("zd", 5, 0),
    ("zu", 5, 2),
    ("zd", 5, 1),
    ("fin", 5),
    ("t0",),
    ("t1",),
    ("t2",),
    ("dlinear", 1),
    ("conv_back", 1, 0),
    ("conv_back", 1, 1),
    ("conv_back", 1, 2),
    ("conv_grads", 1, 0),
    ("conv_grads", 1, 1),
    ("conv_grads", 1, 2),
    ("s1", 1),
    ("s2a", 2),
    ("s2b", 2),
    ("s3a", 2),
    ("s3b", 2),
    ("zu", 2, 3),
    ("zd", 2, 0),
    ("zu", 2, 2),
    ("zd", 2, 1),
    ("fin", 2),
    ("dlinear", 0),
    ("conv_back", 0, 0),
    ("conv_back", 0, 1),
    ("conv_back", 0, 2),
    ("image_grad",),
    ("conv_grads", 0, 0),
    ("conv_grads", 0, 1),
    ("conv_grads", 0, 2),
    ("s1", 0),
    ("s2a", 1),
    ("s2b", 1),
    ("s3a", 1),
    ("s3b", 1),
    ("zu", 1, 3),
    ("zd", 1, 0),
    ("zu", 1, 2),
    ("zd", 1, 1),
    ("fin", 1),
    ("s2a", 0),
    ("s2b", 0),
    ("s3a", 0),
    ("s3b", 0),
    ("zu", 0, 3),
    ("zd", 0, 0),
    ("zu", 0, 2),
    ("zd", 0, 1),
    ("fin", 0),
    ("finish",),
)


def kernel(
    order,
    conv_in,
    head_in,
    raw_in,
    scale_in,
    gain_in,
    offset_in,
    height_in,
    width_in,
    image_in,
    trunk_in,
    cot_in,
    trunk_out,
    heads_out,
    image_out,
    conv_out,
    head_out,
    scale_out,
    rms_out,
    W,
    F3,
    FT,
    FTP,
    NT,
    NTP,
    N,
    GP,
    DT,
    RN,
    COT,
    COTP,
    STG,
    IMG,
    ACC,
    D3P,
    GC2,
    GH,
    RC,
    RH,
    OUTC,
    OUTH,
    SQ,
    LB,
    MR,
    ZB,
    SB,
    SR,
    ag_recv,
    ag_send,
    load_sem,
    rs_recv,
    rs_send,
    pair_recv,
    pair_send,
    stage_sem,
    out_sem,
    small_recv,
    small_send,
    credit,
):
    dpi, fsi = lax.axis_index("dp"), lax.axis_index("fsdp")
    y, c, z, x = dpi // 2, dpi % 2, fsi // 2, fsi % 2

    def dev(yy, cc, zz, xx):
        return (yy * 2 + cc, zz * 2 + xx)

    xn, yn, pn = dev(y, c, z, 1 - x), dev(1 - y, c, z, x), dev(y, 1 - c, z, x)
    up, dn = dev(y, c, jnp.minimum(z + 1, 3), x), dev(y, c, jnp.maximum(z - 1, 0), x)
    sig = [z, z + 1 - 2 * (z % 2), jnp.where(z < 2, 2, 1), jnp.where(z < 2, 3, 0)]
    height, width = height_in[0], width_in[0]

    def when(cond, fn):
        pl.when(cond)(fn)

    def remote(src, dst, send, recv, t):
        return pltpu.make_async_remote_copy(
            src_ref=src, dst_ref=dst, send_sem=send, recv_sem=recv, device_id=t, device_id_type=MESH
        )

    def row(p, yy, cc, s, xx):
        return pl.multiple_of(BASES[p] + ((2 * yy + cc) * 8 + 2 * s + xx) * UNITS[p], 64)

    def ag(p, r, si, ri, t, n=1):
        part = W.at[pl.ds(r, UNITS[p] * n)]
        return pltpu.make_async_remote_copy(
            src_ref=part,
            dst_ref=part,
            send_sem=ag_send.at[p, si],
            recv_sem=ag_recv.at[p, ri],
            device_id=t,
            device_id_type=MESH,
        )

    def ag_start(p, r, si, ri, t):
        ag(p, r, si, ri, t).start()

    def ag_wait(p, ri, n=1):
        ag(p, BASES[p], 0, ri, xn, n).wait_recv()

    def pair(p, r, q):
        ag_start(p, r, 24 + q, 20 + q, pn)

    def direct(p, s, r):
        ag_start(p, r, 8 + s, 4 + s, xn)
        ag_start(p, r, 12 + s, 8 + s, yn)
        pair(p, r, 0)

    def load(p):
        src = conv_in.at[p] if p < 3 else head_in.at[5 - p]
        r = row(p, y, c, z, x)
        return pltpu.make_async_copy(src, W.at[pl.ds(r, UNITS[p])], load_sem.at[p])

    def e0(p):
        r = row(p, y, c, z, x)
        load(p).wait()
        when(z < 3, lambda: ag_start(p, r, z, z, up))
        when(z > 0, lambda: ag_start(p, r, 4 + z, z, dn))
        direct(p, z, r)

    def zj(p, j):
        s = sig[j]
        r = row(p, y, c, s, x)
        ag_wait(p, s)
        when((s < z) & (z < 3), lambda: ag_start(p, r, s, s, up))
        when((s > z) & (z > 0), lambda: ag_start(p, r, 4 + s, s, dn))
        direct(p, s, r)

    def xd(p, j):
        s = sig[j]
        r = row(p, y, c, s, 1 - x)
        ag_wait(p, 4 + s)
        when(s % 2 == 0, lambda: ag_start(p, r, 20 + s, 16 + s, yn))
        pair(p, r, 1)

    def yd(p, j):
        s = sig[j]
        r = row(p, 1 - y, c, s, x)
        ag_wait(p, 8 + s)
        when(s % 2 == 1, lambda: ag_start(p, r, 16 + s, 12 + s, xn))
        pair(p, r, 2)

    def yf(p, k):
        s = jnp.where(z < 2, 2 * k, 2 - 2 * k)
        ag_wait(p, 16 + s)
        pair(p, row(p, 1 - y, c, s, 1 - x), 3)

    def xf(p, k):
        s = jnp.where(z < 2, 1 + 2 * k, 3 - 2 * k)
        ag_wait(p, 12 + s)
        pair(p, row(p, 1 - y, c, s, 1 - x), 3)

    def pw(p):
        for q in range(4):
            ag_wait(p, 20 + q, 4)

    def ag_end(p):
        def done(si, n=1):
            ag(p, BASES[p], si, 0, xn, n).wait_send()

        for s in range(4):
            when((z < 3) & (s <= z), lambda: done(s))
            when((z > 0) & (s >= z), lambda: done(4 + s))
            done(8 + s)
            done(12 + s)
            done(16 + s if s % 2 else 20 + s)
            done(24 + s, 4)

    def grads(p):
        if p == 2:
            return GC2, 0
        if p < 2:
            return W, BASES[2] + (1 - p) * 16 * CONV_UNIT
        return GH, (p - 3) * 16 * HEAD_UNIT

    def grow(p, yy, s, xx):
        return pl.multiple_of(grads(p)[1] + (yy * 8 + 2 * s + xx) * UNITS[p], 64)

    def landing(p):
        if p < 3:
            return RC, (p % 2) * SLOTS * CONV_UNIT
        return RH, (p - 3) * SLOTS * HEAD_UNIT

    def slot(p, k):
        return pl.multiple_of(landing(p)[1] + k * UNITS[p], 64)

    def rs(p, r, k, si, ri, t, n=1):
        u = UNITS[p] * n
        return pltpu.make_async_remote_copy(
            src_ref=grads(p)[0].at[pl.ds(r, u)],
            dst_ref=landing(p)[0].at[pl.ds(slot(p, k), u)],
            send_sem=rs_send.at[p, si],
            recv_sem=rs_recv.at[p, ri],
            device_id=t,
            device_id_type=MESH,
        )

    def rs_start(p, r, k, i, t):
        rs(p, r, k, i, i, t).start()

    def rs_wait(p, ri, n=1):
        rs(p, grads(p)[1], 0, 0, ri, xn, n).wait_recv()

    def took(p, k):
        return landing(p)[0][pl.ds(slot(p, k), UNITS[p]), :].astype(F32)

    def add(p, r, ks):
        ref = grads(p)[0]
        total = ref[pl.ds(r, UNITS[p]), :].astype(F32)
        for k in ks:
            total = total + took(p, k)
        ref[pl.ds(r, UNITS[p]), :] = total.astype(BF)

    def s1(p):
        if p == 0:
            pl.semaphore_wait(credit.at[0], 1)
            pl.semaphore_wait(credit.at[1], 1)
        for s in (0, 2):
            rs_start(p, grow(p, 1 - y, s, 1 - x), s // 2, 0, yn)
        for s in (1, 3):
            rs_start(p, grow(p, 1 - y, s, 1 - x), 2 + s // 2, 1, xn)
        for s in (1, 3):
            rs_start(p, grow(p, y, s, 1 - x), 4 + s, 2, xn)
        for s in (0, 2):
            rs_start(p, grow(p, 1 - y, s, x), 8 + s, 4, yn)

    def s2a(p):
        rs_wait(p, 0, 2)
        for s in (0, 2):
            r = grow(p, y, s, 1 - x)
            add(p, r, (s // 2,))
            rs_start(p, r, 4 + s, 3, xn)

    def s2b(p):
        rs_wait(p, 1, 2)
        for s in (1, 3):
            r = grow(p, 1 - y, s, x)
            add(p, r, (2 + s // 2,))
            rs_start(p, r, 8 + s, 5, yn)

    def s3a(p):
        rs_wait(p, 2, 2)
        rs_wait(p, 4, 2)
        for s in range(4):
            add(p, grow(p, y, s, x), (4 + s,) if s % 2 else (8 + s,))

    def rs_up(p, t):
        rs_start(p, grow(p, y, t, x), 12 + t, 6 + t, up)

    def rs_down(p, t):
        rs_start(p, grow(p, y, t, x), 12 + jnp.where(t == z - 1, 4, t), 10 + t, dn)

    def s3b(p):
        rs_wait(p, 3, 2)
        rs_wait(p, 5, 2)
        if p == 0:
            when(z < 3, lambda: pl.semaphore_wait(credit.at[2], 1))
            when(z > 0, lambda: pl.semaphore_wait(credit.at[3], 1))

        for s in range(4):
            add(p, grow(p, y, s, x), (8 + s,) if s % 2 else (4 + s,))

        @pl.when(z == 0)
        def _():
            for t in (3, 2, 1):
                rs_up(p, t)

        @pl.when(z == 3)
        def _():
            for t in (0, 1, 2):
                rs_down(p, t)

    def zu(p, t):
        @pl.when((z > 0) & (z < t))
        def _():
            rs_wait(p, 6 + t)
            add(p, grow(p, y, t, x), (12 + t,))
            rs_up(p, t)

    def zd(p, t):
        @pl.when((z < 3) & (z > t))
        def _():
            rs_wait(p, 10 + t)
            add(p, grow(p, y, t, x), (12 + t,))
            rs_down(p, t)

    def fin(p):
        ref = grads(p)[0]
        out = OUTC.at[p] if p < 3 else OUTH.at[5 - p]
        out[...] = ref[pl.ds(grow(p, y, z, x), UNITS[p]), :].astype(F32)

        @pl.when(z > 0)
        def _():
            rs_wait(p, 6 + z)
            out[...] += took(p, 12 + z)

        @pl.when(z < 3)
        def _():
            rs_wait(p, 10 + z)
            out[...] += took(p, 16)

        if p == 2:
            for i, t in enumerate((xn, yn)):
                pl.semaphore_signal(credit.at[i], inc=1, device_id=t, device_id_type=MESH)

            @pl.when(z > 0)
            def _():
                pl.semaphore_signal(credit.at[2], inc=1, device_id=dn, device_id_type=MESH)

            @pl.when(z < 3)
            def _():
                pl.semaphore_signal(credit.at[3], inc=1, device_id=up, device_id_type=MESH)

        if p < 3:
            pltpu.make_async_copy(OUTC.at[p], conv_out.at[p], out_sem.at[p]).start()
            return
        layer = 5 - p
        total = jnp.zeros((64, 1), F32)
        for t in range(4):
            rows = pl.ds(64 * t, 64)
            v = out[rows, :]
            total = total + jnp.sum(v * raw_in[layer, rows, :].astype(F32), axis=1, keepdims=True)
            out[rows, :] = v * scale_in[layer]
        SB[0, :, layer : layer + 1] = total
        pltpu.make_async_copy(OUTH.at[layer], head_out.at[layer], out_sem.at[p]).start()

    def rs_end(p):
        def done(si, n=1):
            rs(p, grads(p)[1], 0, si, 0, xn, n).wait_send()

        for i in range(6):
            done(i, 2)
        for t in range(4):
            when((z < 3) & (z < t), lambda t=t: done(6 + t))
            when((z > 0) & (z > t), lambda t=t: done(10 + t))
        if p < 3:
            pltpu.make_async_copy(OUTC.at[p], conv_out.at[p], out_sem.at[p]).wait()
        else:
            pltpu.make_async_copy(OUTH.at[5 - p], head_out.at[5 - p], out_sem.at[p]).wait()

    def share(i, dst_of, src_of, parts):
        return [
            remote(src_of(k), dst_of(k), pair_send.at[i], pair_recv.at[i], pn) for k in range(parts)
        ]

    def share_ft(layer):
        return remote(FT.at[layer], FTP.at[layer], pair_send.at[layer], pair_recv.at[layer], pn)

    def share_nt(layer):
        i = 3 + layer
        return remote(NT, NTP.at[layer % 2], pair_send.at[i], pair_recv.at[i], pn)

    def share_cot(k):
        src = COT.at[pl.ds(7 * k + 3 * (1 - c), 4)]
        return remote(src, COTP.at[k], pair_send.at[6 + k], pair_recv.at[6 + k], pn)

    def share_d(layer, k):
        i = 8 + 2 * layer + k
        src = F3.at[:, 2 * k + 1 - c]
        return remote(src, D3P.at[layer % 2, :, k], pair_send.at[i], pair_recv.at[i], pn)

    def blocks(count, fn):
        def step(m, carry):
            fn(m)
            return carry

        lax.fori_loop(0, count, step, 0)

    def mask_of(first, count):
        at = first + lax.broadcasted_iota(jnp.int32, (count, 1), 0)
        inside = (lax.shift_right_logical(at, 5) < height) & ((at & (WIDE - 1)) < width)
        return jnp.where(inside, 1.0, 0.0).astype(F32)

    def expand():
        def one(r):
            ACC[pl.ds(pl.multiple_of(8 + WIDE * r, 8), 28), :] = IMG[r].astype(F32)

        blocks(24, one)

    def image_load():
        return pltpu.make_async_copy(image_in, IMG, stage_sem.at[2])

    def trunk_load():
        return pltpu.make_async_copy(trunk_in, IMG, stage_sem.at[3])

    def cot_load(k):
        return pltpu.make_async_copy(
            cot_in.at[pl.ds(4 * k, 4)], STG.at[k % 2], stage_sem.at[k % 2]
        )

    def start():
        for p in range(6):
            load(p).start()
        image_load().start()
        for k in range(2):
            cot_load(k).start()
        barrier = pltpu.get_barrier_semaphore()
        for t in (xn, yn, pn):
            pl.semaphore_signal(barrier, inc=1, device_id=t, device_id_type=MESH)
        when(
            z < 3, lambda: pl.semaphore_signal(barrier, inc=1, device_id=up, device_id_type=MESH)
        )
        when(
            z > 0, lambda: pl.semaphore_signal(barrier, inc=1, device_id=dn, device_id_type=MESH)
        )
        pl.semaphore_wait(barrier, jnp.where((z == 0) | (z == 3), 4, 5))

    def prep_in():
        ACC[...] = jnp.zeros_like(ACC)
        SQ[...] = jnp.zeros_like(SQ)
        SB[0] = jnp.zeros((64, 128), F32)
        for b in range(3):
            for k in range(4):
                F3[b, k, 0:32, :] = jnp.zeros((32, 128), BF)
                F3[b, k, 800:832, :] = jnp.zeros((32, 128), BF)
        image_load().wait()
        expand()

        def one(m):
            rows = pl.ds(pl.multiple_of(8 + 64 * m, 8), 64)
            v = ACC[rows, :] * mask_of(64 * m, 64)
            ACC[rows, :] = v
            SQ[0:1, :] += jnp.sum(v * v, axis=0, keepdims=True)

        blocks(12, one)
        trunk_load().start()
        pixels = (height * width).astype(F32) * (1.0 / 512.0)
        SQ[5:6, :] = jnp.full((1, 512), pixels, F32)

    def shifts():
        def one(m):
            v80 = ACC[pl.ds(pl.multiple_of(64 * m, 64), 80), :]
            rows = pl.ds(pl.multiple_of(32 + 64 * m, 32), 64)
            for b in range(3):
                v = v80[7 + b : 71 + b, :].astype(BF)
                for k in range(4):
                    F3[b, k, rows, :] = v[:, 128 * k : 128 * k + 128]

        blocks(12, one)

    def ft(layer):
        shifts()

        def one(m):
            v = ACC[pl.ds(pl.multiple_of(8 + 128 * m, 8), 128), :]
            FT[layer, :, pl.ds(pl.multiple_of(128 * m, 128), 128)] = v.T.astype(BF)

        blocks(6, one)
        share_ft(layer).start()

    def prep_cot():
        def clear(t):
            COT[t] = jnp.zeros((PIX, 128), BF)

        blocks(14, clear)
        for k in range(6):
            cot_load(k).wait()

            def one(i, k=k):
                rows = pl.ds(pl.multiple_of(WIDE * (4 * k + i), 32), 28)
                v = STG[k % 2, i]
                for t in range(14):
                    COT[t, rows, :] = v[:, 128 * t : 128 * t + 128]

            blocks(4, one)
            if k < 4:
                cot_load(k + 2).start()
        for k in range(2):
            share_cot(k).start()

    def taps(a, transposed):
        first = 32 * a if not transposed else 64 - 32 * a
        order = (0, 1, 2) if not transposed else (2, 1, 0)
        return [
            jnp.concatenate([F3[b, k, first : first + PIX, :] for k in range(4)], axis=1)
            for b in order
        ]

    def conv(layer, a):
        left = jnp.concatenate(taps(a, False), axis=1)
        base = BASES[layer] + 1536 * a
        right = jnp.concatenate([W[base + 4608 * k : base + 4608 * k + 1536, :] for k in range(4)], axis=1)
        v = jnp.dot(left, right, preferred_element_type=F32)
        if a == 0:
            ACC[8 : 8 + PIX, :] = v
        else:
            ACC[8 : 8 + PIX, :] += v

    def act(layer):
        gain, offset = gain_in[layer : layer + 1, :], offset_in[layer : layer + 1, :]
        k = 0.7978845608028654

        def one(m):
            rows = pl.ds(pl.multiple_of(8 + 64 * m, 8), 64)
            at = pl.ds(pl.multiple_of(64 * m, 64), 64)
            u = ACC[rows, :] * gain + offset
            mask = mask_of(64 * m, 64)
            u2 = u * u
            t = jnp.tanh(k * u * (1.0 + 0.044715 * u2))
            half = 0.5 * (1.0 + t) * mask
            f = u * half
            slope = half + (0.5 * k) * mask * u * (1.0 - t * t) * (1.0 + 0.134145 * u2)
            squares = f * f
            rn = lax.rsqrt(jnp.mean(squares, axis=-1, keepdims=True) + 1e-5)
            GP[layer, at, :] = (slope * gain).astype(BF)
            N[layer, at, :] = (f * rn).astype(BF)
            RN[at, layer : layer + 1] = rn
            SQ[layer + 1 : layer + 2, :] += jnp.sum(squares, axis=0, keepdims=True)
            if layer < 2:
                ACC[rows, :] = f
            else:
                v = f.astype(BF)
                shifted = pl.ds(pl.multiple_of(32 + 64 * m, 32), 64)
                for b in range(4):
                    F3[1, b, shifted, :] = v[:, 128 * b : 128 * b + 128]

        blocks(12, one)
        if layer == 2:
            for b in range(4):
                trunk_store(b).start()

    def trunk_store(b):
        return pltpu.make_async_copy(
            F3.at[1, b, pl.ds(32, PIX)], trunk_out.at[:, pl.ds(128 * b, 128)], out_sem.at[6 + b]
        )

    def nt(layer):
        if layer > 0:
            share_nt(layer - 1).wait_send()

        def one(m):
            at = pl.ds(pl.multiple_of(128 * m, 128), 128)
            NT[:, at] = N[layer, at, :].astype(F32).T.astype(BF)

        blocks(6, one)
        share_nt(layer).start()

    def head_grads(layer, k):
        if k == 0:
            share_nt(layer).wait_recv()
        if layer == 0:
            share_cot(k).wait_recv()
        own = jnp.concatenate([COT[7 * k + 3 * c + i] for i in range(4)], axis=1)
        other = jnp.concatenate([COTP[k, i] for i in range(4)], axis=1)
        v = jnp.dot(
            jnp.concatenate([NT[...], NTP[layer % 2]], axis=1),
            jnp.concatenate([own, other], axis=0),
            preferred_element_type=F32,
        ).astype(BF)
        base = grads(5 - layer)[1] + k * 8 * HEAD_UNIT
        for f in range(8):
            for t in range(4):
                r = base + f * HEAD_UNIT + 64 * t
                GH[r : r + 64, :] = v[64 * f : 64 * f + 64, 128 * t : 128 * t + 128]

    def head_block(layer, d):
        base = BASES[5 - layer] + d * 8 * HEAD_UNIT
        return jnp.concatenate(
            [
                jnp.concatenate(
                    [W[base + HEAD_UNIT * f + 64 * t : base + HEAD_UNIT * f + 64 * t + 64, :] for f in range(8)],
                    axis=0,
                )
                for t in range(4)
            ],
            axis=1,
        )

    def dtap(layer):
        def one(m):
            at = pl.ds(pl.multiple_of(256 * m, 256), 256)
            h = jnp.zeros((256, 512), F32)
            for d in range(4):
                first = 7 * (d // 2) + 3 * (d % 2)
                left = jnp.concatenate([COT[first + i, at, :] for i in range(4)], axis=1)
                h = h + lax.dot_general(
                    left, head_block(layer, d), (((1,), (1,)), ((), ())), preferred_element_type=F32
                )
            n = N[layer, at, :].astype(F32)
            mean = jnp.mean(h * n, axis=-1, keepdims=True)
            DT[layer, at, :] = ((h - n * mean) * RN[at, layer : layer + 1]).astype(BF)

        blocks(3, one)

    def joined(k):
        if k == 0:
            for i in range(2):
                share_cot(i).wait_send()

        def one(m):
            at = pl.ds(pl.multiple_of(256 * m, 256), 256)
            left = jnp.concatenate([N[i, at, :] for i in range(3)], axis=1)
            pairs = [
                jnp.dot(
                    left,
                    jnp.concatenate([head_block(i, 2 * k + half) for i in range(3)], axis=0),
                    preferred_element_type=F32,
                )
                for half in range(2)
            ]
            low, high = pairs
            tiles = [low[:, 128 * i : 128 * i + 128] for i in range(3)]
            tiles.append(low[:, 384:512] + high[:, 0:128])
            tiles += [high[:, 128 * i : 128 * i + 128] for i in range(1, 4)]
            total = jnp.zeros((1, 128), F32)
            for i, v in enumerate(tiles):
                total = total + jnp.sum(v * v, axis=0, keepdims=True)
                COT[7 * k + i, at, :] = v.astype(BF)
            SQ[4:5, 0:128] += total

        blocks(3, one)
        for i in range(7):
            heads_store(7 * k + i).start()

    def heads_store(t):
        return pltpu.make_async_copy(
            COT.at[t], heads_out.at[:, pl.ds(128 * t, 128)], out_sem.at[10 + t // 7]
        )

    def trunk_cot():
        trunk_load().wait()
        expand()

    def dlinear(layer):
        def one(m):
            rows = pl.ds(pl.multiple_of(8 + 64 * m, 8), 64)
            at = pl.ds(pl.multiple_of(64 * m, 64), 64)
            g = ACC[rows, :] + DT[layer, at, :].astype(F32)
            ACC[rows, :] = g * GP[layer, at, :].astype(F32)

        blocks(12, one)
        if layer == 2:
            for b in range(4):
                trunk_store(b).wait()
        else:
            for k in range(2):
                share_d(layer + 1, k).wait_send()
        shifts()
        for k in range(2):
            share_d(layer, k).start()

    def conv_back(layer, a):
        total = None if a == 0 else ACC[8 : 8 + PIX, :]
        base = BASES[layer] + 1536 * a
        for b, left in enumerate(taps(a, True)):
            first = base + 512 * b
            right = jnp.concatenate([W[first + 4608 * k : first + 4608 * k + 512, :] for k in range(4)], axis=1)
            v = lax.dot_general(left, right, (((1,), (1,)), ((), ())), preferred_element_type=F32)
            total = v if total is None else total + v
        ACC[8 : 8 + PIX, :] = total

    def conv_grads(layer, a):
        if a == 0:
            share_ft(layer).wait_recv()
            for k in range(2):
                share_d(layer, k).wait_recv()
            if layer == 1:
                ag_end(2)
        first = 64 - 32 * a
        own = [F3[2 - b, 2 * k + c, first : first + PIX, :] for b in range(3) for k in range(2)]
        other = [D3P[layer % 2, 2 - b, k, first : first + PIX, :] for b in range(3) for k in range(2)]
        v = jnp.dot(
            jnp.concatenate([FT[layer], FTP[layer]], axis=1),
            jnp.concatenate(
                [jnp.concatenate(own, axis=1), jnp.concatenate(other, axis=1)], axis=0
            ),
            preferred_element_type=F32,
        ).astype(BF)
        ref, base = grads(layer)
        for b in range(3):
            for k in range(2):
                r = base + 4608 * k + 1536 * a + 512 * b
                at = 256 * b + 128 * k
                ref[r : r + 512, :] = v[:, at : at + 128]

    def image_store():
        return pltpu.make_async_copy(DT.at[2], image_out, out_sem.at[12])

    def image_grad():
        def one(m):
            rows = pl.ds(pl.multiple_of(8 + 64 * m, 8), 64)
            at = pl.ds(pl.multiple_of(64 * m, 64), 64)
            DT[2, at, :] = (ACC[rows, :] * mask_of(64 * m, 64)).astype(BF)

        blocks(12, one)
        image_store().start()

    def small(i):
        return remote(LB.at[i], MR.at[i], small_send.at[i], small_recv.at[i], (pn, xn, yn)[i])

    def line(s, i, t):
        return remote(ZB.at[s], ZB.at[s], small_send.at[i], small_recv.at[5 + s], t)

    def m0():
        v = SQ[:, 0:128]
        for i in range(1, 4):
            v = v + SQ[:, 128 * i : 128 * i + 128]
        LB[0] = v
        small(0).start()

    def m1(i):
        small(i).wait_recv()
        v = LB[i] + MR[i]
        if i < 2:
            LB[i + 1] = v
            small(i + 1).start()
            return
        ZB[z] = v
        when(z < 3, lambda: line(z, 5 + z, up).start())
        when(z > 0, lambda: line(z, 9 + z, dn).start())

    def m2(j):
        s = sig[j]
        line(s, 5, up).wait_recv()
        when((s < z) & (z < 3), lambda: line(s, 5 + s, up).start())
        when((s > z) & (z > 0), lambda: line(s, 9 + s, dn).start())

    def m3():
        total = ZB[0] + ZB[1] + ZB[2] + ZB[3]
        v = jnp.sum(total, axis=1, keepdims=True)
        which = lax.broadcasted_iota(jnp.int32, (8, 1), 0)
        wide = jnp.where(which == 4, 1792.0, 512.0).astype(F32)
        rms_out[...] = jnp.broadcast_to(jnp.sqrt(v / (v[5:6] * wide)), (8, 128))

    def scale_sum(i):
        return remote(SB.at[i], SR.at[i], small_send.at[3 + i], small_recv.at[3 + i], (pn, yn)[i])

    def t0():
        scale_sum(0).start()

    def t1():
        scale_sum(0).wait_recv()
        SB[1] = SB[0] + SR[0]
        scale_sum(1).start()

    def t2():
        scale_sum(1).wait_recv()
        scale_out[...] = SB[1] + SR[1]

    def finish():
        for p in range(6):
            if p != 2:
                ag_end(p)
            rs_end(p)
        for i in range(3):
            share_ft(i).wait_send()
            small(i).wait_send()
        share_nt(2).wait_send()
        for k in range(2):
            share_d(0, k).wait_send()
            scale_sum(k).wait_send()
        for s in range(4):
            when((z < 3) & (s <= z), lambda s=s: line(s, 5 + s, up).wait_send())
            when((z > 0) & (s >= z), lambda s=s: line(s, 9 + s, dn).wait_send())
        for k in range(2):
            pltpu.make_async_copy(
                COT.at[pl.ds(7 * k, 7)], COT.at[pl.ds(7 * k, 7)], out_sem.at[10 + k]
            ).wait()
        image_store().wait()

    fns = dict(
        start=start, e0=e0, zj=zj, xd=xd, yd=yd, xf=xf, yf=yf, pw=pw,
        s1=s1, s2a=s2a, s2b=s2b, s3a=s3a, s3b=s3b, zu=zu, zd=zd, fin=fin,
        prep_in=prep_in, prep_cot=prep_cot, ft=ft, conv=conv, act=act, nt=nt,
        head_grads=head_grads, dtap=dtap, joined=joined, trunk_cot=trunk_cot,
        dlinear=dlinear, conv_back=conv_back, conv_grads=conv_grads, image_grad=image_grad,
        m0=m0, m1=m1, m2=m2, m3=m3, t0=t0, t1=t1, t2=t2, finish=finish,
    )
    for name, *args in order:
        fns[name](*args)


def patches(feature):
    height = feature.shape[1]
    breadth = feature.shape[2]
    padded = jnp.pad(feature, ((0, 0), (1, 1), (1, 1), (0, 0)))
    pieces = [
        padded[:, down_step : down_step + height, side_step : side_step + breadth, :]
        for down_step in range(3)
        for side_step in range(3)
    ]
    return jnp.concatenate(pieces, axis=-1)


def unpatch(stacked, channels):
    images, height, breadth, _ = stacked.shape
    padded = jnp.zeros((images, height + 2, breadth + 2, channels), jnp.float32)
    for down_step in range(3):
        for side_step in range(3):
            tap_index = 3 * down_step + side_step
            padded = padded.at[
                :, down_step : down_step + height, side_step : side_step + breadth, :
            ].add(stacked[..., tap_index * channels : (tap_index + 1) * channels])
    return padded[:, 1:-1, 1:-1, :]


def activate(linear, gain_vec, offsets, valid_mask):
    return valid_mask * jax.nn.gelu(linear * gain_vec + offsets)


def tap_piece(feature, scale_vec):
    return (
        feature * lax.rsqrt(jnp.mean(feature * feature, axis=-1, keepdims=True) + 1e-05) * scale_vec
    )


def general(
    inputs,
    heights,
    widths,
    conv_weights,
    affine_scale,
    affine_shift,
    tap_scales,
    head_weights,
    trunk_cot,
    heads_cot,
):
    images, height, breadth, channels = inputs.shape
    layer_count = conv_weights.shape[0]
    row_ids = jnp.arange(height, dtype=jnp.int32)
    col_ids = jnp.arange(breadth, dtype=jnp.int32)
    valid = (row_ids[None, :, None] < heights[:, None, None]) & (
        col_ids[None, None, :] < widths[:, None, None]
    )
    valid_mask = jnp.where(valid, 1.0, 0.0).astype(jnp.float32)[..., None]
    conv_cols, head_cols = (
        lax.all_gather(conv_weights, "dp", axis=2, tiled=True),
        lax.all_gather(head_weights, "dp", axis=2, tiled=True),
    )
    conv_full, head_full, scale_full = (
        lax.all_gather(conv_cols, "fsdp", axis=1, tiled=True),
        lax.all_gather(head_cols, "fsdp", axis=1, tiled=True),
        lax.all_gather(tap_scales, "fsdp", axis=1, tiled=True),
    )
    outputs_wide = head_full.shape[2]
    feature = inputs.astype(jnp.float32) * valid_mask
    squares = [jnp.sum(feature * feature)]
    entering = inputs * valid_mask.astype(jnp.bfloat16)
    kept_in, kept_linear, kept_feature, kept_tap = ([], [], [], [])
    summed = jnp.zeros((images, height, breadth, outputs_wide), jnp.float32)
    for layer_index in range(layer_count):
        stacked = patches(entering)
        linear = jnp.einsum(
            "ghwk,kc->ghwc", stacked, conv_full[layer_index], preferred_element_type=jnp.float32
        )
        feature = activate(linear, affine_scale[layer_index], affine_shift[layer_index], valid_mask)
        tapped = tap_piece(feature, scale_full[layer_index].astype(jnp.float32)).astype(
            jnp.bfloat16
        )
        summed = summed + jnp.einsum(
            "ghwc,co->ghwo", tapped, head_full[layer_index], preferred_element_type=jnp.float32
        )
        kept_in.append(entering)
        kept_linear.append(linear)
        kept_feature.append(feature)
        kept_tap.append(tapped)
        squares.append(jnp.sum(feature * feature))
        entering = feature.astype(jnp.bfloat16)
    squares.append(jnp.sum(summed * summed))
    square_total, pixels = lax.psum((jnp.stack(squares), jnp.sum(valid_mask)), ("dp", "fsdp"))
    divisors = jnp.array([channels] * (layer_count + 1) + [outputs_wide], jnp.float32)
    rms = jnp.sqrt(square_total / (pixels * divisors))
    conv_back, head_back, scale_back = conv_full, head_full, scale_full
    grad_conv = [None] * layer_count
    grad_scale = [None] * layer_count
    grad_head = [None] * layer_count
    grad_feature = trunk_cot.astype(jnp.float32)
    for layer_index in reversed(range(layer_count)):
        grad_head[layer_index] = jnp.einsum(
            "ghwc,ghwo->co", kept_tap[layer_index], heads_cot, preferred_element_type=jnp.float32
        )
        grad_tapped = jnp.einsum(
            "ghwo,co->ghwc", heads_cot, head_back[layer_index], preferred_element_type=jnp.float32
        )
        _, pullback = jax.vjp(
            tap_piece, kept_feature[layer_index], scale_back[layer_index].astype(jnp.float32)
        )
        feature_part, scale_part = pullback(grad_tapped)
        grad_scale[layer_index] = scale_part
        grad_feature = grad_feature + feature_part
        local_act = partial(
            activate,
            gain_vec=affine_scale[layer_index],
            offsets=affine_shift[layer_index],
            valid_mask=valid_mask,
        )
        _, pullback = jax.vjp(local_act, kept_linear[layer_index])
        (grad_linear,) = pullback(grad_feature)
        low_linear = grad_linear.astype(jnp.bfloat16)
        grad_conv[layer_index] = jnp.einsum(
            "ghwk,ghwc->kc",
            patches(kept_in[layer_index]),
            low_linear,
            preferred_element_type=jnp.float32,
        )
        spread = jnp.einsum(
            "ghwc,kc->ghwk", low_linear, conv_back[layer_index], preferred_element_type=jnp.float32
        )
        grad_feature = unpatch(spread, channels)
    input_grad = (grad_feature * valid_mask).astype(jnp.bfloat16)
    stacked_conv = jnp.stack(grad_conv)
    stacked_head = jnp.stack(grad_head)
    stacked_scale = jnp.stack(grad_scale)
    dp_count = lax.axis_size("dp")
    part_conv, part_head, part_scale = (
        lax.psum_scatter(
            stacked_conv.astype(jnp.bfloat16), "fsdp", scatter_dimension=1, tiled=True
        ).astype(jnp.float32),
        lax.psum_scatter(
            stacked_head.astype(jnp.bfloat16), "fsdp", scatter_dimension=1, tiled=True
        ).astype(jnp.float32),
        lax.psum_scatter(
            stacked_scale.astype(jnp.bfloat16), "fsdp", scatter_dimension=1, tiled=True
        ).astype(jnp.float32),
    )
    spread_scale = jnp.broadcast_to(part_scale[:, :, None], part_scale.shape + (dp_count,))
    conv_grad, head_grad, scale_cols = (
        lax.psum_scatter(
            part_conv.astype(jnp.bfloat16), "dp", scatter_dimension=2, tiled=True
        ).astype(jnp.float32),
        lax.psum_scatter(
            part_head.astype(jnp.bfloat16), "dp", scatter_dimension=2, tiled=True
        ).astype(jnp.float32),
        lax.psum_scatter(
            spread_scale.astype(jnp.bfloat16), "dp", scatter_dimension=2, tiled=True
        ).astype(jnp.float32),
    )
    scale_grad = scale_cols[:, :, 0]
    trunk_out = kept_feature[-1].astype(jnp.bfloat16)
    heads_out = summed.astype(jnp.bfloat16)
    return (trunk_out, heads_out, input_grad, conv_grad, scale_grad, head_grad, rms)


def fused(
    inputs,
    heights,
    widths,
    conv_weights,
    affine_scale,
    affine_shift,
    tap_scales,
    head_weights,
    trunk_cot,
    heads_cot,
):
    core = lax.axis_index("dp") % 2
    low = jnp.pad(head_weights, ((0, 0), (0, 0), (0, 64)))
    high = jnp.pad(head_weights, ((0, 0), (0, 0), (64, 0)))
    raw = jnp.where(core == 0, low, high).reshape(3, 64, 4, 128).transpose(0, 2, 1, 3)
    scale = jnp.broadcast_to(tap_scales.astype(F32)[:, :, None], (3, 64, 128))
    scaled = (raw.astype(F32) * scale[:, None]).astype(BF)
    raw, scaled = raw.reshape(3, 256, 128), scaled.reshape(3, 256, 128)
    hbm = pl.BlockSpec(memory_space=pl.ANY)
    vmem = pl.BlockSpec(memory_space=pltpu.VMEM)
    smem = pl.BlockSpec(memory_space=pltpu.SMEM)
    dma = pltpu.SemaphoreType.DMA
    results = pl.pallas_call(
        partial(kernel, ORDER),
        name="conv_block",
        out_shape=(
            jax.ShapeDtypeStruct((PIX, 512), BF),
            jax.ShapeDtypeStruct((PIX, 1792), BF),
            jax.ShapeDtypeStruct((PIX, 512), BF),
            jax.ShapeDtypeStruct((3, 576, 128), F32),
            jax.ShapeDtypeStruct((3, 256, 128), F32),
            jax.ShapeDtypeStruct((64, 128), F32),
            jax.ShapeDtypeStruct((8, 128), F32),
        ),
        in_specs=[hbm, hbm, vmem, vmem, vmem, vmem, smem, smem, hbm, hbm, hbm],
        out_specs=(hbm, hbm, hbm, hbm, hbm, vmem, vmem),
        scratch_shapes=[
            pltpu.VMEM((ROWS, 128), BF),
            pltpu.VMEM((3, 4, 832, 128), BF),
            pltpu.VMEM((3, 512, PIX), BF),
            pltpu.VMEM((3, 512, PIX), BF),
            pltpu.VMEM((512, PIX), BF),
            pltpu.VMEM((2, 512, PIX), BF),
            pltpu.VMEM((3, PIX, 512), BF),
            pltpu.VMEM((3, PIX, 512), BF),
            pltpu.VMEM((3, PIX, 512), BF),
            pltpu.VMEM((PIX, 128), F32),
            pltpu.VMEM((14, PIX, 128), BF),
            pltpu.VMEM((2, 4, PIX, 128), BF),
            pltpu.VMEM((2, 4, 28, 1792), BF),
            pltpu.VMEM((24, 28, 512), BF),
            pltpu.VMEM((16 + PIX, 512), F32),
            pltpu.VMEM((2, 3, 2, 832, 128), BF),
            pltpu.VMEM((16 * CONV_UNIT, 128), BF),
            pltpu.VMEM((3 * 16 * HEAD_UNIT, 128), BF),
            pltpu.VMEM((2 * SLOTS * CONV_UNIT, 128), BF),
            pltpu.VMEM((3 * SLOTS * HEAD_UNIT, 128), BF),
            pltpu.VMEM((3, CONV_UNIT, 128), F32),
            pltpu.VMEM((3, HEAD_UNIT, 128), F32),
            pltpu.VMEM((8, 512), F32),
            pltpu.VMEM((3, 8, 128), F32),
            pltpu.VMEM((3, 8, 128), F32),
            pltpu.VMEM((4, 8, 128), F32),
            pltpu.VMEM((2, 64, 128), F32),
            pltpu.VMEM((2, 64, 128), F32),
            dma((6, 24)),
            dma((6, 28)),
            dma((6,)),
            dma((6, 14)),
            dma((6, 14)),
            dma((14,)),
            dma((14,)),
            dma((4,)),
            dma((13,)),
            dma((9,)),
            dma((13,)),
            pltpu.SemaphoreType.REGULAR((4,)),
        ],
        compiler_params=pltpu.CompilerParams(
            collective_id=0, has_side_effects=True, vmem_limit_bytes=64 * 2**20
        ),
        cost_estimate=pl.CostEstimate(
            flops=45_000_000_000, bytes_accessed=16_000_000, transcendentals=1_200_000
        ),
    )(
        conv_weights,
        scaled,
        raw,
        scale,
        affine_scale,
        affine_shift,
        heights,
        widths,
        inputs[0],
        trunk_cot[0],
        heads_cot[0],
    )
    trunk, heads, image, conv_grad, head_grad, scale_grad, rms = results

    def crop(v):
        return v.reshape(1, 24, WIDE, v.shape[1])[:, :, :28]

    head_grad = head_grad.reshape(3, 4, 64, 128).transpose(0, 2, 1, 3).reshape(3, 64, 512)
    head_grad = lax.dynamic_slice(head_grad, (0, 0, 64 * core), (3, 64, 448))
    return (
        crop(trunk),
        crop(heads),
        crop(image),
        conv_grad,
        scale_grad[:, :3].T,
        head_grad,
        rms[:5, 0],
    )


def solution(mesh):
    in_specs = (
        P(("dp", "fsdp"), None, None, None),
        P(("dp", "fsdp")),
        P(("dp", "fsdp")),
        P(None, "fsdp", "dp"),
        P(),
        P(),
        P(None, "fsdp"),
        P(None, "fsdp", "dp"),
        P(("dp", "fsdp"), None, None, None),
        P(("dp", "fsdp"), None, None, None),
    )
    out_specs = (
        P(("dp", "fsdp"), None, None, None),
        P(("dp", "fsdp"), None, None, None),
        P(("dp", "fsdp"), None, None, None),
        P(None, "fsdp", "dp"),
        P(None, "fsdp"),
        P(None, "fsdp", "dp"),
        P(),
    )
    body = fused if dict(mesh.shape) == {"dp": 4, "fsdp": 8} else general
    return jax.shard_map(body, mesh=mesh, in_specs=in_specs, out_specs=out_specs, check_vma=False)
```

```python
from functools import partial

import jax
import jax.numpy as jnp
from jax import lax
from jax.experimental import pallas as pl
from jax.experimental.pallas import tpu as pltpu
from jax.sharding import PartitionSpec as P

MESH = pl.DeviceIdType.MESH
F32, BF = jnp.float32, jnp.bfloat16

CONV_UNIT, HEAD_UNIT = 576, 256
UNITS = (CONV_UNIT,) * 3 + (HEAD_UNIT,) * 3
BASES = tuple(32 * sum(UNITS[:p]) for p in range(6))
ROWS = 32 * sum(UNITS)
ROUTES = (
    (0, 0, 288, 1),
    (0, 288, 288, 2),
    (1, 0, 576, 0),
    (2, 0, 288, 1),
    (2, 288, 288, 2),
    (3, 0, 128, 1),
    (3, 128, 128, 2),
    (4, 0, 128, 1),
    (4, 128, 128, 2),
    (5, 0, 256, 0),
)
SLOTS = (17, 19, 19)
LAND = tuple(sum(SLOTS[k] * m for _, _, m, k in ROUTES[:r]) for r in range(len(ROUTES) + 1))
HIGH, PIX, PAD = 24, 672, 768
ORDER = (
    ("start",),
    ("ld", 0),
    ("e0", 0),
    ("e0", 1),
    ("ld", 2),
    ("e0", 3),
    ("ld", 1),
    ("prep_heads",),
    ("e0", 6),
    ("e0", 7),
    ("e0", 5),
    ("f1", 1),
    ("e0", 2),
    ("e0", 8),
    ("f1", 0),
    ("zj", 0, 1, 0),
    ("zj", 1, 1, 0),
    ("zj", 7, 1, 0),
    ("zj", 5, 1, 0),
    ("zj", 1, 1, 1),
    ("lj", 3, 0, 0),
    ("lj", 1, 0, 0),
    ("prep_in",),
    ("zj", 0, 2, 0),
    ("zj", 1, 2, 1),
    ("zj", 0, 1, 1),
    ("zj", 1, 2, 0),
    ("zj", 2, 1),
    ("lj", 0, 0, 0),
    ("prep_cot",),
    ("zj", 0, 3, 0),
    ("zj", 1, 3, 0),
    ("f1", 6),
    ("zj", 0, 2, 1),
    ("lj", 1, 0, 1),
    ("lj", 1, 1, 1),
    ("lj", 6, 0, 0),
    ("zj", 8, 1, 0),
    ("zj", 1, 3, 1),
    ("lj", 0, 1, 0),
    ("lj", 0, 0, 1),
    ("lj", 1, 1, 0),
    ("lj", 5, 0, 0),
    ("lj", 5, 1, 0),
    ("zj", 6, 1, 0),
    ("zj", 0, 3, 1),
    ("e0", 4),
    ("lj", 1, 2, 1),
    ("f1", 7),
    ("lj", 0, 1, 1),
    ("lj", 0, 2, 0),
    ("lj", 7, 0, 0),
    ("yd", 2, 0),
    ("lj", 1, 2, 0),
    ("xd", 2, 0),
    ("lj", 1, 3, 0),
    ("lj", 0, 2, 1),
    ("zj", 3, 1, 0),
    ("lj", 0, 3, 0),
    ("yd", 2, 1),
    ("lj", 1, 3, 1),
    ("lj", 0, 3, 1),
    ("lj", 7, 1, 0),
    ("zj", 2, 2),
    ("ft", 0),
    ("pw", 1),
    ("pw", 0),
    ("lj", 8, 0, 0),
    ("conv", 0, 0),
    ("zj", 2, 3),
    ("xd", 2, 1),
    ("f1", 3),
    ("f1", 5),
    ("f1", 8),
    ("conv", 0, 1),
    ("lj", 6, 0, 1),
    ("zj", 6, 1, 1),
    ("conv", 0, 2),
    ("f1", 4),
    ("act", 0),
    ("xd", 2, 2),
    ("e0", 9),
    ("nt", 0),
    ("lj", 7, 0, 1),
    ("xd", 2, 3),
    ("zj", 7, 1, 1),
    ("yd", 2, 2),
    ("ft", 1),
    ("yd", 2, 3),
    ("zj", 5, 2, 0),
    ("zj", 8, 2, 0),
    ("zj", 6, 2, 1),
    ("lj", 6, 1, 1),
    ("zj", 3, 1, 1),
    ("zj", 6, 2, 0),
    ("yf", 2, 0),
    ("head_grads", 0, 0),
    ("zj", 3, 2, 1),
    ("zj", 4, 1, 0),
    ("lj", 3, 0, 1),
    ("xf", 2, 0),
    ("xd", 9, 0),
    ("zj", 7, 2, 1),
    ("zj", 8, 1, 1),
    ("head_grads", 0, 1),
    ("zj", 4, 2, 0),
    ("zj", 4, 1, 1),
    ("lj", 6, 1, 0),
    ("zj", 5, 3, 0),
    ("zj", 5, 1, 1),
    ("lj", 4, 0, 0),
    ("xf", 2, 1),
    ("lj", 8, 0, 1),
    ("lj", 5, 0, 1),
    ("yf", 2, 1),
    ("lj", 3, 1, 0),
    ("lj", 4, 0, 1),
    ("lj", 8, 1, 0),
    ("zj", 4, 3, 0),
    ("zj", 9, 1),
    ("lj", 8, 2, 0),
    ("yd", 9, 0),
    ("lj", 6, 2, 1),
    ("lj", 7, 1, 1),
    ("lj", 6, 2, 0),
    ("zj", 3, 3, 1),
    ("lj", 5, 2, 0),
    ("pw", 2),
    ("conv", 1, 0),
    ("zj", 3, 2, 0),
    ("conv", 1, 1),
    ("zj", 4, 2, 1),
    ("conv", 1, 2),
    ("zj", 4, 3, 1),
    ("act", 1),
    ("zj", 6, 3, 0),
    ("nt", 1),
    ("lj", 3, 1, 1),
    ("zj", 3, 3, 0),
    ("ft", 2),
    ("lj", 3, 2, 1),
    ("lj", 5, 1, 1),
    ("lj", 4, 1, 0),
    ("zj", 8, 3, 0),
    ("lj", 5, 3, 0),
    ("lj", 4, 2, 0),
    ("lj", 8, 1, 1),
    ("yd", 9, 1),
    ("lj", 4, 3, 0),
    ("zj", 5, 2, 1),
    ("zj", 8, 2, 1),
    ("zj", 6, 3, 1),
    ("lj", 7, 2, 1),
    ("lj", 3, 3, 1),
    ("lj", 4, 1, 1),
    ("head_grads", 1, 0),
    ("zj", 5, 3, 1),
    ("head_grads", 1, 1),
    ("zj", 9, 2),
    ("lj", 3, 2, 0),
    ("lj", 4, 2, 1),
    ("xd", 9, 1),
    ("zj", 7, 2, 0),
    ("lj", 3, 3, 0),
    ("s1", 9),
    ("lj", 4, 3, 1),
    ("zj", 7, 3, 1),
    ("lj", 6, 3, 0),
    ("lj", 5, 2, 1),
    ("s1", 7),
    ("lj", 6, 3, 1),
    ("zj", 7, 3, 0),
    ("pw", 3),
    ("s1", 8),
    ("pw", 4),
    ("lj", 8, 3, 0),
    ("conv", 2, 0),
    ("conv", 2, 1),
    ("zj", 8, 3, 1),
    ("conv", 2, 2),
    ("lj", 5, 3, 1),
    ("act", 2),
    ("lj", 8, 2, 1),
    ("pw", 5),
    ("trunk_cot",),
    ("pw", 6),
    ("nt", 2),
    ("dtap", 2),
    ("s2", 8, 0),
    ("s2b", 9),
    ("lj", 7, 2, 0),
    ("dlinear", 2),
    ("lj", 7, 3, 1),
    ("lj", 8, 3, 1),
    ("s2a", 9),
    ("head_grads", 2, 0),
    ("s2", 7, 0),
    ("zj", 9, 3),
    ("head_grads", 2, 1),
    ("s1", 6),
    ("s1", 5),
    ("s3a", 9),
    ("conv_back", 2, 0),
    ("pw", 8),
    ("conv_grads", 2, 0),
    ("conv_grads", 2, 1),
    ("lj", 7, 3, 0),
    ("conv_grads", 2, 2),
    ("s1", 3),
    ("s1", 4),
    ("s3b", 9),
    ("pw", 7),
    ("conv_back", 2, 1),
    ("conv_back", 2, 2),
    ("s2", 5, 1),
    ("dtap", 1),
    ("dlinear", 1),
    ("s2", 6, 0),
    ("zu", 8, 3),
    ("s2", 5, 0),
    ("xd", 9, 2),
    ("zu", 7, 3),
    ("xd", 9, 3),
    ("yf", 9, 0),
    ("yd", 9, 2),
    ("s2", 3, 0),
    ("zu", 9, 3),
    ("yd", 9, 3),
    ("conv_back", 1, 0),
    ("s2", 4, 0),
    ("conv_grads", 1, 0),
    ("conv_grads", 1, 1),
    ("conv_grads", 1, 2),
    ("s1", 2),
    ("s2", 4, 1),
    ("xf", 9, 0),
    ("xf", 9, 1),
    ("s2", 6, 1),
    ("zu", 5, 3),
    ("yf", 9, 1),
    ("zu", 6, 3),
    ("conv_back", 1, 1),
    ("conv_back", 1, 2),
    ("pw", 9),
    ("zu", 3, 3),
    ("dtap", 0),
    ("s2", 3, 1),
    ("s2", 8, 1),
    ("zu", 4, 3),
    ("zd", 8, 0),
    ("zd", 7, 0),
    ("dlinear", 0),
    ("s2a", 2),
    ("zu", 9, 2),
    ("zd", 5, 0),
    ("s2b", 2),
    ("zu", 4, 2),
    ("s2", 7, 1),
    ("zu", 3, 2),
    ("zd", 4, 0),
    ("joined", 0),
    ("zu", 6, 2),
    ("zd", 6, 0),
    ("zu", 5, 2),
    ("zd", 5, 1),
    ("conv_grads", 0, 0),
    ("zd", 6, 1),
    ("conv_grads", 0, 1),
    ("conv_grads", 0, 2),
    ("s1", 1),
    ("zd", 9, 0),
    ("s3a", 2),
    ("s3b", 2),
    ("zd", 3, 0),
    ("zu", 8, 2),
    ("s1", 0),
    ("conv_back", 0, 0),
    ("zu", 7, 2),
    ("zd", 7, 1),
    ("conv_back", 0, 1),
    ("zd", 2, 0),
    ("zd", 8, 1),
    ("zd", 4, 1),
    ("zd", 9, 1),
    ("zu", 2, 3),
    ("zd", 3, 1),
    ("zf", 6),
    ("zf", 7),
    ("zd", 2, 1),
    ("joined", 1),
    ("s2", 1, 0),
    ("m0",),
    ("zu", 1, 3),
    ("conv_back", 0, 2),
    ("zf", 8),
    ("m1", 0),
    ("zf", 9),
    ("s2", 0, 0),
    ("zu", 0, 3),
    ("zd", 0, 0),
    ("s2", 0, 1),
    ("zu", 0, 2),
    ("zf", 5),
    ("zf", 3),
    ("pf", 5),
    ("ff", 8),
    ("s2", 1, 1),
    ("m1", 1),
    ("zd", 1, 0),
    ("zu", 1, 2),
    ("image_grad",),
    ("ff", 5),
    ("ff", 7),
    ("zd", 0, 1),
    ("zd", 1, 1),
    ("ff", 6),
    ("pf", 4),
    ("m1", 2),
    ("zf", 4),
    ("pf", 3),
    ("t0",),
    ("zf", 0),
    ("m2", 1),
    ("zu", 2, 2),
    ("t1",),
    ("zf", 1),
    ("m2", 2),
    ("ff", 3),
    ("m2", 3),
    ("ff", 4),
    ("t2",),
    ("zf", 2),
    ("ff", 0),
    ("pf", 1),
    ("m3",),
    ("pf", 2),
    ("ff", 1),
    ("pf", 0),
    ("finish",),
)


def kernel(
    order,
    conv_in,
    head_in,
    tap_in,
    gain_in,
    offset_in,
    height_in,
    width_in,
    image_in,
    trunk_in,
    cot_in,
    trunk_out,
    heads_out,
    image_out,
    conv_out,
    head_out,
    scale_out,
    rms_out,
    W,
    F3,
    FT,
    FTP,
    NTP,
    N,
    GP,
    DT,
    RN,
    COT,
    COTP,
    ACC,
    D3P,
    GC2,
    GH,
    RL,
    RAW,
    HW,
    SQ,
    LB,
    MR,
    ZB,
    SB,
    SR,
    ag_recv,
    ag_send,
    load_sem,
    rs_recv,
    rs_send,
    pair_recv,
    pair_send,
    in_sem,
    out_sem,
    small_recv,
    small_send,
):
    dpi, fsi = lax.axis_index("dp"), lax.axis_index("fsdp")
    y, c, z, x = dpi // 2, dpi % 2, fsi // 2, fsi % 2

    def dev(yy, cc, zz, xx):
        return (yy * 2 + cc, zz * 2 + xx)

    xn, yn, pn = dev(y, c, z, 1 - x), dev(1 - y, c, z, x), dev(y, 1 - c, z, x)
    up, dn = dev(y, c, jnp.minimum(z + 1, 3), x), dev(y, c, jnp.maximum(z - 1, 0), x)
    sig = [z, z + 1 - 2 * (z % 2), jnp.where(z < 2, 2, 1), jnp.where(z < 2, 3, 0)]
    height, width = height_in[0], width_in[0]

    def when(cond, fn):
        pl.when(cond)(fn)

    def remote(src, dst, send, recv, t):
        return pltpu.make_async_remote_copy(
            src_ref=src, dst_ref=dst, send_sem=send, recv_sem=recv, device_id=t, device_id_type=MESH
        )

    def row(p, yy, cc, s, xx, off=0):
        return pl.multiple_of(BASES[p] + ((2 * yy + cc) * 8 + 2 * s + xx) * UNITS[p] + off, 32)

    def shard(r, first, s, last):
        p, off, _, kind = ROUTES[r]
        return row(p, last, c, s, first, off) if kind < 2 else row(p, first, c, s, last, off)

    def ends(r):
        return (x, y, xn, yn) if ROUTES[r][3] < 2 else (y, x, yn, xn)

    def ag(r, at, si, ri, t, n=1):
        part = W.at[pl.ds(at, ROUTES[r][2] * n)]
        return remote(part, part, ag_send.at[r, si], ag_recv.at[r, ri], t)

    def ag_start(r, at, si, ri, t):
        ag(r, at, si, ri, t).start()

    def ag_wait(r, ri, n=1):
        ag(r, BASES[ROUTES[r][0]], 0, ri, xn, n).wait_recv()

    def pair(r, at, q):
        ag_start(r, at, 25 + q, 20 + q, pn)

    def load(p):
        return pltpu.make_async_copy(
            conv_in.at[p], W.at[pl.ds(row(p, y, c, z, x), CONV_UNIT)], load_sem.at[p]
        )

    def ld(p):
        load(p).wait()

    def along(r, s, at, i, passed=True):
        if not passed:
            when(z < 3, lambda: ag_start(r, at, i + s, i // 2 + s, up))
            when(z > 0, lambda: ag_start(r, at, i + 4 + s, i // 2 + s, dn))
            return
        when((s < z) & (z < 3), lambda: ag_start(r, at, i + s, i // 2 + s, up))
        when((s > z) & (z > 0), lambda: ag_start(r, at, i + 4 + s, i // 2 + s, dn))

    def fan(r, s, at, line):
        if ROUTES[r][3] == 0:
            ag_start(r, at, 8 + s, 4 + s, xn)
            ag_start(r, at, 12 + s, 8 + s, yn)
        else:
            ag_start(r, at, 16 + 4 * line + s, 8 + 4 * line + s, ends(r)[3])
        pair(r, at, line)

    def e0(r):
        first, last, fn, _ = ends(r)
        at = shard(r, first, z, last)
        if ROUTES[r][3]:
            ag_start(r, at, 24, 16, fn)
        along(r, z, at, 0, False)
        fan(r, z, at, 0)

    def f1(r):
        first, last, _, _ = ends(r)
        at = shard(r, 1 - first, z, last)
        ag_wait(r, 16)
        along(r, z, at, 8, False)
        fan(r, z, at, 1)

    def zj(r, j, line=0):
        first, last, _, _ = ends(r)
        s = sig[j]
        at = shard(r, 1 - first if line else first, s, last)
        ag_wait(r, 4 * line + s)
        along(r, s, at, 8 * line)
        fan(r, s, at, line)

    def lj(r, j, line):
        first, last, _, _ = ends(r)
        s = sig[j]
        ag_wait(r, 8 + 4 * line + s)
        pair(r, shard(r, 1 - first if line else first, s, 1 - last), 2 + line)

    def xd(r, j):
        s = sig[j]
        at = shard(r, 1 - x, s, y)
        ag_wait(r, 4 + s)
        when(s % 2 == 0, lambda: ag_start(r, at, 20 + s, 16 + s, yn))
        pair(r, at, 1)

    def yd(r, j):
        s = sig[j]
        at = shard(r, x, s, 1 - y)
        ag_wait(r, 8 + s)
        when(s % 2 == 1, lambda: ag_start(r, at, 16 + s, 12 + s, xn))
        pair(r, at, 2)

    def yf(r, k):
        s = jnp.where(z < 2, 2 * k, 2 - 2 * k)
        ag_wait(r, 16 + s)
        pair(r, shard(r, 1 - x, s, 1 - y), 3)

    def xf(r, k):
        s = jnp.where(z < 2, 1 + 2 * k, 3 - 2 * k)
        ag_wait(r, 12 + s)
        pair(r, shard(r, 1 - x, s, 1 - y), 3)

    def pw(r):
        for q in range(4):
            ag_wait(r, 20 + q, 4)

    def ag_end(r):
        def done(si, n=1):
            ag(r, BASES[ROUTES[r][0]], si, 0, xn, n).wait_send()

        straight = ROUTES[r][3] == 0
        for s in range(4):
            for i in (0,) if straight else (0, 8):
                when((z < 3) & (s <= z), lambda: done(i + s))
                when((z > 0) & (s >= z), lambda: done(i + 4 + s))
            if straight:
                done(8 + s)
                done(12 + s)
                done(16 + s if s % 2 else 20 + s)
            else:
                done(16 + s)
                done(20 + s)
            done(25 + s, 4)
        if not straight:
            done(24)

    def grads(p):
        if p == 2:
            return GC2, 0
        if p < 2:
            return W, BASES[2] + (1 - p) * 16 * CONV_UNIT
        return GH, (p - 3) * 16 * HEAD_UNIT

    def grow(r, first, s, last):
        p, off, _, kind = ROUTES[r]
        yy, xx = (last, first) if kind < 2 else (first, last)
        return pl.multiple_of(grads(p)[1] + (yy * 8 + 2 * s + xx) * UNITS[p] + off, 32)

    def slot(r, k):
        return pl.multiple_of(LAND[r] + k * ROUTES[r][2], 32)

    def rs(r, at, k, si, ri, t, n=1):
        m = ROUTES[r][2] * n
        return remote(
            grads(ROUTES[r][0])[0].at[pl.ds(at, m)],
            RL.at[pl.ds(slot(r, k), m)],
            rs_send.at[r, si],
            rs_recv.at[r, ri],
            t,
        )

    def rs_start(r, at, k, i, t):
        rs(r, at, k, i, i, t).start()

    def rs_wait(r, ri, n=1):
        rs(r, grads(ROUTES[r][0])[1], 0, 0, ri, xn, n).wait_recv()

    def add(r, at, *ks):
        ref, rows = grads(ROUTES[r][0])[0], pl.ds(at, ROUTES[r][2])
        total = ref[rows, :].astype(F32)
        for k in ks:
            total = total + RL[pl.ds(slot(r, k), ROUTES[r][2]), :].astype(F32)
        ref[rows, :] = total.astype(BF)

    def s1(r):
        if ROUTES[r][3] == 0:
            for s in (0, 2):
                rs_start(r, grow(r, 1 - x, s, 1 - y), s // 2, 0, yn)
            for s in (1, 3):
                rs_start(r, grow(r, 1 - x, s, 1 - y), 2 + s // 2, 1, xn)
            for s in (1, 3):
                rs_start(r, grow(r, 1 - x, s, y), 4 + s, 2, xn)
            for s in (0, 2):
                rs_start(r, grow(r, x, s, 1 - y), 8 + s, 4, yn)
            return
        _, last, _, ln = ends(r)
        for i, group in enumerate(((0, 3), (1, 2))):
            for s in group:
                for f in range(2):
                    rs_start(r, grow(r, f, s, 1 - last), 2 * s + f, i, ln)

    def s2a(r):
        rs_wait(r, 0, 2)
        for s in (0, 2):
            at = grow(r, 1 - x, s, y)
            add(r, at, s // 2)
            rs_start(r, at, 4 + s, 3, xn)

    def s2b(r):
        rs_wait(r, 1, 2)
        for s in (1, 3):
            at = grow(r, x, s, 1 - y)
            add(r, at, 2 + s // 2)
            rs_start(r, at, 8 + s, 5, yn)

    def s3a(r):
        rs_wait(r, 2, 2)
        rs_wait(r, 4, 2)
        for s in range(4):
            add(r, grow(r, x, s, y), 4 + s if s % 2 else 8 + s)

    def line_of(r):
        return ((x,), 12, 1) if ROUTES[r][3] == 0 else ((0, 1), 8, 2)

    def rs_up(r, t):
        firsts, base, n = line_of(r)
        for i, f in enumerate(firsts):
            rs_start(r, grow(r, f, t, ends(r)[1]), base + n * t + i, 6 + t, up)

    def rs_down(r, t):
        firsts, base, n = line_of(r)
        for i, f in enumerate(firsts):
            k = jnp.where(t == z - 1, 4, t)
            rs_start(r, grow(r, f, t, ends(r)[1]), base + n * k + i, 10 + t, dn)

    def s3b(r):
        rs_wait(r, 3, 2)
        rs_wait(r, 5, 2)
        for s in range(4):
            add(r, grow(r, x, s, y), 8 + s if s % 2 else 4 + s)

        @pl.when(z == 0)
        def _():
            for t in (3, 2, 1):
                rs_up(r, t)

        @pl.when(z == 3)
        def _():
            for t in (0, 1, 2):
                rs_down(r, t)

    def s2(r, i):
        rs_wait(r, i, 4)
        for s in ((0, 3), (1, 2))[i]:
            for f in range(2):
                add(r, grow(r, f, s, ends(r)[1]), 2 * s + f)

        @pl.when(z == 0)
        def _():
            for t in ((3,), (2, 1))[i]:
                rs_up(r, t)

        @pl.when(z == 3)
        def _():
            for t in ((0,), (1, 2))[i]:
                rs_down(r, t)

    def zu(r, t):
        @pl.when((z > 0) & (z < t))
        def _():
            firsts, base, n = line_of(r)
            rs_wait(r, 6 + t, n)
            for i, f in enumerate(firsts):
                add(r, grow(r, f, t, ends(r)[1]), base + n * t + i)
            rs_up(r, t)

    def zd(r, t):
        @pl.when((z < 3) & (z > t))
        def _():
            firsts, base, n = line_of(r)
            rs_wait(r, 10 + t, n)
            for i, f in enumerate(firsts):
                add(r, grow(r, f, t, ends(r)[1]), base + n * t + i)
            rs_down(r, t)

    def zf(r):
        firsts, base, n = line_of(r)
        first, last, fn, _ = ends(r)
        when(z > 0, lambda: rs_wait(r, 6 + z, n))
        when(z < 3, lambda: rs_wait(r, 10 + z, n))

        def both(*ks):
            for i, f in enumerate(firsts):
                add(r, grow(r, f, z, last), *[base + n * k + i for k in ks])

        when(z == 0, lambda: both(4))
        when(z == 3, lambda: both(3))
        when((z > 0) & (z < 3), lambda: both(z, 4))
        if n == 2:
            rs_start(r, grow(r, 1 - first, z, last), 18, 2, fn)

    def ff(r):
        first, last, _, _ = ends(r)
        rs_wait(r, 2)
        add(r, grow(r, first, z, last), 18)

    def conv_store(p):
        ref, base = grads(p)
        at = pl.multiple_of(base + (y * 8 + 2 * z + x) * CONV_UNIT, 32)
        return pltpu.make_async_copy(ref.at[pl.ds(at, CONV_UNIT)], conv_out.at[p], out_sem.at[p])

    def diagonal():
        shape = (64, 64)
        return lax.broadcasted_iota(jnp.int32, shape, 0) == lax.broadcasted_iota(jnp.int32, shape, 1)

    def tap_column(layer):
        wide = jnp.broadcast_to(tap_in[layer : layer + 1, :].astype(F32), (64, 64))
        return jnp.sum(jnp.where(diagonal(), wide, 0.0), axis=1, keepdims=True)

    def pf(p):
        if p < 3:
            conv_store(p).start()
            return
        layer = 5 - p
        base = pl.multiple_of(grads(p)[1] + (y * 8 + 2 * z + x) * HEAD_UNIT, 32)
        tiles = [GH[pl.ds(base + 64 * t, 64), :].astype(F32) for t in range(4)]
        total = jnp.zeros((64, 1), F32)
        for t in range(4):
            raw = RAW[layer, 64 * t : 64 * t + 64, :].astype(F32)
            total = total + jnp.sum(tiles[t] * raw, axis=1, keepdims=True)
        SB[0, :, layer : layer + 1] = total
        tap = tap_column(layer)
        tiles = [v * tap for v in tiles]
        rolled = [pltpu.roll(v, 64, 1) for v in tiles]
        left = lax.broadcasted_iota(jnp.int32, (64, 128), 1) < 64
        for t in range(4):
            later = rolled[t + 1] if t < 3 else rolled[t]
            v = jnp.where(c == 0, tiles[t], jnp.where(left, rolled[t], later))
            if t < 3:
                head_out[layer, :, 128 * t : 128 * t + 128] = v
            else:
                head_out[layer, :, 384:448] = v[:, 0:64]

    def rs_end(r):
        def done(si, n=1):
            rs(r, grads(ROUTES[r][0])[1], 0, si, 0, xn, n).wait_send()

        n = line_of(r)[2]
        if n == 1:
            for i in range(6):
                done(i, 2)
        else:
            done(0, 4)
            done(1, 4)
            done(2)
        for t in range(4):
            when((z < 3) & (z < t), lambda: done(6 + t, n))
            when((z > 0) & (z > t), lambda: done(10 + t, n))

    def share_ft(layer):
        return remote(FT.at[layer], FTP.at[layer], pair_send.at[layer], pair_recv.at[layer], pn)

    def share_nt(layer):
        i = 3 + layer
        src = GC2.at[pl.ds(0, 6 * 512)]
        return remote(src, NTP.at[layer % 2], pair_send.at[i], pair_recv.at[i], pn)

    def share_cot(k):
        src = COT.at[pl.ds(7 * k + 3 * (1 - c), 4)]
        return remote(src, COTP.at[k], pair_send.at[6 + k], pair_recv.at[6 + k], pn)

    def share_d(layer, k):
        i = 8 + 2 * layer + k
        src = F3.at[:, 2 * k + 1 - c]
        return remote(src, D3P.at[layer % 2, :, k], pair_send.at[i], pair_recv.at[i], pn)

    def blocks(count, fn):
        def step(m, carry):
            fn(m)
            return carry

        lax.fori_loop(0, count, step, 0)

    def at48(m, base=0):
        return pl.ds(pl.multiple_of(base + 48 * m, 8 if base == 8 else 16), 48)

    def place48():
        i = lax.broadcasted_iota(jnp.int32, (48, 1), 0)
        second = i >= HIGH
        return jnp.where(second, i - HIGH, i), jnp.where(second, 1, 0)

    def mask_of(m):
        r, second = place48()
        return jnp.where((r < height) & (2 * m + second < width), 1.0, 0.0).astype(F32)

    def image_part(i):
        src = (image_in, trunk_in)[i // 4].at[:, pl.ds(128 * (i % 4), 128)]
        return pltpu.make_async_copy(src, GC2.at[pl.ds(3072 + PIX * i, PIX)], in_sem.at[i])

    def cot_part(t):
        return pltpu.make_async_copy(
            cot_in.at[:, pl.ds(128 * t, 128)], COT.at[t, pl.ds(0, PIX)], in_sem.at[8 + t]
        )

    def expand(first, masked):
        def one(m):
            at = at48(m, 8)
            for k in range(4):
                rows = pl.ds(pl.multiple_of(3072 + PIX * (first + k) + 48 * m, 16), 48)
                v = GC2[rows, :].astype(F32)
                if masked:
                    v = v * mask_of(m)
                    SQ[0:1, 128 * k : 128 * k + 128] += jnp.sum(v * v, axis=0, keepdims=True)
                ACC[at, 128 * k : 128 * k + 128] = v

        blocks(14, one)

    def start():
        for p in range(3):
            load(p).start()
        for i in range(8):
            image_part(i).start()
        for t in range(14):
            cot_part(t).start()
        barrier = pltpu.get_barrier_semaphore()
        for t in (xn, yn, pn):
            pl.semaphore_signal(barrier, inc=1, device_id=t, device_id_type=MESH)
        when(
            z < 3, lambda: pl.semaphore_signal(barrier, inc=1, device_id=up, device_id_type=MESH)
        )
        when(
            z > 0, lambda: pl.semaphore_signal(barrier, inc=1, device_id=dn, device_id_type=MESH)
        )
        pl.semaphore_wait(barrier, jnp.where((z == 0) | (z == 3), 4, 5))

    def prep_heads():
        left = lax.broadcasted_iota(jnp.int32, (64, 128), 1) < 64
        HW[...] = jnp.zeros_like(HW)
        for layer in range(3):
            HW[:, 0:448] = head_in[layer].astype(F32)
            tap = tap_column(layer)
            base = row(5 - layer, y, c, z, x)
            tiles = [HW[:, 128 * t : 128 * t + 128] for t in range(4)]
            rolled = [pltpu.roll(v, 64, 1) for v in tiles]
            for t in range(4):
                before = rolled[t - 1] if t else jnp.zeros((64, 128), F32)
                v = jnp.where(c == 0, tiles[t], jnp.where(left, before, rolled[t]))
                RAW[layer, 64 * t : 64 * t + 64, :] = v.astype(BF)
                W[pl.ds(base + 64 * t, 64), :] = (v * tap).astype(BF)

    def prep_in():
        ACC[...] = jnp.zeros_like(ACC)
        SQ[...] = jnp.zeros_like(SQ)
        SB[0] = jnp.zeros((64, 128), F32)
        for b in range(3):
            for k in range(4):
                F3[b, k, 0:32, :] = jnp.zeros((32, 128), BF)
                F3[b, k, 704:832, :] = jnp.zeros((128, 128), BF)
        for i in range(4):
            image_part(i).wait()
        expand(0, True)
        pixels = (height * width).astype(F32) * (1.0 / 512.0)
        SQ[5:6, :] = jnp.full((1, 512), pixels, F32)

    def shifts():
        r, _ = place48()

        def one(m):
            v64 = ACC[pl.ds(pl.multiple_of(48 * m, 8), 64), :]
            for b in range(3):
                v = v64[7 + b : 55 + b, :]
                if b != 1:
                    v = jnp.where(r == (0 if b == 0 else HIGH - 1), 0.0, v)
                v = v.astype(BF)
                for k in range(4):
                    F3[b, k, at48(m, 32), :] = v[:, 128 * k : 128 * k + 128]

        blocks(14, one)

    def ft(layer):
        shifts()

        def one(m):
            v = ACC[pl.ds(pl.multiple_of(8 + 128 * m, 8), 128), :]
            FT[layer, :, pl.ds(pl.multiple_of(128 * m, 128), 128)] = v.T.astype(BF)

        blocks(6, one)
        share_ft(layer).start()

    def prep_cot():
        def clear(t):
            COT[t, PIX:PAD, :] = jnp.zeros((PAD - PIX, 128), BF)

        blocks(14, clear)
        for t in range(14):
            cot_part(t).wait()
        for k in range(2):
            share_cot(k).start()

    def taps(a, transposed):
        first = 8 + HIGH * a if not transposed else 8 + HIGH * (2 - a)
        order = (0, 1, 2) if not transposed else (2, 1, 0)
        return [
            jnp.concatenate([F3[b, k, first : first + PIX, :] for k in range(4)], axis=1)
            for b in order
        ]

    def weights(layer, a, b):
        first = BASES[layer] + 512 * (3 * b + a)
        return jnp.concatenate(
            [W[first + 4608 * k : first + 4608 * k + 512, :] for k in range(4)], axis=1
        )

    def conv(layer, a):
        v = jnp.dot(
            jnp.concatenate(taps(a, False), axis=1),
            jnp.concatenate([weights(layer, a, b) for b in range(3)], axis=0),
            preferred_element_type=F32,
        )
        if a == 0:
            ACC[8 : 8 + PIX, :] = v
        else:
            ACC[8 : 8 + PIX, :] += v

    def act(layer):
        gain, offset = gain_in[layer : layer + 1, :], offset_in[layer : layer + 1, :]
        k = 0.7978845608028654

        def one(m):
            rows, at = at48(m, 8), at48(m)
            u = ACC[rows, :] * gain + offset
            mask = mask_of(m)
            u2 = u * u
            t = jnp.tanh(k * u * (1.0 + 0.044715 * u2))
            half = 0.5 * (1.0 + t) * mask
            f = u * half
            slope = half + (0.5 * k) * mask * u * (1.0 - t * t) * (1.0 + 0.134145 * u2)
            squares = f * f
            rn = lax.rsqrt(jnp.mean(squares, axis=-1, keepdims=True) + 1e-5)
            GP[layer, at, :] = (slope * gain).astype(BF)
            N[layer, at, :] = (f * rn).astype(BF)
            RN[at, layer : layer + 1] = rn
            SQ[layer + 1 : layer + 2, :] += jnp.sum(squares, axis=0, keepdims=True)
            if layer < 2:
                ACC[rows, :] = f
            else:
                v = f.astype(BF)
                for b in range(4):
                    F3[1, b, at48(m, 32), :] = v[:, 128 * b : 128 * b + 128]

        blocks(14, one)
        if layer == 2:
            for b in range(4):
                trunk_store(b).start()

    def trunk_store(b):
        return pltpu.make_async_copy(
            F3.at[1, b, pl.ds(32, PIX)], trunk_out.at[:, pl.ds(128 * b, 128)], out_sem.at[6 + b]
        )

    def nt(layer):
        if layer > 0:
            share_nt(layer - 1).wait_send()

        for m in range(6):
            v = N[layer, 128 * m : min(128 * m + 128, PIX), :].astype(F32)
            if m == 5:
                v = jnp.concatenate([v, jnp.zeros((PAD - PIX, 512), F32)], axis=0)
            GC2[512 * m : 512 * m + 512, :] = v.T.astype(BF)
        share_nt(layer).start()

    def head_grads(layer, k):
        if k == 0:
            share_nt(layer).wait_recv()
        if layer == 0:
            share_cot(k).wait_recv()
        mine = [GC2[512 * m : 512 * m + 512, :] for m in range(6)]
        theirs = [NTP[layer % 2, 512 * m : 512 * m + 512, :] for m in range(6)]
        own = jnp.concatenate([COT[7 * k + 3 * c + i] for i in range(4)], axis=1)
        other = jnp.concatenate([COTP[k, i] for i in range(4)], axis=1)
        v = jnp.dot(
            jnp.concatenate(mine + theirs, axis=1),
            jnp.concatenate([own, other], axis=0),
            preferred_element_type=F32,
        ).astype(BF)
        base = grads(5 - layer)[1] + k * 8 * HEAD_UNIT
        for f in range(8):
            for t in range(4):
                r = base + f * HEAD_UNIT + 64 * t
                GH[r : r + 64, :] = v[64 * f : 64 * f + 64, 128 * t : 128 * t + 128]

    def head_block(layer, d):
        base = BASES[5 - layer] + d * 8 * HEAD_UNIT

        def tile(f, t):
            first = base + HEAD_UNIT * f + 64 * t
            return W[first : first + 64, :]

        return jnp.concatenate(
            [jnp.concatenate([tile(f, t) for f in range(8)], axis=0) for t in range(4)], axis=1
        )

    def at224(m):
        return pl.ds(pl.multiple_of(224 * m, 32), 224)

    def dtap(layer):
        def one(m):
            at = at224(m)
            h = jnp.zeros((224, 512), F32)
            for d in range(4):
                first = 7 * (d // 2) + 3 * (d % 2)
                left = jnp.concatenate([COT[first + i, at, :] for i in range(4)], axis=1)
                h = h + lax.dot_general(
                    left, head_block(layer, d), (((1,), (1,)), ((), ())), preferred_element_type=F32
                )
            n = N[layer, at, :].astype(F32)
            mean = jnp.mean(h * n, axis=-1, keepdims=True)
            DT[layer, at, :] = ((h - n * mean) * RN[at, layer : layer + 1]).astype(BF)

        blocks(3, one)

    def joined(k):
        if k == 0:
            for i in range(2):
                share_cot(i).wait_send()

        def one(m):
            at = at224(m)
            left = jnp.concatenate([N[i, at, :] for i in range(3)], axis=1)
            low, high = [
                jnp.dot(
                    left,
                    jnp.concatenate([head_block(i, 2 * k + half) for i in range(3)], axis=0),
                    preferred_element_type=F32,
                )
                for half in range(2)
            ]
            tiles = [low[:, 128 * i : 128 * i + 128] for i in range(3)]
            tiles.append(low[:, 384:512] + high[:, 0:128])
            tiles += [high[:, 128 * i : 128 * i + 128] for i in range(1, 4)]
            total = jnp.zeros((1, 128), F32)
            for i, v in enumerate(tiles):
                total = total + jnp.sum(v * v, axis=0, keepdims=True)
                COT[7 * k + i, at, :] = v.astype(BF)
            SQ[4:5, 0:128] += total

        blocks(3, one)
        for i in range(7):
            heads_store(7 * k + i).start()

    def heads_store(t):
        return pltpu.make_async_copy(
            COT.at[t, pl.ds(0, PIX)], heads_out.at[:, pl.ds(128 * t, 128)], in_sem.at[8 + t]
        )

    def trunk_cot():
        for i in range(4, 8):
            image_part(i).wait()
        expand(4, False)

    def dlinear(layer):
        def one(m):
            rows, at = at48(m, 8), at48(m)
            g = ACC[rows, :] + DT[layer, at, :].astype(F32)
            ACC[rows, :] = g * GP[layer, at, :].astype(F32)

        blocks(14, one)
        if layer == 2:
            for b in range(4):
                trunk_store(b).wait()
        else:
            for k in range(2):
                share_d(layer + 1, k).wait_send()
        shifts()
        for k in range(2):
            share_d(layer, k).start()

    def conv_back(layer, a):
        v = lax.dot_general(
            jnp.concatenate(taps(a, True), axis=1),
            jnp.concatenate([weights(layer, a, b) for b in range(3)], axis=1),
            (((1,), (1,)), ((), ())),
            preferred_element_type=F32,
        )
        if a == 0:
            ACC[8 : 8 + PIX, :] = v
        else:
            ACC[8 : 8 + PIX, :] += v

    def conv_grads(layer, a):
        if a == 0:
            share_ft(layer).wait_recv()
            for k in range(2):
                share_d(layer, k).wait_recv()
            if layer == 2:
                share_nt(2).wait_send()
            if layer == 1:
                for r, route in enumerate(ROUTES):
                    if route[0] == 2:
                        ag_end(r)
        first = 8 + HIGH * (2 - a)
        rows = slice(first, first + PAD)
        own = [F3[2 - b, 2 * k + c, rows, :] for b in range(3) for k in range(2)]
        other = [D3P[layer % 2, 2 - b, k, rows, :] for b in range(3) for k in range(2)]
        v = jnp.dot(
            jnp.concatenate([FT[layer], FTP[layer]], axis=1),
            jnp.concatenate(
                [jnp.concatenate(own, axis=1), jnp.concatenate(other, axis=1)], axis=0
            ),
            preferred_element_type=F32,
        ).astype(BF)
        ref, base = grads(layer)
        for b in range(3):
            for k in range(2):
                r = base + 4608 * k + 512 * (3 * b + a)
                at = 256 * b + 128 * k
                ref[r : r + 512, :] = v[:, at : at + 128]

    def image_store():
        return pltpu.make_async_copy(DT.at[2], image_out, out_sem.at[10])

    def image_grad():
        def one(m):
            DT[2, at48(m), :] = (ACC[at48(m, 8), :] * mask_of(m)).astype(BF)

        blocks(14, one)
        image_store().start()

    def small(i):
        return remote(LB.at[i], MR.at[i], small_send.at[i], small_recv.at[i], (pn, xn, yn)[i])

    def line(s, i, t):
        return remote(ZB.at[s], ZB.at[s], small_send.at[i], small_recv.at[5 + s], t)

    def m0():
        v = SQ[:, 0:128]
        for i in range(1, 4):
            v = v + SQ[:, 128 * i : 128 * i + 128]
        LB[0] = v
        small(0).start()

    def m1(i):
        small(i).wait_recv()
        v = LB[i] + MR[i]
        if i < 2:
            LB[i + 1] = v
            small(i + 1).start()
            return
        ZB[z] = v
        when(z < 3, lambda: line(z, 5 + z, up).start())
        when(z > 0, lambda: line(z, 9 + z, dn).start())

    def m2(j):
        s = sig[j]
        line(s, 5, up).wait_recv()
        when((s < z) & (z < 3), lambda: line(s, 5 + s, up).start())
        when((s > z) & (z > 0), lambda: line(s, 9 + s, dn).start())

    def m3():
        total = ZB[0] + ZB[1] + ZB[2] + ZB[3]
        v = jnp.sum(total, axis=1, keepdims=True)
        which = lax.broadcasted_iota(jnp.int32, (8, 1), 0)
        wide = jnp.where(which == 4, 1792.0, 512.0).astype(F32)
        rms_out[...] = jnp.broadcast_to(jnp.sqrt(v / (v[5:6] * wide)), (8, 128))

    def scale_sum(i):
        return remote(SB.at[i], SR.at[i], small_send.at[3 + i], small_recv.at[3 + i], (pn, yn)[i])

    def t0():
        scale_sum(0).start()

    def t1():
        scale_sum(0).wait_recv()
        SB[1] = SB[0] + SR[0]
        scale_sum(1).start()

    def t2():
        scale_sum(1).wait_recv()
        total = SB[1] + SR[1]
        for layer in range(3):
            v = jnp.where(diagonal(), total[:, layer : layer + 1], 0.0)
            scale_out[layer : layer + 1, :] = jnp.sum(v, axis=0, keepdims=True)

    def finish():
        for r, route in enumerate(ROUTES):
            if route[0] != 2:
                ag_end(r)
            rs_end(r)
        for i in range(3):
            share_ft(i).wait_send()
            small(i).wait_send()
            conv_store(i).wait()
        for k in range(2):
            share_d(0, k).wait_send()
            scale_sum(k).wait_send()
        for s in range(4):
            when((z < 3) & (s <= z), lambda s=s: line(s, 5 + s, up).wait_send())
            when((z > 0) & (s >= z), lambda s=s: line(s, 9 + s, dn).wait_send())
        for t in range(14):
            heads_store(t).wait()
        image_store().wait()

    fns = dict(
        start=start, ld=ld, e0=e0, f1=f1, zj=zj, lj=lj, xd=xd, yd=yd, xf=xf, yf=yf, pw=pw,
        s1=s1, s2a=s2a, s2b=s2b, s3a=s3a, s3b=s3b, s2=s2, zu=zu, zd=zd, zf=zf, ff=ff, pf=pf,
        prep_heads=prep_heads, prep_in=prep_in, prep_cot=prep_cot, ft=ft, conv=conv, act=act, nt=nt,
        head_grads=head_grads, dtap=dtap, joined=joined, trunk_cot=trunk_cot,
        dlinear=dlinear, conv_back=conv_back, conv_grads=conv_grads, image_grad=image_grad,
        m0=m0, m1=m1, m2=m2, m3=m3, t0=t0, t1=t1, t2=t2, finish=finish,
    )
    for name, *args in order:
        fns[name](*args)


def patches(feature):
    height = feature.shape[1]
    breadth = feature.shape[2]
    padded = jnp.pad(feature, ((0, 0), (1, 1), (1, 1), (0, 0)))
    pieces = [
        padded[:, down_step : down_step + height, side_step : side_step + breadth, :]
        for down_step in range(3)
        for side_step in range(3)
    ]
    return jnp.concatenate(pieces, axis=-1)


def unpatch(stacked, channels):
    images, height, breadth, _ = stacked.shape
    padded = jnp.zeros((images, height + 2, breadth + 2, channels), jnp.float32)
    for down_step in range(3):
        for side_step in range(3):
            tap_index = 3 * down_step + side_step
            padded = padded.at[
                :, down_step : down_step + height, side_step : side_step + breadth, :
            ].add(stacked[..., tap_index * channels : (tap_index + 1) * channels])
    return padded[:, 1:-1, 1:-1, :]


def activate(linear, gain_vec, offsets, valid_mask):
    return valid_mask * jax.nn.gelu(linear * gain_vec + offsets)


def tap_piece(feature, scale_vec):
    return (
        feature * lax.rsqrt(jnp.mean(feature * feature, axis=-1, keepdims=True) + 1e-05) * scale_vec
    )


def general(
    inputs,
    heights,
    widths,
    conv_weights,
    affine_scale,
    affine_shift,
    tap_scales,
    head_weights,
    trunk_cot,
    heads_cot,
):
    images, height, breadth, channels = inputs.shape
    layer_count = conv_weights.shape[0]
    row_ids = jnp.arange(height, dtype=jnp.int32)
    col_ids = jnp.arange(breadth, dtype=jnp.int32)
    valid = (row_ids[None, :, None] < heights[:, None, None]) & (
        col_ids[None, None, :] < widths[:, None, None]
    )
    valid_mask = jnp.where(valid, 1.0, 0.0).astype(jnp.float32)[..., None]
    conv_cols, head_cols = (
        lax.all_gather(conv_weights, "dp", axis=2, tiled=True),
        lax.all_gather(head_weights, "dp", axis=2, tiled=True),
    )
    conv_full, head_full, scale_full = (
        lax.all_gather(conv_cols, "fsdp", axis=1, tiled=True),
        lax.all_gather(head_cols, "fsdp", axis=1, tiled=True),
        lax.all_gather(tap_scales, "fsdp", axis=1, tiled=True),
    )
    outputs_wide = head_full.shape[2]
    feature = inputs.astype(jnp.float32) * valid_mask
    squares = [jnp.sum(feature * feature)]
    entering = inputs * valid_mask.astype(jnp.bfloat16)
    kept_in, kept_linear, kept_feature, kept_tap = ([], [], [], [])
    summed = jnp.zeros((images, height, breadth, outputs_wide), jnp.float32)
    for layer_index in range(layer_count):
        stacked = patches(entering)
        linear = jnp.einsum(
            "ghwk,kc->ghwc", stacked, conv_full[layer_index], preferred_element_type=jnp.float32
        )
        feature = activate(linear, affine_scale[layer_index], affine_shift[layer_index], valid_mask)
        tapped = tap_piece(feature, scale_full[layer_index].astype(jnp.float32)).astype(
            jnp.bfloat16
        )
        summed = summed + jnp.einsum(
            "ghwc,co->ghwo", tapped, head_full[layer_index], preferred_element_type=jnp.float32
        )
        kept_in.append(entering)
        kept_linear.append(linear)
        kept_feature.append(feature)
        kept_tap.append(tapped)
        squares.append(jnp.sum(feature * feature))
        entering = feature.astype(jnp.bfloat16)
    squares.append(jnp.sum(summed * summed))
    square_total, pixels = lax.psum((jnp.stack(squares), jnp.sum(valid_mask)), ("dp", "fsdp"))
    divisors = jnp.array([channels] * (layer_count + 1) + [outputs_wide], jnp.float32)
    rms = jnp.sqrt(square_total / (pixels * divisors))
    conv_back, head_back, scale_back = conv_full, head_full, scale_full
    grad_conv = [None] * layer_count
    grad_scale = [None] * layer_count
    grad_head = [None] * layer_count
    grad_feature = trunk_cot.astype(jnp.float32)
    for layer_index in reversed(range(layer_count)):
        grad_head[layer_index] = jnp.einsum(
            "ghwc,ghwo->co", kept_tap[layer_index], heads_cot, preferred_element_type=jnp.float32
        )
        grad_tapped = jnp.einsum(
            "ghwo,co->ghwc", heads_cot, head_back[layer_index], preferred_element_type=jnp.float32
        )
        _, pullback = jax.vjp(
            tap_piece, kept_feature[layer_index], scale_back[layer_index].astype(jnp.float32)
        )
        feature_part, scale_part = pullback(grad_tapped)
        grad_scale[layer_index] = scale_part
        grad_feature = grad_feature + feature_part
        local_act = partial(
            activate,
            gain_vec=affine_scale[layer_index],
            offsets=affine_shift[layer_index],
            valid_mask=valid_mask,
        )
        _, pullback = jax.vjp(local_act, kept_linear[layer_index])
        (grad_linear,) = pullback(grad_feature)
        low_linear = grad_linear.astype(jnp.bfloat16)
        grad_conv[layer_index] = jnp.einsum(
            "ghwk,ghwc->kc",
            patches(kept_in[layer_index]),
            low_linear,
            preferred_element_type=jnp.float32,
        )
        spread = jnp.einsum(
            "ghwc,kc->ghwk", low_linear, conv_back[layer_index], preferred_element_type=jnp.float32
        )
        grad_feature = unpatch(spread, channels)
    input_grad = (grad_feature * valid_mask).astype(jnp.bfloat16)
    stacked_conv = jnp.stack(grad_conv)
    stacked_head = jnp.stack(grad_head)
    stacked_scale = jnp.stack(grad_scale)
    dp_count = lax.axis_size("dp")
    part_conv, part_head, part_scale = (
        lax.psum_scatter(
            stacked_conv.astype(jnp.bfloat16), "fsdp", scatter_dimension=1, tiled=True
        ).astype(jnp.float32),
        lax.psum_scatter(
            stacked_head.astype(jnp.bfloat16), "fsdp", scatter_dimension=1, tiled=True
        ).astype(jnp.float32),
        lax.psum_scatter(
            stacked_scale.astype(jnp.bfloat16), "fsdp", scatter_dimension=1, tiled=True
        ).astype(jnp.float32),
    )
    spread_scale = jnp.broadcast_to(part_scale[:, :, None], part_scale.shape + (dp_count,))
    conv_grad, head_grad, scale_cols = (
        lax.psum_scatter(
            part_conv.astype(jnp.bfloat16), "dp", scatter_dimension=2, tiled=True
        ).astype(jnp.float32),
        lax.psum_scatter(
            part_head.astype(jnp.bfloat16), "dp", scatter_dimension=2, tiled=True
        ).astype(jnp.float32),
        lax.psum_scatter(
            spread_scale.astype(jnp.bfloat16), "dp", scatter_dimension=2, tiled=True
        ).astype(jnp.float32),
    )
    scale_grad = scale_cols[:, :, 0]
    trunk_out = kept_feature[-1].astype(jnp.bfloat16)
    heads_out = summed.astype(jnp.bfloat16)
    return (trunk_out, heads_out, input_grad, conv_grad, scale_grad, head_grad, rms)


def fused(
    inputs,
    heights,
    widths,
    conv_weights,
    affine_scale,
    affine_shift,
    tap_scales,
    head_weights,
    trunk_cot,
    heads_cot,
):
    hbm = pl.BlockSpec(memory_space=pl.ANY)
    vmem = pl.BlockSpec(memory_space=pltpu.VMEM)
    smem = pl.BlockSpec(memory_space=pltpu.SMEM)
    dma = pltpu.SemaphoreType.DMA
    count = len(ROUTES)

    def flat(v):
        return v[0].transpose(1, 0, 2).reshape(PIX, v.shape[3])

    results = pl.pallas_call(
        partial(kernel, ORDER),
        name="conv_block",
        out_shape=(
            jax.ShapeDtypeStruct((PIX, 512), BF),
            jax.ShapeDtypeStruct((PIX, 1792), BF),
            jax.ShapeDtypeStruct((PIX, 512), BF),
            jax.ShapeDtypeStruct((3, 576, 128), BF),
            jax.ShapeDtypeStruct((3, 64, 448), F32),
            jax.ShapeDtypeStruct((3, 64), F32),
            jax.ShapeDtypeStruct((8, 128), F32),
        ),
        in_specs=[hbm, vmem, vmem, vmem, vmem, smem, smem, hbm, hbm, hbm],
        out_specs=(hbm, hbm, hbm, hbm, vmem, vmem, vmem),
        scratch_shapes=[
            pltpu.VMEM((ROWS, 128), BF),
            pltpu.VMEM((3, 4, 832, 128), BF),
            pltpu.VMEM((3, 512, PAD), BF),
            pltpu.VMEM((3, 512, PAD), BF),
            pltpu.VMEM((2, 6 * 512, 128), BF),
            pltpu.VMEM((3, PIX, 512), BF),
            pltpu.VMEM((3, PIX, 512), BF),
            pltpu.VMEM((3, PIX, 512), BF),
            pltpu.VMEM((PIX, 128), F32),
            pltpu.VMEM((14, PAD, 128), BF),
            pltpu.VMEM((2, 4, PAD, 128), BF),
            pltpu.VMEM((16 + PAD, 512), F32),
            pltpu.VMEM((2, 3, 2, 832, 128), BF),
            pltpu.VMEM((16 * CONV_UNIT, 128), BF),
            pltpu.VMEM((3 * 16 * HEAD_UNIT, 128), BF),
            pltpu.VMEM((LAND[-1], 128), BF),
            pltpu.VMEM((3, HEAD_UNIT, 128), BF),
            pltpu.VMEM((64, 512), F32),
            pltpu.VMEM((8, 512), F32),
            pltpu.VMEM((3, 8, 128), F32),
            pltpu.VMEM((3, 8, 128), F32),
            pltpu.VMEM((4, 8, 128), F32),
            pltpu.VMEM((2, 64, 128), F32),
            pltpu.VMEM((2, 64, 128), F32),
            dma((count, 24)),
            dma((count, 29)),
            dma((3,)),
            dma((count, 14)),
            dma((count, 14)),
            dma((14,)),
            dma((14,)),
            dma((22,)),
            dma((11,)),
            dma((9,)),
            dma((13,)),
        ],
        compiler_params=pltpu.CompilerParams(
            collective_id=0, has_side_effects=True, vmem_limit_bytes=64 * 2**20
        ),
        cost_estimate=pl.CostEstimate(
            flops=45_000_000_000, bytes_accessed=16_000_000, transcendentals=1_200_000
        ),
    )(
        conv_weights,
        head_weights,
        tap_scales,
        affine_scale,
        affine_shift,
        heights,
        widths,
        flat(inputs),
        flat(trunk_cot),
        flat(heads_cot),
    )
    trunk, heads, image, conv_grad, head_grad, scale_grad, rms = results

    def image_of(v):
        return v.reshape(28, HIGH, v.shape[1]).transpose(1, 0, 2)[None]

    return (
        image_of(trunk),
        image_of(heads),
        image_of(image),
        conv_grad.astype(F32),
        scale_grad,
        head_grad,
        rms[:5, 0],
    )


def solution(mesh):
    in_specs = (
        P(("dp", "fsdp"), None, None, None),
        P(("dp", "fsdp")),
        P(("dp", "fsdp")),
        P(None, "fsdp", "dp"),
        P(),
        P(),
        P(None, "fsdp"),
        P(None, "fsdp", "dp"),
        P(("dp", "fsdp"), None, None, None),
        P(("dp", "fsdp"), None, None, None),
    )
    out_specs = (
        P(("dp", "fsdp"), None, None, None),
        P(("dp", "fsdp"), None, None, None),
        P(("dp", "fsdp"), None, None, None),
        P(None, "fsdp", "dp"),
        P(None, "fsdp"),
        P(None, "fsdp", "dp"),
        P(),
    )
    body = fused if dict(mesh.shape) == {"dp": 4, "fsdp": 8} else general
    return jax.shard_map(body, mesh=mesh, in_specs=in_specs, out_specs=out_specs, check_vma=False)
```

```python
from functools import partial

import jax
import jax.numpy as jnp
from jax import lax
from jax.experimental import pallas as pl
from jax.experimental.pallas import tpu as pltpu
from jax.sharding import PartitionSpec as P

MESH = pl.DeviceIdType.MESH
F32, BF = jnp.float32, jnp.bfloat16

CONV_UNIT, HEAD_UNIT = 576, 224
UNITS = (CONV_UNIT,) * 3 + (HEAD_UNIT,) * 3
BASES = tuple(32 * sum(UNITS[:p]) for p in range(6))
ROWS = 32 * sum(UNITS)
ROUTES = (
    (0, 0, 256, 0),
    (0, 256, 160, 1),
    (0, 416, 160, 2),
    (1, 0, 256, 0),
    (1, 256, 160, 1),
    (1, 416, 160, 2),
    (2, 0, 192, 0),
    (2, 192, 192, 1),
    (2, 384, 192, 2),
    (3, 0, 224, 0),
    (4, 0, 224, 1),
    (5, 0, 224, 2),
)
BACK = (
    (0, 0, 256, 0),
    (0, 256, 160, 1),
    (0, 416, 160, 2),
    (1, 0, 192, 0),
    (1, 192, 192, 1),
    (1, 384, 192, 2),
    (2, 0, 192, 0),
    (2, 192, 192, 1),
    (2, 384, 192, 2),
    (3, 0, 224, 0),
    (4, 0, 224, 1),
    (5, 0, 224, 2),
)
SLOTS = (17, 19, 19, 23, 23)
LAND = tuple(sum(SLOTS[k] * m for _, _, m, k in BACK[:r]) for r in range(len(BACK) + 1))
HIGH, PIX, PAD = 24, 672, 768
ORDER = (
    ("start",),
    ("ld", 0),
    ("e0", 0),
    ("e0", 1),
    ("prep_heads",),
    ("e0", 2),
    ("ld", 1),
    ("e0", 5),
    ("e0", 4),
    ("prep_in",),
    ("zj", 1, 1, 0),
    ("f1", 1),
    ("zj", 0, 1),
    ("f1", 2),
    ("e0", 3),
    ("zj", 1, 1, 1),
    ("zj", 2, 1, 0),
    ("xd", 0, 0),
    ("zj", 2, 2, 0),
    ("f1", 4),
    ("zj", 0, 2),
    ("zj", 0, 3),
    ("lj", 2, 0),
    ("zj", 2, 1, 1),
    ("yd", 0, 0),
    ("lj", 1, 0),
    ("xd", 0, 1),
    ("yd", 0, 1),
    ("zj", 3, 1),
    ("zj", 2, 2, 1),
    ("ld", 2),
    ("zj", 1, 2, 0),
    ("zj", 1, 2, 1),
    ("zj", 2, 3, 0),
    ("xd", 0, 2),
    ("ft", 0),
    ("yd", 0, 2),
    ("zj", 1, 3, 1),
    ("zj", 2, 3, 1),
    ("f1", 5),
    ("yd", 0, 3),
    ("zj", 1, 3, 0),
    ("prep_cot",),
    ("lj", 2, 1),
    ("xd", 0, 3),
    ("zj", 3, 2),
    ("lj", 1, 1),
    ("yd", 3, 0),
    ("e0", 8),
    ("lj", 2, 2),
    ("zj", 5, 1, 0),
    ("zj", 4, 1, 1),
    ("xd", 3, 0),
    ("e0", 7),
    ("zj", 4, 1, 0),
    ("e0", 6),
    ("zj", 4, 2, 1),
    ("lj", 1, 2),
    ("lj", 2, 3),
    ("lj", 1, 3),
    ("xf", 0, 0),
    ("xf", 0, 1),
    ("yf", 0, 0),
    ("zj", 3, 3),
    ("yd", 3, 1),
    ("yf", 0, 1),
    ("zj", 5, 1, 1),
    ("xd", 3, 1),
    ("lj", 5, 0),
    ("zj", 4, 3, 1),
    ("lj", 4, 0),
    ("pw", 1),
    ("zj", 5, 2, 0),
    ("pw", 2),
    ("f1", 8),
    ("pw", 0),
    ("conv", 0, 0),
    ("conv", 0, 1),
    ("conv", 0, 2),
    ("zj", 5, 2, 1),
    ("zj", 4, 2, 0),
    ("zj", 6, 1),
    ("zj", 5, 3, 0),
    ("f1", 7),
    ("act", 0),
    ("zj", 4, 3, 0),
    ("zj", 5, 3, 1),
    ("xd", 3, 2),
    ("nt", 0),
    ("lj", 4, 1),
    ("yd", 3, 2),
    ("yd", 3, 3),
    ("zj", 8, 1, 0),
    ("xd", 3, 3),
    ("zj", 6, 2),
    ("yf", 3, 0),
    ("lj", 5, 1),
    ("lj", 5, 2),
    ("xf", 3, 0),
    ("yd", 6, 0),
    ("zj", 8, 2, 0),
    ("zj", 6, 3),
    ("zj", 8, 1, 1),
    ("lj", 4, 2),
    ("head_grads", 0, 0),
    ("xd", 6, 0),
    ("e0", 9),
    ("lj", 4, 3),
    ("lj", 5, 3),
    ("zj", 7, 1, 0),
    ("yd", 6, 1),
    ("head_grads", 0, 1),
    ("zj", 7, 1, 1),
    ("lj", 8, 0),
    ("zj", 7, 2, 0),
    ("xd", 6, 1),
    ("yf", 3, 1),
    ("lj", 7, 0),
    ("xf", 3, 1),
    ("zj", 8, 2, 1),
    ("pw", 5),
    ("yd", 6, 2),
    ("ft", 1),
    ("pw", 4),
    ("zj", 7, 2, 1),
    ("xd", 6, 2),
    ("yd", 6, 3),
    ("pw", 3),
    ("zj", 8, 3, 0),
    ("conv", 1, 0),
    ("zj", 7, 3, 1),
    ("conv", 1, 1),
    ("xd", 6, 3),
    ("zj", 8, 3, 1),
    ("zj", 7, 3, 0),
    ("conv", 1, 2),
    ("zj", 9, 1),
    ("lj", 7, 1),
    ("e0", 10),
    ("xf", 6, 0),
    ("e0", 11),
    ("lj", 8, 1),
    ("act", 1),
    ("xf", 6, 1),
    ("yf", 6, 0),
    ("lj", 7, 2),
    ("zj", 9, 2),
    ("lj", 8, 2),
    ("zj", 9, 3),
    ("yd", 9, 0),
    ("yf", 6, 1),
    ("xd", 9, 0),
    ("lj", 8, 3),
    ("lj", 7, 3),
    ("nt", 1),
    ("ft", 2),
    ("pw", 8),
    ("yd", 9, 1),
    ("pw", 6),
    ("xd", 9, 1),
    ("pw", 7),
    ("conv", 2, 0),
    ("conv", 2, 1),
    ("f1", 10),
    ("zj", 10, 1, 0),
    ("zj", 11, 1, 0),
    ("head_grads", 1, 0),
    ("xd", 9, 2),
    ("head_grads", 1, 1),
    ("xd", 9, 3),
    ("yd", 9, 2),
    ("zj", 10, 2, 0),
    ("yf", 9, 0),
    ("yd", 9, 3),
    ("xf", 9, 0),
    ("s1", 10),
    ("s1", 11),
    ("conv", 2, 2),
    ("act", 2),
    ("yf", 9, 1),
    ("xf", 9, 1),
    ("trunk_cot",),
    ("f1", 11),
    ("zj", 10, 1, 1),
    ("nt", 2),
    ("pw", 9),
    ("unpack", 2),
    ("zj", 10, 2, 1),
    ("dtap", 2),
    ("zj", 10, 3, 0),
    ("head_grads", 2, 0),
    ("zj", 11, 2, 0),
    ("dlinear", 2),
    ("zj", 10, 3, 1),
    ("head_grads", 2, 1),
    ("zj", 11, 3, 0),
    ("zj", 11, 1, 1),
    ("s2", 10, 0),
    ("s1", 9),
    ("conv_back", 2, 0),
    ("lj", 10, 0),
    ("s2", 10, 1),
    ("conv_grads", 2, 0),
    ("conv_grads", 2, 1),
    ("lj", 10, 1),
    ("zj", 11, 2, 1),
    ("s2", 11, 0),
    ("conv_back", 2, 1),
    ("lj", 10, 2),
    ("lj", 11, 0),
    ("conv_back", 2, 2),
    ("lj", 10, 3),
    ("lj", 11, 1),
    ("s2a", 9),
    ("conv_grads", 2, 2),
    ("pw", 10),
    ("s2", 11, 1),
    ("s2b", 9),
    ("s1", 8),
    ("s1", 7),
    ("unpack", 1),
    ("dtap", 1),
    ("lj", 11, 2),
    ("dlinear", 1),
    ("s3a", 9),
    ("conv_back", 1, 0),
    ("s3b", 9),
    ("s2", 8, 0),
    ("zj", 11, 3, 1),
    ("zd", 11, 0),
    ("conv_back", 1, 1),
    ("s1", 6),
    ("conv_grads", 1, 0),
    ("s2", 7, 0),
    ("conv_grads", 1, 1),
    ("lj", 11, 3),
    ("conv_grads", 1, 2),
    ("s1", 5),
    ("zd", 10, 0),
    ("s2", 7, 1),
    ("pw", 11),
    ("s1", 4),
    ("s2", 8, 1),
    ("unpack", 0),
    ("conv_back", 1, 2),
    ("zd", 9, 0),
    ("dtap", 0),
    ("zd", 8, 0),
    ("dlinear", 0),
    ("zd", 7, 0),
    ("zu", 9, 3),
    ("s2", 4, 0),
    ("s2b", 6),
    ("zd", 9, 1),
    ("zu", 8, 3),
    ("zd", 10, 1),
    ("s1", 3),
    ("conv_back", 0, 0),
    ("s2a", 6),
    ("zd", 7, 1),
    ("zu", 11, 3),
    ("zu", 9, 2),
    ("s2", 5, 1),
    ("conv_grads", 0, 0),
    ("conv_grads", 0, 1),
    ("zu", 7, 3),
    ("conv_grads", 0, 2),
    ("s1", 1),
    ("s1", 2),
    ("zu", 10, 3),
    ("zd", 8, 1),
    ("zd", 11, 1),
    ("s2", 5, 0),
    ("s3a", 6),
    ("s3b", 6),
    ("joined", 0),
    ("zu", 4, 3),
    ("conv_back", 0, 1),
    ("s2a", 3),
    ("zu", 5, 3),
    ("s2b", 3),
    ("s2", 1, 0),
    ("s3a", 3),
    ("zu", 6, 3),
    ("s2", 2, 0),
    ("joined", 1),
    ("s1", 0),
    ("m0",),
    ("zu", 1, 3),
    ("s2", 4, 1),
    ("zu", 2, 3),
    ("zu", 11, 2),
    ("zu", 10, 2),
    ("zu", 8, 2),
    ("zd", 6, 0),
    ("s2", 1, 1),
    ("zu", 7, 2),
    ("zf", 9),
    ("zu", 1, 2),
    ("zu", 6, 2),
    ("zd", 2, 0),
    ("m1", 0),
    ("zf", 11),
    ("s2", 2, 1),
    ("zd", 4, 0),
    ("pf", 3),
    ("s3b", 3),
    ("s2a", 0),
    ("zu", 2, 2),
    ("zd", 5, 0),
    ("s2b", 0),
    ("zf", 10),
    ("conv_back", 0, 2),
    ("zu", 4, 2),
    ("zd", 1, 0),
    ("image_grad",),
    ("m1", 1),
    ("ff", 11),
    ("zd", 2, 1),
    ("zu", 5, 2),
    ("pf", 5),
    ("zf", 8),
    ("s3a", 0),
    ("zf", 7),
    ("zd", 3, 0),
    ("s3b", 0),
    ("zd", 0, 0),
    ("zd", 1, 1),
    ("zd", 5, 1),
    ("m1", 2),
    ("zd", 4, 1),
    ("m2", 1),
    ("ff", 10),
    ("zd", 6, 1),
    ("zd", 0, 1),
    ("zu", 0, 3),
    ("zd", 3, 1),
    ("pf", 4),
    ("t0",),
    ("zf", 2),
    ("zu", 3, 3),
    ("ff", 7),
    ("ff", 8),
    ("zf", 1),
    ("zu", 3, 2),
    ("zu", 0, 2),
    ("zf", 5),
    ("t1",),
    ("zf", 4),
    ("m2", 2),
    ("m2", 3),
    ("m3",),
    ("zf", 6),
    ("ff", 2),
    ("ff", 1),
    ("zf", 0),
    ("zf", 3),
    ("pf", 2),
    ("ff", 5),
    ("pf", 0),
    ("ff", 4),
    ("pf", 1),
    ("t2",),
    ("finish",),
)


def kernel(
    order,
    conv_in,
    head_in,
    tap_in,
    gain_in,
    offset_in,
    height_in,
    width_in,
    image_in,
    trunk_in,
    cot_in,
    trunk_out,
    heads_out,
    image_out,
    conv_out,
    head_out,
    scale_out,
    rms_out,
    W,
    F3,
    FT,
    FTP,
    NTP,
    N,
    GP,
    DT,
    RN,
    COT,
    COTP,
    ACC,
    D3P,
    GC2,
    GH,
    RL,
    RAW,
    HB,
    SQ,
    LB,
    MR,
    ZB,
    SB,
    SR,
    ag_recv,
    ag_send,
    load_sem,
    rs_recv,
    rs_send,
    pair_recv,
    pair_send,
    in_sem,
    out_sem,
    small_recv,
    small_send,
):
    dpi, fsi = lax.axis_index("dp"), lax.axis_index("fsdp")
    y, c, z, x = dpi // 2, dpi % 2, fsi // 2, fsi % 2

    def dev(yy, cc, zz, xx):
        return (yy * 2 + cc, zz * 2 + xx)

    xn, yn, pn = dev(y, c, z, 1 - x), dev(1 - y, c, z, x), dev(y, 1 - c, z, x)
    up, dn = dev(y, c, jnp.minimum(z + 1, 3), x), dev(y, c, jnp.maximum(z - 1, 0), x)
    sig = [z, z + 1 - 2 * (z % 2), jnp.where(z < 2, 2, 1), jnp.where(z < 2, 3, 0)]
    height, width = height_in[0], width_in[0]

    def when(cond, fn):
        pl.when(cond)(fn)

    def remote(src, dst, send, recv, t):
        return pltpu.make_async_remote_copy(
            src_ref=src, dst_ref=dst, send_sem=send, recv_sem=recv, device_id=t, device_id_type=MESH
        )

    def row(p, yy, cc, s, xx, off=0):
        return pl.multiple_of(BASES[p] + ((2 * yy + cc) * 8 + 2 * s + xx) * UNITS[p] + off, 32)

    def x_first(kind):
        return kind not in (2, 4)

    def shard(r, first, s, last):
        p, off, _, kind = ROUTES[r]
        yy, xx = (last, first) if x_first(kind) else (first, last)
        return row(p, yy, c, s, xx, off)

    def ends(r, routes=ROUTES):
        return (x, y, xn, yn) if x_first(routes[r][3]) else (y, x, yn, xn)

    def place(r, line):
        first, last, _, _ = ends(r)
        return (1 - first if line % 2 else first), (1 - last if line // 2 else last)

    def ag(r, at, si, ri, t, n=1):
        part = W.at[pl.ds(at, ROUTES[r][2] * n)]
        return remote(part, part, ag_send.at[r, si], ag_recv.at[r, ri], t)

    def ag_start(r, at, si, ri, t):
        ag(r, at, si, ri, t).start()

    def ag_wait(r, ri, n=1):
        ag(r, BASES[ROUTES[r][0]], 0, ri, xn, n).wait_recv()

    def pair(r, at, q):
        ag_start(r, at, 36 + q, 20 + q, pn)

    def load(p):
        return pltpu.make_async_copy(
            conv_in.at[p], W.at[pl.ds(row(p, y, c, z, x), CONV_UNIT)], load_sem.at[p]
        )

    def ld(p):
        load(p).wait()

    def along(r, s, at, line, passed=True):
        climbs = (s < z) & (z < 3) if passed else z < 3
        sinks = (s > z) & (z > 0) if passed else z > 0
        when(climbs, lambda: ag_start(r, at, 4 * line + s, 4 * line + s, up))
        when(sinks, lambda: ag_start(r, at, 16 + 4 * line + s, 4 * line + s, dn))

    def fan(r, s, at, line):
        kind = ROUTES[r][3]
        if kind == 0:
            ag_start(r, at, 4 + s, 4 + s, xn)
            ag_start(r, at, 8 + s, 8 + s, yn)
        elif kind < 3:
            ag_start(r, at, 8 + 4 * line + s, 8 + 4 * line + s, ends(r)[3])
        pair(r, at, line)

    def e0(r):
        first, last, fn, ln = ends(r)
        at = shard(r, first, z, last)
        if ROUTES[r][3]:
            ag_start(r, at, 32, 16, fn)
        if ROUTES[r][3] > 2:
            ag_start(r, at, 33, 17, ln)
        along(r, z, at, 0, False)
        fan(r, z, at, 0)

    def f1(r):
        first, last, _, ln = ends(r)
        at = shard(r, 1 - first, z, last)
        ag_wait(r, 16)
        if ROUTES[r][3] > 2:
            ag_start(r, at, 34, 18, ln)
        along(r, z, at, 1, False)
        fan(r, z, at, 1)

    def g1(r, i):
        f, l = place(r, 2 + i)
        at = shard(r, f, z, l)
        ag_wait(r, 17 + i)
        along(r, z, at, 2 + i, False)
        fan(r, z, at, 2 + i)

    def zj(r, j, only=0):
        s = sig[j]
        for line in range(4) if ROUTES[r][3] > 2 else (only,):
            f, l = place(r, line)
            at = shard(r, f, s, l)
            ag_wait(r, 4 * line + s)
            along(r, s, at, line)
            fan(r, s, at, line)

    def lj(r, j):
        first, last, _, _ = ends(r)
        s = sig[j]
        for line in range(2):
            ag_wait(r, 8 + 4 * line + s)
            pair(r, shard(r, place(r, line)[0], s, 1 - last), 2 + line)

    def xd(r, j):
        s = sig[j]
        at = shard(r, 1 - x, s, y)
        ag_wait(r, 4 + s)
        when(s % 2 == 0, lambda: ag_start(r, at, 24 + s, 16 + s, yn))
        pair(r, at, 1)

    def yd(r, j):
        s = sig[j]
        at = shard(r, x, s, 1 - y)
        ag_wait(r, 8 + s)
        when(s % 2 == 1, lambda: ag_start(r, at, 20 + s, 12 + s, xn))
        pair(r, at, 2)

    def yf(r, k):
        s = jnp.where(z < 2, 2 * k, 2 - 2 * k)
        ag_wait(r, 16 + s)
        pair(r, shard(r, 1 - x, s, 1 - y), 3)

    def xf(r, k):
        s = jnp.where(z < 2, 1 + 2 * k, 3 - 2 * k)
        ag_wait(r, 12 + s)
        pair(r, shard(r, 1 - x, s, 1 - y), 3)

    def pw(r):
        for q in range(4):
            ag_wait(r, 20 + q, 4)

    def ag_end(r):
        def done(si, n=1):
            ag(r, BASES[ROUTES[r][0]], si, 0, xn, n).wait_send()

        kind = ROUTES[r][3]
        for s in range(4):
            for line in range((1, 2, 2, 4, 4)[kind]):
                when((z < 3) & (s <= z), lambda: done(4 * line + s))
                when((z > 0) & (s >= z), lambda: done(16 + 4 * line + s))
            if kind == 0:
                done(4 + s)
                done(8 + s)
                done(20 + s if s % 2 else 24 + s)
            elif kind < 3:
                done(8 + s)
                done(12 + s)
            done(36 + s, 4)
        if kind:
            done(32)
        if kind > 2:
            done(33)
            done(34)

    def grads(p):
        if p == 2:
            return GC2, 0
        if p < 2:
            return W, BASES[2] + (1 - p) * 16 * CONV_UNIT
        return GH, (p - 3) * 16 * HEAD_UNIT

    def grow(r, first, s, last):
        p, off, _, kind = BACK[r]
        yy, xx = (last, first) if x_first(kind) else (first, last)
        return pl.multiple_of(grads(p)[1] + (yy * 8 + 2 * s + xx) * UNITS[p] + off, 32)

    def slot(r, k):
        return pl.multiple_of(LAND[r] + k * BACK[r][2], 32)

    def rs(r, at, k, si, ri, t, n=1):
        m = BACK[r][2] * n
        return remote(
            grads(BACK[r][0])[0].at[pl.ds(at, m)],
            RL.at[pl.ds(slot(r, k), m)],
            rs_send.at[r, si],
            rs_recv.at[r, ri],
            t,
        )

    def rs_start(r, at, k, i, t):
        rs(r, at, k, i, i, t).start()

    def rs_wait(r, ri, n=1):
        rs(r, grads(BACK[r][0])[1], 0, 0, ri, xn, n).wait_recv()

    def add(r, at, *ks):
        ref, rows = grads(BACK[r][0])[0], pl.ds(at, BACK[r][2])
        total = ref[rows, :].astype(F32)
        for k in ks:
            total = total + RL[pl.ds(slot(r, k), BACK[r][2]), :].astype(F32)
        ref[rows, :] = total.astype(BF)

    def s1(r):
        if BACK[r][3] == 0:
            for s in (0, 2):
                rs_start(r, grow(r, 1 - x, s, 1 - y), s // 2, 0, yn)
            for s in (1, 3):
                rs_start(r, grow(r, 1 - x, s, 1 - y), 2 + s // 2, 1, xn)
            for s in (1, 3):
                rs_start(r, grow(r, 1 - x, s, y), 4 + s, 2, xn)
            for s in (0, 2):
                rs_start(r, grow(r, x, s, 1 - y), 8 + s, 4, yn)
            return
        if BACK[r][3] > 2:
            far(r)
            return
        _, last, _, ln = ends(r, BACK)
        for i, group in enumerate(((0, 3), (1, 2))):
            for s in group:
                for f in range(2):
                    rs_start(r, grow(r, f, s, 1 - last), 2 * s + f, i, ln)

    def s2a(r):
        rs_wait(r, 0, 2)
        for s in (0, 2):
            at = grow(r, 1 - x, s, y)
            add(r, at, s // 2)
            rs_start(r, at, 4 + s, 3, xn)

    def s2b(r):
        rs_wait(r, 1, 2)
        for s in (1, 3):
            at = grow(r, x, s, 1 - y)
            add(r, at, 2 + s // 2)
            rs_start(r, at, 8 + s, 5, yn)

    def s3a(r):
        rs_wait(r, 2, 2)
        rs_wait(r, 4, 2)
        for s in range(4):
            add(r, grow(r, x, s, y), 4 + s if s % 2 else 8 + s)

    def line_of(r):
        kind, last = BACK[r][3], ends(r, BACK)[1]
        if kind == 0:
            return ((x, y),), 12, 1
        if kind < 3:
            return ((0, last), (1, last)), 8, 2
        return ((0, 0), (1, 0), (0, 1), (1, 1)), 0, 4

    def rs_up(r, t):
        places, base, n = line_of(r)
        for i, (f, l) in enumerate(places):
            rs_start(r, grow(r, f, t, l), base + n * t + i, 6 + t, up)

    def rs_down(r, t):
        places, base, n = line_of(r)
        for i, (f, l) in enumerate(places):
            k = jnp.where(t == z - 1, 4, t)
            rs_start(r, grow(r, f, t, l), base + n * k + i, 10 + t, dn)

    def far(r):
        @pl.when(z == 0)
        def _():
            for t in (3, 2, 1):
                rs_up(r, t)

        @pl.when(z == 3)
        def _():
            for t in (0, 1, 2):
                rs_down(r, t)

    def s3b(r):
        rs_wait(r, 3, 2)
        rs_wait(r, 5, 2)
        for s in range(4):
            add(r, grow(r, x, s, y), 8 + s if s % 2 else 4 + s)
        far(r)

    def s2(r, i):
        rs_wait(r, i, 4)
        for s in ((0, 3), (1, 2))[i]:
            for f in range(2):
                add(r, grow(r, f, s, ends(r, BACK)[1]), 2 * s + f)

        @pl.when(z == 0)
        def _():
            for t in ((3,), (2, 1))[i]:
                rs_up(r, t)

        @pl.when(z == 3)
        def _():
            for t in ((0,), (1, 2))[i]:
                rs_down(r, t)

    def zu(r, t):
        @pl.when((z > 0) & (z < t))
        def _():
            places, base, n = line_of(r)
            rs_wait(r, 6 + t, n)
            for i, (f, l) in enumerate(places):
                add(r, grow(r, f, t, l), base + n * t + i)
            rs_up(r, t)

    def zd(r, t):
        @pl.when((z < 3) & (z > t))
        def _():
            places, base, n = line_of(r)
            rs_wait(r, 10 + t, n)
            for i, (f, l) in enumerate(places):
                add(r, grow(r, f, t, l), base + n * t + i)
            rs_down(r, t)

    def zf(r):
        places, base, n = line_of(r)
        first, last, fn, ln = ends(r, BACK)
        when(z > 0, lambda: rs_wait(r, 6 + z, n))
        when(z < 3, lambda: rs_wait(r, 10 + z, n))

        def both(*ks):
            for i, (f, l) in enumerate(places):
                add(r, grow(r, f, z, l), *[base + n * k + i for k in ks])

        when(z == 0, lambda: both(4))
        when(z == 3, lambda: both(3))
        when((z > 0) & (z < 3), lambda: both(z, 4))
        if n == 2:
            rs_start(r, grow(r, 1 - first, z, last), 18, 2, fn)
        if n == 4:
            for f in range(2):
                rs_start(r, grow(r, f, z, 1 - last), 20 + f, 0, ln)

    def gg(r):
        first, last, fn, _ = ends(r, BACK)
        rs_wait(r, 0, 2)
        for f in range(2):
            add(r, grow(r, f, z, last), 20 + f)
        rs_start(r, grow(r, 1 - first, z, last), 22, 2, fn)

    def ff(r):
        first, last, _, _ = ends(r, BACK)
        rs_wait(r, 2)
        add(r, grow(r, first, z, last), 22 if BACK[r][3] > 2 else 18)

    def conv_store(p):
        ref, base = grads(p)
        at = pl.multiple_of(base + (y * 8 + 2 * z + x) * CONV_UNIT, 32)
        return pltpu.make_async_copy(ref.at[pl.ds(at, CONV_UNIT)], conv_out.at[p], out_sem.at[p])

    def diagonal():
        shape = (64, 64)
        return lax.broadcasted_iota(jnp.int32, shape, 0) == lax.broadcasted_iota(jnp.int32, shape, 1)

    def tap_column(layer):
        wide = jnp.broadcast_to(tap_in[layer : layer + 1, :].astype(F32), (64, 64))
        return jnp.sum(jnp.where(diagonal(), wide, 0.0), axis=1, keepdims=True)

    def left_lanes(count):
        return lax.broadcasted_iota(jnp.int32, (count, 128), 1) < 64

    def unfold(v, upper):
        turned = pltpu.roll(v, 64, 1)
        return jnp.concatenate([jnp.where(upper, v, 0.0), jnp.where(upper, turned, 0.0)], axis=0)

    def pf(p):
        if p < 3:
            conv_store(p).start()
            return
        layer = 5 - p
        base = pl.multiple_of(grads(p)[1] + (y * 8 + 2 * z + x) * HEAD_UNIT, 32)
        full = [GH[pl.ds(base + 64 * t, 64), :].astype(F32) for t in range(3)]
        half = unfold(GH[pl.ds(base + 192, 32), :].astype(F32), (left_lanes(32) == (c == 0)))
        tiles = [jnp.where(c == 0, a, b) for a, b in zip(full + [half], [half] + full)]
        total = jnp.zeros((64, 1), F32)
        for t in range(4):
            raw = RAW[layer, 64 * t : 64 * t + 64, :].astype(F32)
            total = total + jnp.sum(tiles[t] * raw, axis=1, keepdims=True)
        SB[0, :, layer : layer + 1] = total
        tap = tap_column(layer)
        tiles = [v * tap for v in tiles]
        rolled = [pltpu.roll(v, 64, 1) for v in tiles]
        left = left_lanes(64)
        for t in range(4):
            later = rolled[t + 1] if t < 3 else rolled[t]
            v = jnp.where(c == 0, tiles[t], jnp.where(left, rolled[t], later))
            if t < 3:
                head_out[layer, :, 128 * t : 128 * t + 128] = v
            else:
                head_out[layer, :, 384:448] = v[:, 0:64]

    def rs_end(r):
        def done(si, n=1):
            rs(r, grads(BACK[r][0])[1], 0, si, 0, xn, n).wait_send()

        n = line_of(r)[2]
        if n == 1:
            for i in range(6):
                done(i, 2)
        elif n == 2:
            done(0, 4)
            done(1, 4)
            done(2)
        else:
            done(0, 2)
            done(2)
        for t in range(4):
            when((z < 3) & (z < t), lambda: done(6 + t, n))
            when((z > 0) & (z > t), lambda: done(10 + t, n))

    def share_ft(layer):
        return remote(FT.at[layer], FTP.at[layer], pair_send.at[layer], pair_recv.at[layer], pn)

    def share_nt(layer):
        i = 3 + layer
        src = GC2.at[pl.ds(0, 6 * 512)]
        return remote(src, NTP.at[layer % 2], pair_send.at[i], pair_recv.at[i], pn)

    def share_cot(k):
        src = COT.at[pl.ds(7 * k + 3 * (1 - c), 4)]
        return remote(src, COTP.at[k], pair_send.at[6 + k], pair_recv.at[6 + k], pn)

    def share_d(layer, k):
        i = 8 + 2 * layer + k
        src = F3.at[:, 2 * k + 1 - c]
        return remote(src, D3P.at[layer % 2, :, k], pair_send.at[i], pair_recv.at[i], pn)

    def blocks(count, fn):
        def step(m, carry):
            fn(m)
            return carry

        lax.fori_loop(0, count, step, 0)

    one_time = jnp.where(dpi >= 0, 1, 2)

    def apart(fn):
        def wrapped(*args):
            def step(m, carry):
                fn(*args)
                return carry

            lax.fori_loop(0, one_time, step, 0)

        return wrapped

    def at48(m, base=0):
        return pl.ds(pl.multiple_of(base + 48 * m, 8 if base == 8 else 16), 48)

    def place48():
        i = lax.broadcasted_iota(jnp.int32, (48, 1), 0)
        second = i >= HIGH
        return jnp.where(second, i - HIGH, i), jnp.where(second, 1, 0)

    def mask_of(m):
        r, second = place48()
        return jnp.where((r < height) & (2 * m + second < width), 1.0, 0.0).astype(F32)

    def image_part(i):
        src = (image_in, trunk_in)[i // 4].at[:, pl.ds(128 * (i % 4), 128)]
        return pltpu.make_async_copy(src, GC2.at[pl.ds(3072 + PIX * i, PIX)], in_sem.at[i])

    def cot_part(t):
        return pltpu.make_async_copy(
            cot_in.at[:, pl.ds(128 * t, 128)], COT.at[t, pl.ds(0, PIX)], in_sem.at[8 + t]
        )

    def expand(first, masked):
        def one(m):
            at = at48(m, 8)
            for k in range(4):
                rows = pl.ds(pl.multiple_of(3072 + PIX * (first + k) + 48 * m, 16), 48)
                v = GC2[rows, :].astype(F32)
                if masked:
                    v = v * mask_of(m)
                    SQ[0:1, 128 * k : 128 * k + 128] += jnp.sum(v * v, axis=0, keepdims=True)
                ACC[at, 128 * k : 128 * k + 128] = v

        blocks(14, one)

    def start():
        for p in range(3):
            load(p).start()
        for i in range(8):
            image_part(i).start()
        for t in range(14):
            cot_part(t).start()
        barrier = pltpu.get_barrier_semaphore()
        for t in (xn, yn, pn):
            pl.semaphore_signal(barrier, inc=1, device_id=t, device_id_type=MESH)
        when(
            z < 3, lambda: pl.semaphore_signal(barrier, inc=1, device_id=up, device_id_type=MESH)
        )
        when(
            z > 0, lambda: pl.semaphore_signal(barrier, inc=1, device_id=dn, device_id_type=MESH)
        )
        pl.semaphore_wait(barrier, jnp.where((z == 0) | (z == 3), 4, 5))

    def prep_heads():
        left = left_lanes(64)
        ACC[0:64, :] = jnp.zeros((64, 512), F32)
        for layer in range(3):
            ACC[0:64, 0:448] = head_in[layer].astype(F32)
            tap = tap_column(layer)
            base = row(5 - layer, y, c, z, x)
            tiles = [ACC[0:64, 128 * t : 128 * t + 128] for t in range(4)]
            rolled = [pltpu.roll(v, 64, 1) for v in tiles]
            moved = [
                jnp.where(left, rolled[t - 1] if t else 0.0, rolled[t]) for t in range(4)
            ]
            for t in range(4):
                v = jnp.where(c == 0, tiles[t], moved[t])
                RAW[layer, 64 * t : 64 * t + 64, :] = v.astype(BF)
            for t in range(3):
                v = jnp.where(c == 0, tiles[t], moved[t + 1])
                W[pl.ds(base + 64 * t, 64), :] = (v * tap).astype(BF)
            v = jnp.where(c == 0, tiles[3], moved[0]) * tap
            W[pl.ds(base + 192, 32), :] = (v[0:32] + pltpu.roll(v[32:64], 64, 1)).astype(BF)

    def prep_in():
        ACC[...] = jnp.zeros_like(ACC)
        SQ[...] = jnp.zeros_like(SQ)
        SB[0] = jnp.zeros((64, 128), F32)
        for b in range(3):
            for k in range(4):
                F3[b, k, 0:32, :] = jnp.zeros((32, 128), BF)
                F3[b, k, 704:832, :] = jnp.zeros((128, 128), BF)
        for i in range(4):
            image_part(i).wait()
        expand(0, True)
        pixels = (height * width).astype(F32) * (1.0 / 512.0)
        SQ[5:6, :] = jnp.full((1, 512), pixels, F32)

    def shifts():
        r, _ = place48()

        def one(m):
            v64 = ACC[pl.ds(pl.multiple_of(48 * m, 8), 64), :]
            for b in range(3):
                v = v64[7 + b : 55 + b, :]
                if b != 1:
                    v = jnp.where(r == (0 if b == 0 else HIGH - 1), 0.0, v)
                v = v.astype(BF)
                for k in range(4):
                    F3[b, k, at48(m, 32), :] = v[:, 128 * k : 128 * k + 128]

        blocks(14, one)

    def ft(layer):
        shifts()

        def one(m):
            v = ACC[pl.ds(pl.multiple_of(8 + 128 * m, 8), 128), :]
            FT[layer, :, pl.ds(pl.multiple_of(128 * m, 128), 128)] = v.T.astype(BF)

        blocks(6, one)
        share_ft(layer).start()

    def prep_cot():
        def clear(t):
            COT[t, PIX:PAD, :] = jnp.zeros((PAD - PIX, 128), BF)

        blocks(14, clear)
        for t in range(14):
            cot_part(t).wait()
        for k in range(2):
            share_cot(k).start()

    def taps(a, transposed):
        first = 8 + HIGH * a if not transposed else 8 + HIGH * (2 - a)
        order = (0, 1, 2) if not transposed else (2, 1, 0)
        return [
            jnp.concatenate([F3[b, k, first : first + PIX, :] for k in range(4)], axis=1)
            for b in order
        ]

    def weights(layer, a, b):
        first = BASES[layer] + 512 * (3 * b + a)
        return jnp.concatenate(
            [W[first + 4608 * k : first + 4608 * k + 512, :] for k in range(4)], axis=1
        )

    @apart
    def conv(layer, a):
        v = jnp.dot(
            jnp.concatenate(taps(a, False), axis=1),
            jnp.concatenate([weights(layer, a, b) for b in range(3)], axis=0),
            preferred_element_type=F32,
        )
        if a == 0:
            ACC[8 : 8 + PIX, :] = v
        else:
            ACC[8 : 8 + PIX, :] += v

    def act(layer):
        gain, offset = gain_in[layer : layer + 1, :], offset_in[layer : layer + 1, :]
        k = 0.7978845608028654

        def one(m):
            rows, at = at48(m, 8), at48(m)
            u = ACC[rows, :] * gain + offset
            mask = mask_of(m)
            u2 = u * u
            t = jnp.tanh(k * u * (1.0 + 0.044715 * u2))
            half = 0.5 * (1.0 + t) * mask
            f = u * half
            slope = half + (0.5 * k) * mask * u * (1.0 - t * t) * (1.0 + 0.134145 * u2)
            squares = f * f
            rn = lax.rsqrt(jnp.mean(squares, axis=-1, keepdims=True) + 1e-5)
            GP[layer, at, :] = (slope * gain).astype(BF)
            N[layer, at, :] = (f * rn).astype(BF)
            RN[at, layer : layer + 1] = rn
            SQ[layer + 1 : layer + 2, :] += jnp.sum(squares, axis=0, keepdims=True)
            if layer < 2:
                ACC[rows, :] = f
            else:
                v = f.astype(BF)
                for b in range(4):
                    F3[1, b, at48(m, 32), :] = v[:, 128 * b : 128 * b + 128]

        blocks(14, one)
        if layer == 2:
            for b in range(4):
                trunk_store(b).start()

    def trunk_store(b):
        return pltpu.make_async_copy(
            F3.at[1, b, pl.ds(32, PIX)], trunk_out.at[:, pl.ds(128 * b, 128)], out_sem.at[6 + b]
        )

    def nt(layer):
        if layer > 0:
            share_nt(layer - 1).wait_send()

        turn(layer)
        share_nt(layer).start()

    @apart
    def turn(layer):
        for m in range(6):
            v = N[layer, 128 * m : min(128 * m + 128, PIX), :].astype(F32)
            if m == 5:
                v = jnp.concatenate([v, jnp.zeros((PAD - PIX, 512), F32)], axis=0)
            GC2[512 * m : 512 * m + 512, :] = v.T.astype(BF)

    def head_grads(layer, k):
        if k == 0:
            share_nt(layer).wait_recv()
        if layer == 0:
            share_cot(k).wait_recv()
        head_grads_of(layer, k)

    @apart
    def head_grads_of(layer, k):
        mine = [GC2[512 * m : 512 * m + 512, :] for m in range(6)]
        theirs = [NTP[layer % 2, 512 * m : 512 * m + 512, :] for m in range(6)]
        own = jnp.concatenate([COT[7 * k + 3 * c + i] for i in range(4)], axis=1)
        other = jnp.concatenate([COTP[k, i] for i in range(4)], axis=1)
        v = jnp.dot(
            jnp.concatenate(mine + theirs, axis=1),
            jnp.concatenate([own, other], axis=0),
            preferred_element_type=F32,
        )
        base = grads(5 - layer)[1] + k * 8 * HEAD_UNIT
        tiles = [v[:, 128 * t : 128 * t + 128] for t in range(4)]
        valid = left_lanes(32) == (c == 0)
        for f in range(8):
            rows = slice(64 * f, 64 * f + 64)
            first = base + f * HEAD_UNIT
            for t in range(3):
                part = jnp.where(c == 0, tiles[t][rows], tiles[t + 1][rows])
                GH[first + 64 * t : first + 64 * t + 64, :] = part.astype(BF)
            half = jnp.where(c == 0, tiles[3][rows], tiles[0][rows])
            lower = pltpu.roll(jnp.where(valid, half[32:64], 0.0), 64, 1)
            GH[first + 192 : first + 224, :] = jnp.where(valid, half[0:32], lower).astype(BF)

    def unpack(layer):
        left = left_lanes(32)

        def one(f):
            for k in range(2):
                base = BASES[5 - layer] + 16 * k * HEAD_UNIT + 192
                low, high = [
                    W[pl.ds(pl.multiple_of(base + (8 * i + f) * HEAD_UNIT, 32), 32), :].astype(F32)
                    for i in range(2)
                ]
                HB[layer, k, f, 0:32, :] = jnp.where(left, low, high).astype(BF)
                v = jnp.where(left, pltpu.roll(low, 64, 1), pltpu.roll(high, 64, 1))
                HB[layer, k, f, 32:64, :] = v.astype(BF)

        blocks(8, one)

    def head_pair(layer, k):
        def tile(f, t):
            if t == 3:
                return HB[layer, k, f]
            i, t = (0, t) if t < 3 else (1, t - 4)
            first = BASES[5 - layer] + (16 * k + 8 * i + f) * HEAD_UNIT + 64 * t
            return W[first : first + 64, :]

        return jnp.concatenate(
            [jnp.concatenate([tile(f, t) for f in range(8)], axis=0) for t in range(7)], axis=1
        )

    def at224(m):
        return pl.ds(pl.multiple_of(224 * m, 32), 224)

    def dtap(layer):
        def one(m):
            at = at224(m)
            h = jnp.zeros((224, 512), F32)
            for k in range(2):
                left = jnp.concatenate([COT[7 * k + i, at, :] for i in range(7)], axis=1)
                h = h + lax.dot_general(
                    left, head_pair(layer, k), (((1,), (1,)), ((), ())), preferred_element_type=F32
                )
            n = N[layer, at, :].astype(F32)
            mean = jnp.mean(h * n, axis=-1, keepdims=True)
            DT[layer, at, :] = ((h - n * mean) * RN[at, layer : layer + 1]).astype(BF)

        blocks(3, one)

    def joined(k):
        if k == 0:
            for i in range(2):
                share_cot(i).wait_send()

        def one(m):
            at = at224(m)
            left = jnp.concatenate([N[i, at, :] for i in range(3)], axis=1)
            v = jnp.dot(
                left,
                jnp.concatenate([head_pair(i, k) for i in range(3)], axis=0),
                preferred_element_type=F32,
            )
            total = jnp.zeros((1, 128), F32)
            for i in range(7):
                tile = v[:, 128 * i : 128 * i + 128]
                total = total + jnp.sum(tile * tile, axis=0, keepdims=True)
                COT[7 * k + i, at, :] = tile.astype(BF)
            SQ[4:5, 0:128] += total

        blocks(3, one)
        for i in range(7):
            heads_store(7 * k + i).start()

    def heads_store(t):
        return pltpu.make_async_copy(
            COT.at[t, pl.ds(0, PIX)], heads_out.at[:, pl.ds(128 * t, 128)], in_sem.at[8 + t]
        )

    def trunk_cot():
        for i in range(4, 8):
            image_part(i).wait()
        expand(4, False)

    def dlinear(layer):
        def one(m):
            rows, at = at48(m, 8), at48(m)
            g = ACC[rows, :] + DT[layer, at, :].astype(F32)
            ACC[rows, :] = g * GP[layer, at, :].astype(F32)

        blocks(14, one)
        if layer == 2:
            for b in range(4):
                trunk_store(b).wait()
        else:
            for k in range(2):
                share_d(layer + 1, k).wait_send()
        shifts()
        for k in range(2):
            share_d(layer, k).start()

    @apart
    def conv_back(layer, a):
        v = lax.dot_general(
            jnp.concatenate(taps(a, True), axis=1),
            jnp.concatenate([weights(layer, a, b) for b in range(3)], axis=1),
            (((1,), (1,)), ((), ())),
            preferred_element_type=F32,
        )
        if a == 0:
            ACC[8 : 8 + PIX, :] = v
        else:
            ACC[8 : 8 + PIX, :] += v

    def conv_grads(layer, a):
        if a == 0:
            share_ft(layer).wait_recv()
            for k in range(2):
                share_d(layer, k).wait_recv()
            if layer == 2:
                share_nt(2).wait_send()
            if layer == 1:
                for r, route in enumerate(ROUTES):
                    if route[0] == 2:
                        ag_end(r)
        conv_grads_of(layer, a)

    @apart
    def conv_grads_of(layer, a):
        first = 8 + HIGH * (2 - a)
        rows = slice(first, first + PAD)
        own = [F3[2 - b, 2 * k + c, rows, :] for b in range(3) for k in range(2)]
        other = [D3P[layer % 2, 2 - b, k, rows, :] for b in range(3) for k in range(2)]
        v = jnp.dot(
            jnp.concatenate([FT[layer], FTP[layer]], axis=1),
            jnp.concatenate(
                [jnp.concatenate(own, axis=1), jnp.concatenate(other, axis=1)], axis=0
            ),
            preferred_element_type=F32,
        ).astype(BF)
        ref, base = grads(layer)
        for b in range(3):
            for k in range(2):
                r = base + 4608 * k + 512 * (3 * b + a)
                at = 256 * b + 128 * k
                ref[r : r + 512, :] = v[:, at : at + 128]

    def image_store():
        return pltpu.make_async_copy(DT.at[2], image_out, out_sem.at[10])

    def image_grad():
        def one(m):
            DT[2, at48(m), :] = (ACC[at48(m, 8), :] * mask_of(m)).astype(BF)

        blocks(14, one)
        image_store().start()

    def small(i):
        return remote(LB.at[i], MR.at[i], small_send.at[i], small_recv.at[i], (pn, xn, yn)[i])

    def line(s, i, t):
        return remote(ZB.at[s], ZB.at[s], small_send.at[i], small_recv.at[5 + s], t)

    def m0():
        v = SQ[:, 0:128]
        for i in range(1, 4):
            v = v + SQ[:, 128 * i : 128 * i + 128]
        LB[0] = v
        small(0).start()

    def m1(i):
        small(i).wait_recv()
        v = LB[i] + MR[i]
        if i < 2:
            LB[i + 1] = v
            small(i + 1).start()
            return
        ZB[z] = v
        when(z < 3, lambda: line(z, 5 + z, up).start())
        when(z > 0, lambda: line(z, 9 + z, dn).start())

    def m2(j):
        s = sig[j]
        line(s, 5, up).wait_recv()
        when((s < z) & (z < 3), lambda: line(s, 5 + s, up).start())
        when((s > z) & (z > 0), lambda: line(s, 9 + s, dn).start())

    def m3():
        total = ZB[0] + ZB[1] + ZB[2] + ZB[3]
        v = jnp.sum(total, axis=1, keepdims=True)
        which = lax.broadcasted_iota(jnp.int32, (8, 1), 0)
        wide = jnp.where(which == 4, 1792.0, 512.0).astype(F32)
        rms_out[...] = jnp.broadcast_to(jnp.sqrt(v / (v[5:6] * wide)), (8, 128))

    def scale_sum(i):
        return remote(SB.at[i], SR.at[i], small_send.at[3 + i], small_recv.at[3 + i], (pn, yn)[i])

    def t0():
        scale_sum(0).start()

    def t1():
        scale_sum(0).wait_recv()
        SB[1] = SB[0] + SR[0]
        scale_sum(1).start()

    def t2():
        scale_sum(1).wait_recv()
        total = SB[1] + SR[1]
        for layer in range(3):
            v = jnp.where(diagonal(), total[:, layer : layer + 1], 0.0)
            scale_out[layer : layer + 1, :] = jnp.sum(v, axis=0, keepdims=True)

    def finish():
        for r, route in enumerate(ROUTES):
            if route[0] != 2:
                ag_end(r)
        for r in range(len(BACK)):
            rs_end(r)
        for i in range(3):
            share_ft(i).wait_send()
            small(i).wait_send()
            conv_store(i).wait()
        for k in range(2):
            share_d(0, k).wait_send()
            scale_sum(k).wait_send()
        for s in range(4):
            when((z < 3) & (s <= z), lambda s=s: line(s, 5 + s, up).wait_send())
            when((z > 0) & (s >= z), lambda s=s: line(s, 9 + s, dn).wait_send())
        for t in range(14):
            heads_store(t).wait()
        image_store().wait()

    fns = dict(
        start=start, ld=ld, e0=e0, f1=f1, g1=g1, gg=gg, zj=zj, lj=lj, xd=xd, yd=yd, xf=xf, yf=yf, pw=pw,
        s1=s1, s2a=s2a, s2b=s2b, s3a=s3a, s3b=s3b, s2=s2, zu=zu, zd=zd, zf=zf, ff=ff, pf=pf,
        prep_heads=prep_heads, prep_in=prep_in, prep_cot=prep_cot, ft=ft, conv=conv, act=act, nt=nt,
        head_grads=head_grads, unpack=unpack, dtap=dtap, joined=joined, trunk_cot=trunk_cot,
        dlinear=dlinear, conv_back=conv_back, conv_grads=conv_grads, image_grad=image_grad,
        m0=m0, m1=m1, m2=m2, m3=m3, t0=t0, t1=t1, t2=t2, finish=finish,
    )
    for name, *args in order:
        fns[name](*args)


def patches(feature):
    height = feature.shape[1]
    breadth = feature.shape[2]
    padded = jnp.pad(feature, ((0, 0), (1, 1), (1, 1), (0, 0)))
    pieces = [
        padded[:, down_step : down_step + height, side_step : side_step + breadth, :]
        for down_step in range(3)
        for side_step in range(3)
    ]
    return jnp.concatenate(pieces, axis=-1)


def unpatch(stacked, channels):
    images, height, breadth, _ = stacked.shape
    padded = jnp.zeros((images, height + 2, breadth + 2, channels), jnp.float32)
    for down_step in range(3):
        for side_step in range(3):
            tap_index = 3 * down_step + side_step
            padded = padded.at[
                :, down_step : down_step + height, side_step : side_step + breadth, :
            ].add(stacked[..., tap_index * channels : (tap_index + 1) * channels])
    return padded[:, 1:-1, 1:-1, :]


def activate(linear, gain_vec, offsets, valid_mask):
    return valid_mask * jax.nn.gelu(linear * gain_vec + offsets)


def tap_piece(feature, scale_vec):
    return (
        feature * lax.rsqrt(jnp.mean(feature * feature, axis=-1, keepdims=True) + 1e-05) * scale_vec
    )


def general(
    inputs,
    heights,
    widths,
    conv_weights,
    affine_scale,
    affine_shift,
    tap_scales,
    head_weights,
    trunk_cot,
    heads_cot,
):
    images, height, breadth, channels = inputs.shape
    layer_count = conv_weights.shape[0]
    row_ids = jnp.arange(height, dtype=jnp.int32)
    col_ids = jnp.arange(breadth, dtype=jnp.int32)
    valid = (row_ids[None, :, None] < heights[:, None, None]) & (
        col_ids[None, None, :] < widths[:, None, None]
    )
    valid_mask = jnp.where(valid, 1.0, 0.0).astype(jnp.float32)[..., None]
    conv_cols, head_cols = (
        lax.all_gather(conv_weights, "dp", axis=2, tiled=True),
        lax.all_gather(head_weights, "dp", axis=2, tiled=True),
    )
    conv_full, head_full, scale_full = (
        lax.all_gather(conv_cols, "fsdp", axis=1, tiled=True),
        lax.all_gather(head_cols, "fsdp", axis=1, tiled=True),
        lax.all_gather(tap_scales, "fsdp", axis=1, tiled=True),
    )
    outputs_wide = head_full.shape[2]
    feature = inputs.astype(jnp.float32) * valid_mask
    squares = [jnp.sum(feature * feature)]
    entering = inputs * valid_mask.astype(jnp.bfloat16)
    kept_in, kept_linear, kept_feature, kept_tap = ([], [], [], [])
    summed = jnp.zeros((images, height, breadth, outputs_wide), jnp.float32)
    for layer_index in range(layer_count):
        stacked = patches(entering)
        linear = jnp.einsum(
            "ghwk,kc->ghwc", stacked, conv_full[layer_index], preferred_element_type=jnp.float32
        )
        feature = activate(linear, affine_scale[layer_index], affine_shift[layer_index], valid_mask)
        tapped = tap_piece(feature, scale_full[layer_index].astype(jnp.float32)).astype(
            jnp.bfloat16
        )
        summed = summed + jnp.einsum(
            "ghwc,co->ghwo", tapped, head_full[layer_index], preferred_element_type=jnp.float32
        )
        kept_in.append(entering)
        kept_linear.append(linear)
        kept_feature.append(feature)
        kept_tap.append(tapped)
        squares.append(jnp.sum(feature * feature))
        entering = feature.astype(jnp.bfloat16)
    squares.append(jnp.sum(summed * summed))
    square_total, pixels = lax.psum((jnp.stack(squares), jnp.sum(valid_mask)), ("dp", "fsdp"))
    divisors = jnp.array([channels] * (layer_count + 1) + [outputs_wide], jnp.float32)
    rms = jnp.sqrt(square_total / (pixels * divisors))
    conv_back, head_back, scale_back = conv_full, head_full, scale_full
    grad_conv = [None] * layer_count
    grad_scale = [None] * layer_count
    grad_head = [None] * layer_count
    grad_feature = trunk_cot.astype(jnp.float32)
    for layer_index in reversed(range(layer_count)):
        grad_head[layer_index] = jnp.einsum(
            "ghwc,ghwo->co", kept_tap[layer_index], heads_cot, preferred_element_type=jnp.float32
        )
        grad_tapped = jnp.einsum(
            "ghwo,co->ghwc", heads_cot, head_back[layer_index], preferred_element_type=jnp.float32
        )
        _, pullback = jax.vjp(
            tap_piece, kept_feature[layer_index], scale_back[layer_index].astype(jnp.float32)
        )
        feature_part, scale_part = pullback(grad_tapped)
        grad_scale[layer_index] = scale_part
        grad_feature = grad_feature + feature_part
        local_act = partial(
            activate,
            gain_vec=affine_scale[layer_index],
            offsets=affine_shift[layer_index],
            valid_mask=valid_mask,
        )
        _, pullback = jax.vjp(local_act, kept_linear[layer_index])
        (grad_linear,) = pullback(grad_feature)
        low_linear = grad_linear.astype(jnp.bfloat16)
        grad_conv[layer_index] = jnp.einsum(
            "ghwk,ghwc->kc",
            patches(kept_in[layer_index]),
            low_linear,
            preferred_element_type=jnp.float32,
        )
        spread = jnp.einsum(
            "ghwc,kc->ghwk", low_linear, conv_back[layer_index], preferred_element_type=jnp.float32
        )
        grad_feature = unpatch(spread, channels)
    input_grad = (grad_feature * valid_mask).astype(jnp.bfloat16)
    stacked_conv = jnp.stack(grad_conv)
    stacked_head = jnp.stack(grad_head)
    stacked_scale = jnp.stack(grad_scale)
    dp_count = lax.axis_size("dp")
    part_conv, part_head, part_scale = (
        lax.psum_scatter(
            stacked_conv.astype(jnp.bfloat16), "fsdp", scatter_dimension=1, tiled=True
        ).astype(jnp.float32),
        lax.psum_scatter(
            stacked_head.astype(jnp.bfloat16), "fsdp", scatter_dimension=1, tiled=True
        ).astype(jnp.float32),
        lax.psum_scatter(
            stacked_scale.astype(jnp.bfloat16), "fsdp", scatter_dimension=1, tiled=True
        ).astype(jnp.float32),
    )
    spread_scale = jnp.broadcast_to(part_scale[:, :, None], part_scale.shape + (dp_count,))
    conv_grad, head_grad, scale_cols = (
        lax.psum_scatter(
            part_conv.astype(jnp.bfloat16), "dp", scatter_dimension=2, tiled=True
        ).astype(jnp.float32),
        lax.psum_scatter(
            part_head.astype(jnp.bfloat16), "dp", scatter_dimension=2, tiled=True
        ).astype(jnp.float32),
        lax.psum_scatter(
            spread_scale.astype(jnp.bfloat16), "dp", scatter_dimension=2, tiled=True
        ).astype(jnp.float32),
    )
    scale_grad = scale_cols[:, :, 0]
    trunk_out = kept_feature[-1].astype(jnp.bfloat16)
    heads_out = summed.astype(jnp.bfloat16)
    return (trunk_out, heads_out, input_grad, conv_grad, scale_grad, head_grad, rms)


def settle(trunk, heads, image, conv, head, scale, rms, *rest):
    trunk_to, heads_to, image_to, conv_to, head_to, scale_to, rms_to = rest[:7]
    at_trunk, at_heads, at_image, at_conv, at_head, wide, come, go = rest[7:]
    moves = [(conv, at_conv, conv_to)]
    for i in range(3):
        rows = pl.ds(224 * i, 224)
        moves.append((heads.at[rows], at_heads.at[rows], heads_to.at[rows]))
    moves += [(trunk, at_trunk, trunk_to), (image, at_image, image_to), (head, at_head, head_to)]
    fetches = [pltpu.make_async_copy(a, b, come.at[i]) for i, (a, b, _) in enumerate(moves)]
    stores = [pltpu.make_async_copy(b, c, go.at[i]) for i, (_, b, c) in enumerate(moves)]
    stores[0] = pltpu.make_async_copy(wide, conv_to, go.at[0])
    for fetch in fetches:
        fetch.start()
    scale_to[...] = scale[...]
    for i in range(5):
        rms_to[i] = rms[i, 0]
    for i, (fetch, store) in enumerate(zip(fetches, stores)):
        fetch.wait()
        if i == 0:
            wide[...] = at_conv[...].astype(F32)
        store.start()
    for store in stores:
        store.wait()


def settled(results):
    hbm = pl.BlockSpec(memory_space=pl.ANY)
    vmem = pl.BlockSpec(memory_space=pltpu.VMEM)
    smem = pl.BlockSpec(memory_space=pltpu.SMEM)
    shapes = [jax.ShapeDtypeStruct(v.shape, v.dtype) for v in results[:6]]
    shapes[3] = jax.ShapeDtypeStruct(results[3].shape, F32)
    shapes.append(jax.ShapeDtypeStruct((5,), F32))
    return pl.pallas_call(
        settle,
        name="settle",
        out_shape=shapes,
        in_specs=[hbm, hbm, hbm, hbm, hbm, vmem, smem],
        out_specs=[hbm, hbm, hbm, hbm, hbm, vmem, smem],
        scratch_shapes=[pltpu.VMEM(v.shape, v.dtype) for v in results[:5]]
        + [
            pltpu.VMEM(results[3].shape, F32),
            pltpu.SemaphoreType.DMA((7,)),
            pltpu.SemaphoreType.DMA((7,)),
        ],
        compiler_params=pltpu.CompilerParams(vmem_limit_bytes=63 * 2**20),
    )(*results)


def fused(
    inputs,
    heights,
    widths,
    conv_weights,
    affine_scale,
    affine_shift,
    tap_scales,
    head_weights,
    trunk_cot,
    heads_cot,
):
    hbm = pl.BlockSpec(memory_space=pl.ANY)
    vmem = pl.BlockSpec(memory_space=pltpu.VMEM)
    smem = pl.BlockSpec(memory_space=pltpu.SMEM)
    dma = pltpu.SemaphoreType.DMA
    ahead, back = len(ROUTES), len(BACK)

    def flat(v):
        return v[0].transpose(1, 0, 2).reshape(PIX, v.shape[3])

    results = pl.pallas_call(
        partial(kernel, ORDER),
        name="conv_block",
        out_shape=(
            jax.ShapeDtypeStruct((PIX, 512), BF),
            jax.ShapeDtypeStruct((PIX, 1792), BF),
            jax.ShapeDtypeStruct((PIX, 512), BF),
            jax.ShapeDtypeStruct((3, 576, 128), BF),
            jax.ShapeDtypeStruct((3, 64, 448), F32),
            jax.ShapeDtypeStruct((3, 64), F32),
            jax.ShapeDtypeStruct((8, 128), F32),
        ),
        in_specs=[hbm, vmem, vmem, vmem, vmem, smem, smem, hbm, hbm, hbm],
        out_specs=(hbm, hbm, hbm, hbm, vmem, vmem, vmem),
        scratch_shapes=[
            pltpu.VMEM((ROWS, 128), BF),
            pltpu.VMEM((3, 4, 832, 128), BF),
            pltpu.VMEM((3, 512, PAD), BF),
            pltpu.VMEM((3, 512, PAD), BF),
            pltpu.VMEM((2, 6 * 512, 128), BF),
            pltpu.VMEM((3, PIX, 512), BF),
            pltpu.VMEM((3, PIX, 512), BF),
            pltpu.VMEM((3, PIX, 512), BF),
            pltpu.VMEM((PIX, 128), F32),
            pltpu.VMEM((14, PAD, 128), BF),
            pltpu.VMEM((2, 4, PAD, 128), BF),
            pltpu.VMEM((16 + PAD, 512), F32),
            pltpu.VMEM((2, 3, 2, 832, 128), BF),
            pltpu.VMEM((16 * CONV_UNIT, 128), BF),
            pltpu.VMEM((3 * 16 * HEAD_UNIT, 128), BF),
            pltpu.VMEM((LAND[-1], 128), BF),
            pltpu.VMEM((3, 256, 128), BF),
            pltpu.VMEM((3, 2, 8, 64, 128), BF),
            pltpu.VMEM((8, 512), F32),
            pltpu.VMEM((3, 8, 128), F32),
            pltpu.VMEM((3, 8, 128), F32),
            pltpu.VMEM((4, 8, 128), F32),
            pltpu.VMEM((2, 64, 128), F32),
            pltpu.VMEM((2, 64, 128), F32),
            dma((ahead, 24)),
            dma((ahead, 40)),
            dma((3,)),
            dma((back, 14)),
            dma((back, 14)),
            dma((14,)),
            dma((14,)),
            dma((22,)),
            dma((11,)),
            dma((9,)),
            dma((13,)),
        ],
        compiler_params=pltpu.CompilerParams(
            collective_id=0, has_side_effects=True, vmem_limit_bytes=64 * 2**20
        ),
        cost_estimate=pl.CostEstimate(
            flops=45_000_000_000, bytes_accessed=16_000_000, transcendentals=1_200_000
        ),
    )(
        conv_weights,
        head_weights,
        tap_scales,
        affine_scale,
        affine_shift,
        heights,
        widths,
        flat(inputs),
        flat(trunk_cot),
        flat(heads_cot),
    )
    trunk, heads, image, conv_grad, head_grad, scale_grad, rms = settled(results)

    def image_of(v):
        return v.reshape(28, HIGH, v.shape[1]).transpose(1, 0, 2)[None]

    return (
        image_of(trunk),
        image_of(heads),
        image_of(image),
        conv_grad,
        scale_grad,
        head_grad,
        rms,
    )


def solution(mesh):
    in_specs = (
        P(("dp", "fsdp"), None, None, None),
        P(("dp", "fsdp")),
        P(("dp", "fsdp")),
        P(None, "fsdp", "dp"),
        P(),
        P(),
        P(None, "fsdp"),
        P(None, "fsdp", "dp"),
        P(("dp", "fsdp"), None, None, None),
        P(("dp", "fsdp"), None, None, None),
    )
    out_specs = (
        P(("dp", "fsdp"), None, None, None),
        P(("dp", "fsdp"), None, None, None),
        P(("dp", "fsdp"), None, None, None),
        P(None, "fsdp", "dp"),
        P(None, "fsdp"),
        P(None, "fsdp", "dp"),
        P(),
    )
    body = fused if dict(mesh.shape) == {"dp": 4, "fsdp": 8} else general
    return jax.shard_map(body, mesh=mesh, in_specs=in_specs, out_specs=out_specs, check_vma=False)
```

```python
from functools import partial

import jax
import jax.numpy as jnp
from jax import lax
from jax.experimental import pallas as pl
from jax.experimental.pallas import tpu as pltpu
from jax.sharding import PartitionSpec as P

MESH = pl.DeviceIdType.MESH
F32, BF = jnp.float32, jnp.bfloat16

CONV_UNIT, HEAD_UNIT = 576, 224
UNITS = (CONV_UNIT,) * 3 + (HEAD_UNIT,) * 3
BASES = tuple(32 * sum(UNITS[:p]) for p in range(6))
ROWS = 32 * sum(UNITS)
ROUTES = (
    (0, 0, 256, 0),
    (0, 256, 160, 1),
    (0, 416, 160, 2),
    (1, 0, 256, 0),
    (1, 256, 160, 1),
    (1, 416, 160, 2),
    (2, 0, 192, 0),
    (2, 192, 192, 1),
    (2, 384, 192, 2),
    (3, 0, 224, 0),
    (4, 0, 224, 1),
    (5, 0, 224, 2),
)
BACK = (
    (0, 0, 256, 0),
    (0, 256, 160, 1),
    (0, 416, 160, 2),
    (1, 0, 192, 0),
    (1, 192, 192, 1),
    (1, 384, 192, 2),
    (2, 0, 192, 0),
    (2, 192, 192, 1),
    (2, 384, 192, 2),
    (3, 0, 224, 0),
    (4, 0, 224, 1),
    (5, 0, 224, 2),
)
SLOTS = (17, 19, 19, 23, 23)
PAIR = (16, 17, 17, 19, 19)
LAND = tuple(sum(SLOTS[k] * m for _, _, m, k in BACK[:r]) for r in range(len(BACK) + 1))
HIGH, PIX, PAD = 24, 672, 768
ORDER = (
    ("start",),
    ("ld", 0),
    ("e0", 0),
    ("e0", 1),
    ("prep_heads",),
    ("e0", 2),
    ("ld", 1),
    ("e0", 5),
    ("e0", 4),
    ("prep_in",),
    ("zj", 1, 1, 0),
    ("f1", 1),
    ("zj", 0, 1),
    ("f1", 2),
    ("e0", 3),
    ("zj", 1, 1, 1),
    ("zj", 2, 1, 0),
    ("xd", 0, 0),
    ("zj", 2, 2, 0),
    ("f1", 4),
    ("zj", 0, 2),
    ("zj", 0, 3),
    ("lj", 2, 0),
    ("zj", 2, 1, 1),
    ("yd", 0, 0),
    ("lj", 1, 0),
    ("xd", 0, 1),
    ("yd", 0, 1),
    ("zj", 3, 1),
    ("zj", 2, 2, 1),
    ("ld", 2),
    ("zj", 1, 2, 0),
    ("zj", 1, 2, 1),
    ("zj", 2, 3, 0),
    ("xd", 0, 2),
    ("ft", 0),
    ("yd", 0, 2),
    ("zj", 1, 3, 1),
    ("zj", 2, 3, 1),
    ("f1", 5),
    ("yd", 0, 3),
    ("zj", 1, 3, 0),
    ("prep_cot",),
    ("lj", 2, 1),
    ("xd", 0, 3),
    ("zj", 3, 2),
    ("lj", 1, 1),
    ("yd", 3, 0),
    ("e0", 8),
    ("lj", 2, 2),
    ("zj", 5, 1, 0),
    ("zj", 4, 1, 1),
    ("xd", 3, 0),
    ("e0", 7),
    ("zj", 4, 1, 0),
    ("e0", 6),
    ("zj", 4, 2, 1),
    ("lj", 1, 2),
    ("lj", 2, 3),
    ("lj", 1, 3),
    ("xf", 0, 0),
    ("xf", 0, 1),
    ("yf", 0, 0),
    ("zj", 3, 3),
    ("yd", 3, 1),
    ("yf", 0, 1),
    ("zj", 5, 1, 1),
    ("xd", 3, 1),
    ("lj", 5, 0),
    ("zj", 4, 3, 1),
    ("lj", 4, 0),
    ("pw", 1),
    ("zj", 5, 2, 0),
    ("pw", 2),
    ("f1", 8),
    ("pw", 0),
    ("conv", 0, 0),
    ("conv", 0, 1),
    ("conv", 0, 2),
    ("zj", 5, 2, 1),
    ("zj", 4, 2, 0),
    ("zj", 6, 1),
    ("zj", 5, 3, 0),
    ("f1", 7),
    ("act", 0),
    ("zj", 4, 3, 0),
    ("zj", 5, 3, 1),
    ("xd", 3, 2),
    ("nt", 0),
    ("lj", 4, 1),
    ("yd", 3, 2),
    ("yd", 3, 3),
    ("zj", 8, 1, 0),
    ("xd", 3, 3),
    ("zj", 6, 2),
    ("yf", 3, 0),
    ("lj", 5, 1),
    ("lj", 5, 2),
    ("xf", 3, 0),
    ("yd", 6, 0),
    ("zj", 8, 2, 0),
    ("zj", 6, 3),
    ("zj", 8, 1, 1),
    ("lj", 4, 2),
    ("head_grads", 0, 0),
    ("xd", 6, 0),
    ("e0", 9),
    ("lj", 4, 3),
    ("lj", 5, 3),
    ("zj", 7, 1, 0),
    ("yd", 6, 1),
    ("head_grads", 0, 1),
    ("zj", 7, 1, 1),
    ("lj", 8, 0),
    ("zj", 7, 2, 0),
    ("xd", 6, 1),
    ("yf", 3, 1),
    ("lj", 7, 0),
    ("xf", 3, 1),
    ("zj", 8, 2, 1),
    ("pw", 5),
    ("yd", 6, 2),
    ("ft", 1),
    ("pw", 4),
    ("zj", 7, 2, 1),
    ("xd", 6, 2),
    ("yd", 6, 3),
    ("pw", 3),
    ("zj", 8, 3, 0),
    ("conv", 1, 0),
    ("zj", 7, 3, 1),
    ("conv", 1, 1),
    ("xd", 6, 3),
    ("zj", 8, 3, 1),
    ("zj", 7, 3, 0),
    ("conv", 1, 2),
    ("zj", 9, 1),
    ("lj", 7, 1),
    ("e0", 10),
    ("xf", 6, 0),
    ("e0", 11),
    ("lj", 8, 1),
    ("act", 1),
    ("xf", 6, 1),
    ("yf", 6, 0),
    ("lj", 7, 2),
    ("zj", 9, 2),
    ("lj", 8, 2),
    ("zj", 9, 3),
    ("yd", 9, 0),
    ("yf", 6, 1),
    ("xd", 9, 0),
    ("lj", 8, 3),
    ("lj", 7, 3),
    ("nt", 1),
    ("ft", 2),
    ("pw", 8),
    ("yd", 9, 1),
    ("pw", 6),
    ("xd", 9, 1),
    ("pw", 7),
    ("conv", 2, 0),
    ("conv", 2, 1),
    ("f1", 10),
    ("zj", 10, 1, 0),
    ("zj", 11, 1, 0),
    ("head_grads", 1, 0),
    ("xd", 9, 2),
    ("head_grads", 1, 1),
    ("xd", 9, 3),
    ("yd", 9, 2),
    ("zj", 10, 2, 0),
    ("yf", 9, 0),
    ("yd", 9, 3),
    ("xf", 9, 0),
    ("s1", 10),
    ("s1", 11),
    ("conv", 2, 2),
    ("act", 2),
    ("yf", 9, 1),
    ("xf", 9, 1),
    ("trunk_cot",),
    ("f1", 11),
    ("zj", 10, 1, 1),
    ("nt", 2),
    ("pw", 9),
    ("unpack", 2),
    ("zj", 10, 2, 1),
    ("dtap", 2),
    ("zj", 10, 3, 0),
    ("head_grads", 2, 0),
    ("zj", 11, 2, 0),
    ("dlinear", 2),
    ("zj", 10, 3, 1),
    ("head_grads", 2, 1),
    ("zj", 11, 3, 0),
    ("zj", 11, 1, 1),
    ("s2", 10, 0),
    ("s1", 9),
    ("conv_back", 2, 0),
    ("lj", 10, 0),
    ("s2", 10, 1),
    ("conv_grads", 2, 0),
    ("conv_grads", 2, 1),
    ("lj", 10, 1),
    ("zj", 11, 2, 1),
    ("s2", 11, 0),
    ("conv_back", 2, 1),
    ("lj", 10, 2),
    ("lj", 11, 0),
    ("conv_back", 2, 2),
    ("lj", 10, 3),
    ("lj", 11, 1),
    ("s2a", 9),
    ("conv_grads", 2, 2),
    ("pw", 10),
    ("s2", 11, 1),
    ("s2b", 9),
    ("s1", 8),
    ("s1", 7),
    ("unpack", 1),
    ("dtap", 1),
    ("lj", 11, 2),
    ("dlinear", 1),
    ("s3a", 9),
    ("conv_back", 1, 0),
    ("s3b", 9),
    ("s2", 8, 0),
    ("zj", 11, 3, 1),
    ("zd", 11, 0),
    ("conv_back", 1, 1),
    ("s1", 6),
    ("conv_grads", 1, 0),
    ("s2", 7, 0),
    ("conv_grads", 1, 1),
    ("lj", 11, 3),
    ("conv_grads", 1, 2),
    ("s1", 5),
    ("zd", 10, 0),
    ("s2", 7, 1),
    ("pw", 11),
    ("s1", 4),
    ("s2", 8, 1),
    ("unpack", 0),
    ("conv_back", 1, 2),
    ("zd", 9, 0),
    ("dtap", 0),
    ("zd", 8, 0),
    ("dlinear", 0),
    ("zd", 7, 0),
    ("zu", 9, 3),
    ("s2", 4, 0),
    ("s2b", 6),
    ("zd", 9, 1),
    ("zu", 8, 3),
    ("zd", 10, 1),
    ("s1", 3),
    ("conv_back", 0, 0),
    ("s2a", 6),
    ("zd", 7, 1),
    ("zu", 11, 3),
    ("zu", 9, 2),
    ("s2", 5, 1),
    ("conv_grads", 0, 0),
    ("conv_grads", 0, 1),
    ("zu", 7, 3),
    ("conv_grads", 0, 2),
    ("s1", 1),
    ("s1", 2),
    ("zu", 10, 3),
    ("zd", 8, 1),
    ("zd", 11, 1),
    ("s2", 5, 0),
    ("s3a", 6),
    ("s3b", 6),
    ("joined", 0),
    ("zu", 4, 3),
    ("conv_back", 0, 1),
    ("s2a", 3),
    ("zu", 5, 3),
    ("s2b", 3),
    ("s2", 1, 0),
    ("s3a", 3),
    ("zu", 6, 3),
    ("s2", 2, 0),
    ("joined", 1),
    ("s1", 0),
    ("m0",),
    ("zu", 1, 3),
    ("s2", 4, 1),
    ("zu", 2, 3),
    ("zu", 11, 2),
    ("zu", 10, 2),
    ("zu", 8, 2),
    ("zd", 6, 0),
    ("s2", 1, 1),
    ("zu", 7, 2),
    ("zf", 9),
    ("zu", 1, 2),
    ("zu", 6, 2),
    ("zd", 2, 0),
    ("m1", 0),
    ("zf", 11),
    ("s2", 2, 1),
    ("zd", 4, 0),
    ("pf", 3),
    ("s3b", 3),
    ("s2a", 0),
    ("zu", 2, 2),
    ("zd", 5, 0),
    ("s2b", 0),
    ("zf", 10),
    ("conv_back", 0, 2),
    ("zu", 4, 2),
    ("zd", 1, 0),
    ("image_grad",),
    ("m1", 1),
    ("ff", 11),
    ("zd", 2, 1),
    ("zu", 5, 2),
    ("pf", 5),
    ("zf", 8),
    ("s3a", 0),
    ("zf", 7),
    ("zd", 3, 0),
    ("s3b", 0),
    ("zd", 0, 0),
    ("zd", 1, 1),
    ("zd", 5, 1),
    ("m1", 2),
    ("zd", 4, 1),
    ("m2", 1),
    ("ff", 10),
    ("zd", 6, 1),
    ("zd", 0, 1),
    ("zu", 0, 3),
    ("zd", 3, 1),
    ("pf", 4),
    ("t0",),
    ("zf", 2),
    ("zu", 3, 3),
    ("ff", 7),
    ("ff", 8),
    ("zf", 1),
    ("zu", 3, 2),
    ("zu", 0, 2),
    ("zf", 5),
    ("t1",),
    ("zf", 4),
    ("m2", 2),
    ("m2", 3),
    ("m3",),
    ("zf", 6),
    ("ff", 2),
    ("ff", 1),
    ("zf", 0),
    ("zf", 3),
    ("pf", 2),
    ("ff", 5),
    ("pf", 0),
    ("ff", 4),
    ("pf", 1),
    ("t2",),
    ("finish",),
)


def kernel(
    order,
    conv_in,
    head_in,
    tap_in,
    gain_in,
    offset_in,
    height_in,
    width_in,
    image_in,
    trunk_in,
    cot_in,
    trunk_out,
    heads_out,
    image_out,
    conv_out,
    head_out,
    scale_out,
    rms_out,
    W,
    F3,
    FT,
    FTP,
    NTP,
    N,
    GP,
    DT,
    RN,
    COT,
    COTP,
    ACC,
    D3P,
    GC2,
    GH,
    RL,
    RAW,
    HB,
    H,
    SQ,
    LB,
    MR,
    ZB,
    SB,
    SR,
    ag_recv,
    ag_send,
    load_sem,
    rs_recv,
    rs_send,
    pair_recv,
    pair_send,
    in_sem,
    out_sem,
    small_recv,
    small_send,
):
    dpi, fsi = lax.axis_index("dp"), lax.axis_index("fsdp")
    y, c, z, x = dpi // 2, dpi % 2, fsi // 2, fsi % 2

    def dev(yy, cc, zz, xx):
        return (yy * 2 + cc, zz * 2 + xx)

    xn, yn, pn = dev(y, c, z, 1 - x), dev(1 - y, c, z, x), dev(y, 1 - c, z, x)
    up, dn = dev(y, c, jnp.minimum(z + 1, 3), x), dev(y, c, jnp.maximum(z - 1, 0), x)
    sig = [z, z + 1 - 2 * (z % 2), jnp.where(z < 2, 2, 1), jnp.where(z < 2, 3, 0)]
    height, width = height_in[0], width_in[0]

    def when(cond, fn):
        pl.when(cond)(fn)

    def remote(src, dst, send, recv, t):
        return pltpu.make_async_remote_copy(
            src_ref=src, dst_ref=dst, send_sem=send, recv_sem=recv, device_id=t, device_id_type=MESH
        )

    def row(p, yy, cc, s, xx, off=0):
        return pl.multiple_of(BASES[p] + ((2 * yy + cc) * 8 + 2 * s + xx) * UNITS[p] + off, 32)

    def x_first(kind):
        return kind not in (2, 4)

    def shard(r, first, s, last):
        p, off, _, kind = ROUTES[r]
        yy, xx = (last, first) if x_first(kind) else (first, last)
        return row(p, yy, c, s, xx, off)

    def ends(r, routes=ROUTES):
        return (x, y, xn, yn) if x_first(routes[r][3]) else (y, x, yn, xn)

    def place(r, line):
        first, last, _, _ = ends(r)
        return (1 - first if line % 2 else first), (1 - last if line // 2 else last)

    def ag(r, at, si, ri, t, n=1):
        part = W.at[pl.ds(at, ROUTES[r][2] * n)]
        return remote(part, part, ag_send.at[ROUTES[r][0], si], ag_recv.at[r, ri], t)

    def ag_start(r, at, si, ri, t):
        ag(r, at, si, ri, t).start()

    def ag_wait(r, ri, n=1):
        ag(r, BASES[ROUTES[r][0]], 0, ri, xn, n).wait_recv()

    def pair(r, at):
        ag_start(r, at, 0, PAIR[ROUTES[r][3]], pn)

    def load(p):
        return pltpu.make_async_copy(
            conv_in.at[p], W.at[pl.ds(row(p, y, c, z, x), CONV_UNIT)], load_sem.at[p]
        )

    def ld(p):
        load(p).wait()

    def along(r, s, at, line, passed=True):
        climbs = (s < z) & (z < 3) if passed else z < 3
        sinks = (s > z) & (z > 0) if passed else z > 0
        when(climbs, lambda: ag_start(r, at, 1, 4 * line + s, up))
        when(sinks, lambda: ag_start(r, at, 2, 4 * line + s, dn))

    def fan(r, s, at, line):
        kind = ROUTES[r][3]
        if kind == 0:
            ag_start(r, at, 0, 4 + s, xn)
            ag_start(r, at, 0, 8 + s, yn)
        elif kind < 3:
            ag_start(r, at, 0, 8 + 4 * line + s, ends(r)[3])
        pair(r, at)

    def e0(r):
        first, last, fn, ln = ends(r)
        at = shard(r, first, z, last)
        if ROUTES[r][3]:
            ag_start(r, at, 0, 16, fn)
        if ROUTES[r][3] > 2:
            ag_start(r, at, 0, 17, ln)
        along(r, z, at, 0, False)
        fan(r, z, at, 0)

    def f1(r):
        first, last, _, ln = ends(r)
        at = shard(r, 1 - first, z, last)
        ag_wait(r, 16)
        if ROUTES[r][3] > 2:
            ag_start(r, at, 0, 18, ln)
        along(r, z, at, 1, False)
        fan(r, z, at, 1)

    def g1(r, i):
        f, l = place(r, 2 + i)
        at = shard(r, f, z, l)
        ag_wait(r, 17 + i)
        along(r, z, at, 2 + i, False)
        fan(r, z, at, 2 + i)

    def zj(r, j, only=0):
        s = sig[j]
        for line in range(4) if ROUTES[r][3] > 2 else (only,):
            f, l = place(r, line)
            at = shard(r, f, s, l)
            ag_wait(r, 4 * line + s)
            along(r, s, at, line)
            fan(r, s, at, line)

    def lj(r, j):
        first, last, _, _ = ends(r)
        s = sig[j]
        for line in range(2):
            ag_wait(r, 8 + 4 * line + s)
            pair(r, shard(r, place(r, line)[0], s, 1 - last))

    def xd(r, j):
        s = sig[j]
        at = shard(r, 1 - x, s, y)
        ag_wait(r, 4 + s)
        when(s % 2 == 0, lambda: ag_start(r, at, 0, 12 + s, yn))
        pair(r, at)

    def yd(r, j):
        s = sig[j]
        at = shard(r, x, s, 1 - y)
        ag_wait(r, 8 + s)
        when(s % 2 == 1, lambda: ag_start(r, at, 0, 12 + s, xn))
        pair(r, at)

    def yf(r, k):
        s = jnp.where(z < 2, 2 * k, 2 - 2 * k)
        ag_wait(r, 12 + s)
        pair(r, shard(r, 1 - x, s, 1 - y))

    def xf(r, k):
        s = jnp.where(z < 2, 1 + 2 * k, 3 - 2 * k)
        ag_wait(r, 12 + s)
        pair(r, shard(r, 1 - x, s, 1 - y))

    def pw(r):
        ag_wait(r, PAIR[ROUTES[r][3]], 16)

    def sent(copy_of, sems, main, line, climbs, sinks):
        copy_of(main, sems.at[0]).wait_send()
        for k in range(4):
            if climbs(k):
                when(z == k, lambda: copy_of(line * climbs(k), sems.at[1]).wait_send())
            if sinks(k):
                when(z == k, lambda: copy_of(line * sinks(k), sems.at[2]).wait_send())

    def ag_end(p):
        mine = [(m, kind) for q, _, m, kind in ROUTES if q == p]

        def copy_of(rows, sem):
            return remote(W.at[pl.ds(0, rows)], W.at[pl.ds(0, rows)], sem, ag_recv.at[0, 0], xn)

        sent(
            copy_of,
            ag_send.at[p],
            sum(m * (28, 25, 25, 19, 19)[kind] for m, kind in mine),
            sum(m * (1, 2, 2, 4, 4)[kind] for m, kind in mine),
            lambda k: k + 1 if k < 3 else 0,
            lambda k: 4 - k if k > 0 else 0,
        )

    def grads(p):
        if p == 2:
            return GC2, 0
        if p < 2:
            return W, BASES[2] + (1 - p) * 16 * CONV_UNIT
        return GH, (p - 3) * 16 * HEAD_UNIT

    def grow(r, first, s, last):
        p, off, _, kind = BACK[r]
        yy, xx = (last, first) if x_first(kind) else (first, last)
        return pl.multiple_of(grads(p)[1] + (yy * 8 + 2 * s + xx) * UNITS[p] + off, 32)

    def slot(r, k):
        return pl.multiple_of(LAND[r] + k * BACK[r][2], 32)

    def rs(r, at, k, si, ri, t, n=1):
        m = BACK[r][2] * n
        return remote(
            grads(BACK[r][0])[0].at[pl.ds(at, m)],
            RL.at[pl.ds(slot(r, k), m)],
            rs_send.at[BACK[r][0], si],
            rs_recv.at[r, ri],
            t,
        )

    def rs_start(r, at, k, i, t):
        rs(r, at, k, 0 if i < 6 else 1 if i < 9 else 2, i, t).start()

    def rs_wait(r, ri, n=1):
        rs(r, grads(BACK[r][0])[1], 0, 0, ri, xn, n).wait_recv()

    def add(r, at, *ks):
        ref, rows = grads(BACK[r][0])[0], pl.ds(at, BACK[r][2])
        total = ref[rows, :].astype(F32)
        for k in ks:
            total = total + RL[pl.ds(slot(r, k), BACK[r][2]), :].astype(F32)
        ref[rows, :] = total.astype(BF)

    def s1(r):
        if BACK[r][3] == 0:
            for s in (0, 2):
                rs_start(r, grow(r, 1 - x, s, 1 - y), s // 2, 0, yn)
            for s in (1, 3):
                rs_start(r, grow(r, 1 - x, s, 1 - y), 2 + s // 2, 1, xn)
            for s in (1, 3):
                rs_start(r, grow(r, 1 - x, s, y), 4 + s, 2, xn)
            for s in (0, 2):
                rs_start(r, grow(r, x, s, 1 - y), 8 + s, 4, yn)
            return
        if BACK[r][3] > 2:
            far(r)
            return
        _, last, _, ln = ends(r, BACK)
        for i, group in enumerate(((0, 3), (1, 2))):
            for s in group:
                for f in range(2):
                    rs_start(r, grow(r, f, s, 1 - last), 2 * s + f, i, ln)

    def s2a(r):
        rs_wait(r, 0, 2)
        for s in (0, 2):
            at = grow(r, 1 - x, s, y)
            add(r, at, s // 2)
            rs_start(r, at, 4 + s, 3, xn)

    def s2b(r):
        rs_wait(r, 1, 2)
        for s in (1, 3):
            at = grow(r, x, s, 1 - y)
            add(r, at, 2 + s // 2)
            rs_start(r, at, 8 + s, 5, yn)

    def s3a(r):
        rs_wait(r, 2, 2)
        rs_wait(r, 4, 2)
        for s in range(4):
            add(r, grow(r, x, s, y), 4 + s if s % 2 else 8 + s)

    def line_of(r):
        kind, last = BACK[r][3], ends(r, BACK)[1]
        if kind == 0:
            return ((x, y),), 12, 1
        if kind < 3:
            return ((0, last), (1, last)), 8, 2
        return ((0, 0), (1, 0), (0, 1), (1, 1)), 0, 4

    def rs_up(r, t):
        places, base, n = line_of(r)
        for i, (f, l) in enumerate(places):
            rs_start(r, grow(r, f, t, l), base + n * t + i, 5 + t, up)

    def rs_down(r, t):
        places, base, n = line_of(r)
        for i, (f, l) in enumerate(places):
            k = jnp.where(t == z - 1, 4, t)
            rs_start(r, grow(r, f, t, l), base + n * k + i, 9 + t, dn)

    def far(r):
        @pl.when(z == 0)
        def _():
            for t in (3, 2, 1):
                rs_up(r, t)

        @pl.when(z == 3)
        def _():
            for t in (0, 1, 2):
                rs_down(r, t)

    def s3b(r):
        rs_wait(r, 3, 2)
        rs_wait(r, 5, 2)
        for s in range(4):
            add(r, grow(r, x, s, y), 8 + s if s % 2 else 4 + s)
        far(r)

    def s2(r, i):
        rs_wait(r, i, 4)
        for s in ((0, 3), (1, 2))[i]:
            for f in range(2):
                add(r, grow(r, f, s, ends(r, BACK)[1]), 2 * s + f)

        @pl.when(z == 0)
        def _():
            for t in ((3,), (2, 1))[i]:
                rs_up(r, t)

        @pl.when(z == 3)
        def _():
            for t in ((0,), (1, 2))[i]:
                rs_down(r, t)

    def zu(r, t):
        @pl.when((z > 0) & (z < t))
        def _():
            places, base, n = line_of(r)
            rs_wait(r, 5 + t, n)
            for i, (f, l) in enumerate(places):
                add(r, grow(r, f, t, l), base + n * t + i)
            rs_up(r, t)

    def zd(r, t):
        @pl.when((z < 3) & (z > t))
        def _():
            places, base, n = line_of(r)
            rs_wait(r, 9 + t, n)
            for i, (f, l) in enumerate(places):
                add(r, grow(r, f, t, l), base + n * t + i)
            rs_down(r, t)

    def zf(r):
        places, base, n = line_of(r)
        first, last, fn, ln = ends(r, BACK)
        when(z > 0, lambda: rs_wait(r, 5 + z, n))
        when(z < 3, lambda: rs_wait(r, 9 + z, n))

        def both(*ks):
            for i, (f, l) in enumerate(places):
                add(r, grow(r, f, z, l), *[base + n * k + i for k in ks])

        when(z == 0, lambda: both(4))
        when(z == 3, lambda: both(3))
        when((z > 0) & (z < 3), lambda: both(z, 4))
        if n == 2:
            rs_start(r, grow(r, 1 - first, z, last), 18, 2, fn)
        if n == 4:
            for f in range(2):
                rs_start(r, grow(r, f, z, 1 - last), 20 + f, 0, ln)

    def gg(r):
        first, last, fn, _ = ends(r, BACK)
        rs_wait(r, 0, 2)
        for f in range(2):
            add(r, grow(r, f, z, last), 20 + f)
        rs_start(r, grow(r, 1 - first, z, last), 22, 2, fn)

    def ff(r):
        first, last, _, _ = ends(r, BACK)
        rs_wait(r, 2)
        add(r, grow(r, first, z, last), 22 if BACK[r][3] > 2 else 18)

    def conv_store(p):
        ref, base = grads(p)
        at = pl.multiple_of(base + (y * 8 + 2 * z + x) * CONV_UNIT, 32)
        return pltpu.make_async_copy(ref.at[pl.ds(at, CONV_UNIT)], conv_out.at[p], out_sem.at[p])

    def diagonal():
        shape = (64, 64)
        return lax.broadcasted_iota(jnp.int32, shape, 0) == lax.broadcasted_iota(jnp.int32, shape, 1)

    def tap_column(layer):
        wide = jnp.broadcast_to(tap_in[layer : layer + 1, :].astype(F32), (64, 64))
        return jnp.sum(jnp.where(diagonal(), wide, 0.0), axis=1, keepdims=True)

    def left_lanes(count):
        return lax.broadcasted_iota(jnp.int32, (count, 128), 1) < 64

    def unfold(v, upper):
        turned = pltpu.roll(v, 64, 1)
        return jnp.concatenate([jnp.where(upper, v, 0.0), jnp.where(upper, turned, 0.0)], axis=0)

    def pf(p):
        if p < 3:
            conv_store(p).start()
            return
        layer = 5 - p
        base = pl.multiple_of(grads(p)[1] + (y * 8 + 2 * z + x) * HEAD_UNIT, 32)
        full = [GH[pl.ds(base + 64 * t, 64), :].astype(F32) for t in range(3)]
        half = unfold(GH[pl.ds(base + 192, 32), :].astype(F32), (left_lanes(32) == (c == 0)))
        tiles = [jnp.where(c == 0, a, b) for a, b in zip(full + [half], [half] + full)]
        total = jnp.zeros((64, 1), F32)
        for t in range(4):
            raw = RAW[layer, 64 * t : 64 * t + 64, :].astype(F32)
            total = total + jnp.sum(tiles[t] * raw, axis=1, keepdims=True)
        SB[0, :, layer : layer + 1] = total
        tap = tap_column(layer)
        tiles = [v * tap for v in tiles]
        rolled = [pltpu.roll(v, 64, 1) for v in tiles]
        left = left_lanes(64)
        for t in range(4):
            later = rolled[t + 1] if t < 3 else rolled[t]
            v = jnp.where(c == 0, tiles[t], jnp.where(left, rolled[t], later))
            if t < 3:
                head_out[layer, :, 128 * t : 128 * t + 128] = v
            else:
                head_out[layer, :, 384:448] = v[:, 0:64]

    def rs_end(p):
        mine = [(m, kind) for q, _, m, kind in BACK if q == p]
        ref, base = grads(p)

        def copy_of(rows, sem):
            return remote(ref.at[pl.ds(base, rows)], RL.at[pl.ds(0, rows)], sem, rs_recv.at[0, 0], xn)

        sent(
            copy_of,
            rs_send.at[p],
            sum(m * (12, 9, 9, 3, 3)[kind] for m, kind in mine),
            sum(m * (1, 2, 2, 4, 4)[kind] for m, kind in mine),
            lambda k: 3 - k,
            lambda k: k,
        )

    def share_ft(layer):
        return remote(FT.at[layer], FTP.at[layer], pair_send.at[layer], pair_recv.at[layer], pn)

    def share_nt(layer):
        i = 3 + layer
        src = GC2.at[pl.ds(0, 6 * 512)]
        return remote(src, NTP.at[layer % 2], pair_send.at[i], pair_recv.at[i], pn)

    def share_cot(k):
        src = COT.at[pl.ds(7 * k + 3 * (1 - c), 4)]
        return remote(src, COTP.at[k], pair_send.at[6 + k], pair_recv.at[6 + k], pn)

    def share_d(layer, k):
        i = 8 + 2 * layer + k
        src = F3.at[:, 2 * k + 1 - c]
        return remote(src, D3P.at[layer % 2, :, k], pair_send.at[i], pair_recv.at[i], pn)

    def blocks(count, fn):
        def step(m, carry):
            fn(m)
            return carry

        lax.fori_loop(0, count, step, 0)

    one_time = jnp.where(dpi >= 0, 1, 2)

    def apart(fn):
        def wrapped(*args):
            def step(m, carry):
                fn(*args)
                return carry

            lax.fori_loop(0, one_time, step, 0)

        return wrapped

    def at48(m, base=0):
        return pl.ds(pl.multiple_of(base + 48 * m, 8 if base == 8 else 16), 48)

    def place48():
        i = lax.broadcasted_iota(jnp.int32, (48, 1), 0)
        second = i >= HIGH
        return jnp.where(second, i - HIGH, i), jnp.where(second, 1, 0)

    def mask_of(m):
        r, second = place48()
        return jnp.where((r < height) & (2 * m + second < width), 1.0, 0.0).astype(F32)

    def image_part(i):
        src = (image_in, trunk_in)[i // 4].at[:, pl.ds(128 * (i % 4), 128)]
        return pltpu.make_async_copy(src, GC2.at[pl.ds(3072 + PIX * i, PIX)], in_sem.at[i // 4])

    def image_wait(i):
        part = GC2.at[pl.ds(3072 + 4 * PIX * i, 4 * PIX)]
        pltpu.make_async_copy(part, part, in_sem.at[i]).wait()

    def cot_part(t):
        return pltpu.make_async_copy(
            cot_in.at[:, pl.ds(128 * t, 128)], COT.at[t, pl.ds(0, PIX)], in_sem.at[2]
        )

    def cot_wait(first, count, sem):
        part = COT.at[pl.ds(first, count), pl.ds(0, PIX)]
        pltpu.make_async_copy(part, part, sem).wait()

    def expand(first, masked):
        def one(m):
            at = at48(m, 8)
            for k in range(4):
                rows = pl.ds(pl.multiple_of(3072 + PIX * (first + k) + 48 * m, 16), 48)
                v = GC2[rows, :].astype(F32)
                if masked:
                    v = v * mask_of(m)
                    SQ[0:1, 128 * k : 128 * k + 128] += jnp.sum(v * v, axis=0, keepdims=True)
                ACC[at, 128 * k : 128 * k + 128] = v

        blocks(14, one)

    def start():
        for p in range(3):
            load(p).start()
        for i in range(8):
            image_part(i).start()
        for t in range(14):
            cot_part(t).start()
        barrier = pltpu.get_barrier_semaphore()
        for t in (xn, yn, pn):
            pl.semaphore_signal(barrier, inc=1, device_id=t, device_id_type=MESH)
        when(
            z < 3, lambda: pl.semaphore_signal(barrier, inc=1, device_id=up, device_id_type=MESH)
        )
        when(
            z > 0, lambda: pl.semaphore_signal(barrier, inc=1, device_id=dn, device_id_type=MESH)
        )
        pl.semaphore_wait(barrier, jnp.where((z == 0) | (z == 3), 4, 5))

    def prep_heads():
        left = left_lanes(64)
        ACC[0:64, :] = jnp.zeros((64, 512), F32)
        for layer in range(3):
            ACC[0:64, 0:448] = head_in[layer].astype(F32)
            tap = tap_column(layer)
            base = row(5 - layer, y, c, z, x)
            tiles = [ACC[0:64, 128 * t : 128 * t + 128] for t in range(4)]
            rolled = [pltpu.roll(v, 64, 1) for v in tiles]
            moved = [
                jnp.where(left, rolled[t - 1] if t else 0.0, rolled[t]) for t in range(4)
            ]
            for t in range(4):
                v = jnp.where(c == 0, tiles[t], moved[t])
                RAW[layer, 64 * t : 64 * t + 64, :] = v.astype(BF)
            for t in range(3):
                v = jnp.where(c == 0, tiles[t], moved[t + 1])
                W[pl.ds(base + 64 * t, 64), :] = (v * tap).astype(BF)
            v = jnp.where(c == 0, tiles[3], moved[0]) * tap
            W[pl.ds(base + 192, 32), :] = (v[0:32] + pltpu.roll(v[32:64], 64, 1)).astype(BF)

    def prep_in():
        ACC[...] = jnp.zeros_like(ACC)
        SQ[...] = jnp.zeros_like(SQ)
        SB[0] = jnp.zeros((64, 128), F32)
        for b in range(3):
            for k in range(4):
                F3[b, k, 0:32, :] = jnp.zeros((32, 128), BF)
                F3[b, k, 704:832, :] = jnp.zeros((128, 128), BF)
        image_wait(0)
        expand(0, True)
        pixels = (height * width).astype(F32) * (1.0 / 512.0)
        SQ[5:6, :] = jnp.full((1, 512), pixels, F32)

    def shifts():
        r, _ = place48()

        def one(m):
            v64 = ACC[pl.ds(pl.multiple_of(48 * m, 8), 64), :]
            for b in range(3):
                v = v64[7 + b : 55 + b, :]
                if b != 1:
                    v = jnp.where(r == (0 if b == 0 else HIGH - 1), 0.0, v)
                v = v.astype(BF)
                for k in range(4):
                    F3[b, k, at48(m, 32), :] = v[:, 128 * k : 128 * k + 128]

        blocks(14, one)

    def ft(layer):
        shifts()

        def one(m):
            v = ACC[pl.ds(pl.multiple_of(8 + 128 * m, 8), 128), :]
            FT[layer, :, pl.ds(pl.multiple_of(128 * m, 128), 128)] = v.T.astype(BF)

        blocks(6, one)
        share_ft(layer).start()

    def prep_cot():
        def clear(t):
            COT[t, PIX:PAD, :] = jnp.zeros((PAD - PIX, 128), BF)

        blocks(14, clear)
        cot_wait(0, 14, in_sem.at[2])
        for k in range(2):
            share_cot(k).start()

    def taps(a, transposed):
        first = 8 + HIGH * a if not transposed else 8 + HIGH * (2 - a)
        order = (0, 1, 2) if not transposed else (2, 1, 0)
        return [
            jnp.concatenate([F3[b, k, first : first + PIX, :] for k in range(4)], axis=1)
            for b in order
        ]

    def weights(layer, a, b):
        first = BASES[layer] + 512 * (3 * b + a)
        return jnp.concatenate(
            [W[first + 4608 * k : first + 4608 * k + 512, :] for k in range(4)], axis=1
        )

    @apart
    def conv(layer, a):
        v = jnp.dot(
            jnp.concatenate(taps(a, False), axis=1),
            jnp.concatenate([weights(layer, a, b) for b in range(3)], axis=0),
            preferred_element_type=F32,
        )
        if a == 0:
            ACC[8 : 8 + PIX, :] = v
        else:
            ACC[8 : 8 + PIX, :] += v

    def act(layer):
        gain, offset = gain_in[layer : layer + 1, :], offset_in[layer : layer + 1, :]
        k = 0.7978845608028654

        def one(m):
            rows, at = at48(m, 8), at48(m)
            u = ACC[rows, :] * gain + offset
            mask = mask_of(m)
            u2 = u * u
            t = jnp.tanh(k * u * (1.0 + 0.044715 * u2))
            half = 0.5 * (1.0 + t) * mask
            f = u * half
            slope = half + (0.5 * k) * mask * u * (1.0 - t * t) * (1.0 + 0.134145 * u2)
            squares = f * f
            rn = lax.rsqrt(jnp.mean(squares, axis=-1, keepdims=True) + 1e-5)
            GP[layer, at, :] = (slope * gain).astype(BF)
            N[layer, at, :] = (f * rn).astype(BF)
            RN[at, layer : layer + 1] = rn
            SQ[layer + 1 : layer + 2, :] += jnp.sum(squares, axis=0, keepdims=True)
            if layer < 2:
                ACC[rows, :] = f
            else:
                v = f.astype(BF)
                for b in range(4):
                    F3[1, b, at48(m, 32), :] = v[:, 128 * b : 128 * b + 128]

        blocks(14, one)
        if layer == 2:
            for b in range(4):
                trunk_store(b).start()

    def trunk_store(b):
        return pltpu.make_async_copy(
            F3.at[1, b, pl.ds(32, PIX)], trunk_out.at[:, pl.ds(128 * b, 128)], out_sem.at[3]
        )

    def nt(layer):
        if layer > 0:
            share_nt(layer - 1).wait_send()

        turn(layer)
        share_nt(layer).start()

    @apart
    def turn(layer):
        for m in range(6):
            v = N[layer, 128 * m : min(128 * m + 128, PIX), :].astype(F32)
            if m == 5:
                v = jnp.concatenate([v, jnp.zeros((PAD - PIX, 512), F32)], axis=0)
            GC2[512 * m : 512 * m + 512, :] = v.T.astype(BF)

    def head_grads(layer, k):
        if k == 0:
            share_nt(layer).wait_recv()
        if layer == 0:
            share_cot(k).wait_recv()
        head_grads_of(layer, k)

    @apart
    def head_grads_of(layer, k):
        mine = [GC2[512 * m : 512 * m + 512, :] for m in range(6)]
        theirs = [NTP[layer % 2, 512 * m : 512 * m + 512, :] for m in range(6)]
        own = [COT[7 * k + 4 * c + i] for i in range(3)] + [COT[7 * k + 3]]
        other = [COTP[k, c + i] for i in range(3)] + [COTP[k, 3 * (1 - c)]]
        v = jnp.dot(
            jnp.concatenate(mine + theirs, axis=1),
            jnp.concatenate(
                [jnp.concatenate(own, axis=1), jnp.concatenate(other, axis=1)], axis=0
            ),
            preferred_element_type=F32,
        )
        base = grads(5 - layer)[1] + k * 8 * HEAD_UNIT
        valid = left_lanes(32) == (c == 0)
        for f in range(8):
            first = base + f * HEAD_UNIT
            for t in range(3):
                part = v[64 * f : 64 * f + 64, 128 * t : 128 * t + 128]
                GH[first + 64 * t : first + 64 * t + 64, :] = part.astype(BF)
            half = v[64 * f : 64 * f + 64, 384:512]
            lower = pltpu.roll(half[32:64], 64, 1)
            GH[first + 192 : first + 224, :] = jnp.where(valid, half[0:32], lower).astype(BF)

    def unpack(layer):
        left = left_lanes(32)

        def one(f):
            for k in range(2):
                base = BASES[5 - layer] + 16 * k * HEAD_UNIT + 192
                low, high = [
                    W[pl.ds(pl.multiple_of(base + (8 * i + f) * HEAD_UNIT, 32), 32), :].astype(F32)
                    for i in range(2)
                ]
                HB[layer, k, f, 0:32, :] = jnp.where(left, low, high).astype(BF)
                v = jnp.where(left, pltpu.roll(low, 64, 1), pltpu.roll(high, 64, 1))
                HB[layer, k, f, 32:64, :] = v.astype(BF)

        blocks(8, one)

    def head_pair(layer, k, low=0, high=7):
        def tile(f, t):
            if t == 3:
                return HB[layer, k, f]
            i, t = (0, t) if t < 3 else (1, t - 4)
            first = BASES[5 - layer] + (16 * k + 8 * i + f) * HEAD_UNIT + 64 * t
            return W[first : first + 64, :]

        return jnp.concatenate(
            [jnp.concatenate([tile(f, t) for f in range(8)], axis=0) for t in range(low, high)], axis=1
        )

    def dtap(layer):
        h_of(layer)

        def one(m):
            at = at48(m)
            h = H[at, :]
            n = N[layer, at, :].astype(F32)
            mean = jnp.mean(h * n, axis=-1, keepdims=True)
            DT[layer, at, :] = ((h - n * mean) * RN[at, layer : layer + 1]).astype(BF)

        blocks(14, one)

    @apart
    def h_of(layer):
        H[...] = lax.dot_general(
            jnp.concatenate([COT[i, 0:PIX, :] for i in range(14)], axis=1),
            jnp.concatenate([head_pair(layer, k) for k in range(2)], axis=1),
            (((1,), (1,)), ((), ())),
            preferred_element_type=F32,
        )

    def joined(k):
        if k == 0:
            for i in range(2):
                share_cot(i).wait_send()
        joined_of(k, 0, 4)
        joined_of(k, 4, 7)
        for i in range(7):
            heads_store(7 * k + i).start()

    @apart
    def joined_of(k, first, last):
        v = jnp.dot(
            jnp.concatenate([N[i] for i in range(3)], axis=1),
            jnp.concatenate([head_pair(i, k, first, last) for i in range(3)], axis=0),
            preferred_element_type=F32,
        )
        squares = jnp.sum(v * v, axis=0, keepdims=True)
        for i in range(last - first):
            SQ[4:5, 0:128] += squares[:, 128 * i : 128 * i + 128]
            COT[7 * k + first + i, 0:PIX, :] = v[:, 128 * i : 128 * i + 128].astype(BF)

    def heads_store(t):
        return pltpu.make_async_copy(
            COT.at[t, pl.ds(0, PIX)], heads_out.at[:, pl.ds(128 * t, 128)], in_sem.at[3 + t // 7]
        )

    def trunk_cot():
        image_wait(1)
        expand(4, False)

    def dlinear(layer):
        def one(m):
            rows, at = at48(m, 8), at48(m)
            g = ACC[rows, :] + DT[layer, at, :].astype(F32)
            ACC[rows, :] = g * GP[layer, at, :].astype(F32)

        blocks(14, one)
        if layer == 2:
            part = F3.at[1, :, pl.ds(32, PIX)]
            pltpu.make_async_copy(part, part, out_sem.at[3]).wait()
        else:
            for k in range(2):
                share_d(layer + 1, k).wait_send()
        shifts()
        for k in range(2):
            share_d(layer, k).start()

    @apart
    def conv_back(layer, a):
        v = lax.dot_general(
            jnp.concatenate(taps(a, True), axis=1),
            jnp.concatenate([weights(layer, a, b) for b in range(3)], axis=1),
            (((1,), (1,)), ((), ())),
            preferred_element_type=F32,
        )
        if a == 0:
            ACC[8 : 8 + PIX, :] = v
        else:
            ACC[8 : 8 + PIX, :] += v

    def conv_grads(layer, a):
        if a == 0:
            share_ft(layer).wait_recv()
            for k in range(2):
                share_d(layer, k).wait_recv()
            if layer == 2:
                share_nt(2).wait_send()
            if layer == 1:
                ag_end(2)
        conv_grads_of(layer, a)

    @apart
    def conv_grads_of(layer, a):
        first = 8 + HIGH * (2 - a)
        rows = slice(first, first + PAD)
        own = [F3[2 - b, 2 * k + c, rows, :] for b in range(3) for k in range(2)]
        other = [D3P[layer % 2, 2 - b, k, rows, :] for b in range(3) for k in range(2)]
        v = jnp.dot(
            jnp.concatenate([FT[layer], FTP[layer]], axis=1),
            jnp.concatenate(
                [jnp.concatenate(own, axis=1), jnp.concatenate(other, axis=1)], axis=0
            ),
            preferred_element_type=F32,
        ).astype(BF)
        ref, base = grads(layer)
        for b in range(3):
            for k in range(2):
                r = base + 4608 * k + 512 * (3 * b + a)
                at = 256 * b + 128 * k
                ref[r : r + 512, :] = v[:, at : at + 128]

    def image_store():
        return pltpu.make_async_copy(DT.at[2], image_out, out_sem.at[4])

    def image_grad():
        def one(m):
            DT[2, at48(m), :] = (ACC[at48(m, 8), :] * mask_of(m)).astype(BF)

        blocks(14, one)
        image_store().start()

    def small(i):
        return remote(LB.at[i], MR.at[i], small_send.at[i], small_recv.at[i], (pn, xn, yn)[i])

    def line(s, i, t):
        return remote(ZB.at[s], ZB.at[s], small_send.at[i], small_recv.at[5 + s], t)

    def m0():
        v = SQ[:, 0:128]
        for i in range(1, 4):
            v = v + SQ[:, 128 * i : 128 * i + 128]
        LB[0] = v
        small(0).start()

    def m1(i):
        small(i).wait_recv()
        v = LB[i] + MR[i]
        if i < 2:
            LB[i + 1] = v
            small(i + 1).start()
            return
        ZB[z] = v
        when(z < 3, lambda: line(z, 5 + z, up).start())
        when(z > 0, lambda: line(z, 9 + z, dn).start())

    def m2(j):
        s = sig[j]
        line(s, 5, up).wait_recv()
        when((s < z) & (z < 3), lambda: line(s, 5 + s, up).start())
        when((s > z) & (z > 0), lambda: line(s, 9 + s, dn).start())

    def m3():
        total = ZB[0] + ZB[1] + ZB[2] + ZB[3]
        v = jnp.sum(total, axis=1, keepdims=True)
        which = lax.broadcasted_iota(jnp.int32, (8, 1), 0)
        wide = jnp.where(which == 4, 1792.0, 512.0).astype(F32)
        rms_out[...] = jnp.broadcast_to(jnp.sqrt(v / (v[5:6] * wide)), (8, 128))

    def scale_sum(i):
        return remote(SB.at[i], SR.at[i], small_send.at[3 + i], small_recv.at[3 + i], (pn, yn)[i])

    def t0():
        scale_sum(0).start()

    def t1():
        scale_sum(0).wait_recv()
        SB[1] = SB[0] + SR[0]
        scale_sum(1).start()

    def t2():
        scale_sum(1).wait_recv()
        total = SB[1] + SR[1]
        for layer in range(3):
            v = jnp.where(diagonal(), total[:, layer : layer + 1], 0.0)
            scale_out[layer : layer + 1, :] = jnp.sum(v, axis=0, keepdims=True)

    def finish():
        for p in range(6):
            if p != 2:
                ag_end(p)
            rs_end(p)
        for i in range(3):
            share_ft(i).wait_send()
            small(i).wait_send()
            conv_store(i).wait()
        for k in range(2):
            share_d(0, k).wait_send()
            scale_sum(k).wait_send()
        for s in range(4):
            when((z < 3) & (s <= z), lambda s=s: line(s, 5 + s, up).wait_send())
            when((z > 0) & (s >= z), lambda s=s: line(s, 9 + s, dn).wait_send())
        for k in range(2):
            cot_wait(7 * k, 7, in_sem.at[3 + k])
        image_store().wait()

    fns = dict(
        start=start, ld=ld, e0=e0, f1=f1, g1=g1, gg=gg, zj=zj, lj=lj, xd=xd, yd=yd, xf=xf, yf=yf, pw=pw,
        s1=s1, s2a=s2a, s2b=s2b, s3a=s3a, s3b=s3b, s2=s2, zu=zu, zd=zd, zf=zf, ff=ff, pf=pf,
        prep_heads=prep_heads, prep_in=prep_in, prep_cot=prep_cot, ft=ft, conv=conv, act=act, nt=nt,
        head_grads=head_grads, unpack=unpack, dtap=dtap, joined=joined, trunk_cot=trunk_cot,
        dlinear=dlinear, conv_back=conv_back, conv_grads=conv_grads, image_grad=image_grad,
        m0=m0, m1=m1, m2=m2, m3=m3, t0=t0, t1=t1, t2=t2, finish=finish,
    )
    for name, *args in order:
        fns[name](*args)


def patches(feature):
    height = feature.shape[1]
    breadth = feature.shape[2]
    padded = jnp.pad(feature, ((0, 0), (1, 1), (1, 1), (0, 0)))
    pieces = [
        padded[:, down_step : down_step + height, side_step : side_step + breadth, :]
        for down_step in range(3)
        for side_step in range(3)
    ]
    return jnp.concatenate(pieces, axis=-1)


def unpatch(stacked, channels):
    images, height, breadth, _ = stacked.shape
    padded = jnp.zeros((images, height + 2, breadth + 2, channels), jnp.float32)
    for down_step in range(3):
        for side_step in range(3):
            tap_index = 3 * down_step + side_step
            padded = padded.at[
                :, down_step : down_step + height, side_step : side_step + breadth, :
            ].add(stacked[..., tap_index * channels : (tap_index + 1) * channels])
    return padded[:, 1:-1, 1:-1, :]


def activate(linear, gain_vec, offsets, valid_mask):
    return valid_mask * jax.nn.gelu(linear * gain_vec + offsets)


def tap_piece(feature, scale_vec):
    return (
        feature * lax.rsqrt(jnp.mean(feature * feature, axis=-1, keepdims=True) + 1e-05) * scale_vec
    )


def general(
    inputs,
    heights,
    widths,
    conv_weights,
    affine_scale,
    affine_shift,
    tap_scales,
    head_weights,
    trunk_cot,
    heads_cot,
):
    images, height, breadth, channels = inputs.shape
    layer_count = conv_weights.shape[0]
    row_ids = jnp.arange(height, dtype=jnp.int32)
    col_ids = jnp.arange(breadth, dtype=jnp.int32)
    valid = (row_ids[None, :, None] < heights[:, None, None]) & (
        col_ids[None, None, :] < widths[:, None, None]
    )
    valid_mask = jnp.where(valid, 1.0, 0.0).astype(jnp.float32)[..., None]
    conv_cols, head_cols = (
        lax.all_gather(conv_weights, "dp", axis=2, tiled=True),
        lax.all_gather(head_weights, "dp", axis=2, tiled=True),
    )
    conv_full, head_full, scale_full = (
        lax.all_gather(conv_cols, "fsdp", axis=1, tiled=True),
        lax.all_gather(head_cols, "fsdp", axis=1, tiled=True),
        lax.all_gather(tap_scales, "fsdp", axis=1, tiled=True),
    )
    outputs_wide = head_full.shape[2]
    feature = inputs.astype(jnp.float32) * valid_mask
    squares = [jnp.sum(feature * feature)]
    entering = inputs * valid_mask.astype(jnp.bfloat16)
    kept_in, kept_linear, kept_feature, kept_tap = ([], [], [], [])
    summed = jnp.zeros((images, height, breadth, outputs_wide), jnp.float32)
    for layer_index in range(layer_count):
        stacked = patches(entering)
        linear = jnp.einsum(
            "ghwk,kc->ghwc", stacked, conv_full[layer_index], preferred_element_type=jnp.float32
        )
        feature = activate(linear, affine_scale[layer_index], affine_shift[layer_index], valid_mask)
        tapped = tap_piece(feature, scale_full[layer_index].astype(jnp.float32)).astype(
            jnp.bfloat16
        )
        summed = summed + jnp.einsum(
            "ghwc,co->ghwo", tapped, head_full[layer_index], preferred_element_type=jnp.float32
        )
        kept_in.append(entering)
        kept_linear.append(linear)
        kept_feature.append(feature)
        kept_tap.append(tapped)
        squares.append(jnp.sum(feature * feature))
        entering = feature.astype(jnp.bfloat16)
    squares.append(jnp.sum(summed * summed))
    square_total, pixels = lax.psum((jnp.stack(squares), jnp.sum(valid_mask)), ("dp", "fsdp"))
    divisors = jnp.array([channels] * (layer_count + 1) + [outputs_wide], jnp.float32)
    rms = jnp.sqrt(square_total / (pixels * divisors))
    conv_back, head_back, scale_back = conv_full, head_full, scale_full
    grad_conv = [None] * layer_count
    grad_scale = [None] * layer_count
    grad_head = [None] * layer_count
    grad_feature = trunk_cot.astype(jnp.float32)
    for layer_index in reversed(range(layer_count)):
        grad_head[layer_index] = jnp.einsum(
            "ghwc,ghwo->co", kept_tap[layer_index], heads_cot, preferred_element_type=jnp.float32
        )
        grad_tapped = jnp.einsum(
            "ghwo,co->ghwc", heads_cot, head_back[layer_index], preferred_element_type=jnp.float32
        )
        _, pullback = jax.vjp(
            tap_piece, kept_feature[layer_index], scale_back[layer_index].astype(jnp.float32)
        )
        feature_part, scale_part = pullback(grad_tapped)
        grad_scale[layer_index] = scale_part
        grad_feature = grad_feature + feature_part
        local_act = partial(
            activate,
            gain_vec=affine_scale[layer_index],
            offsets=affine_shift[layer_index],
            valid_mask=valid_mask,
        )
        _, pullback = jax.vjp(local_act, kept_linear[layer_index])
        (grad_linear,) = pullback(grad_feature)
        low_linear = grad_linear.astype(jnp.bfloat16)
        grad_conv[layer_index] = jnp.einsum(
            "ghwk,ghwc->kc",
            patches(kept_in[layer_index]),
            low_linear,
            preferred_element_type=jnp.float32,
        )
        spread = jnp.einsum(
            "ghwc,kc->ghwk", low_linear, conv_back[layer_index], preferred_element_type=jnp.float32
        )
        grad_feature = unpatch(spread, channels)
    input_grad = (grad_feature * valid_mask).astype(jnp.bfloat16)
    stacked_conv = jnp.stack(grad_conv)
    stacked_head = jnp.stack(grad_head)
    stacked_scale = jnp.stack(grad_scale)
    dp_count = lax.axis_size("dp")
    part_conv, part_head, part_scale = (
        lax.psum_scatter(
            stacked_conv.astype(jnp.bfloat16), "fsdp", scatter_dimension=1, tiled=True
        ).astype(jnp.float32),
        lax.psum_scatter(
            stacked_head.astype(jnp.bfloat16), "fsdp", scatter_dimension=1, tiled=True
        ).astype(jnp.float32),
        lax.psum_scatter(
            stacked_scale.astype(jnp.bfloat16), "fsdp", scatter_dimension=1, tiled=True
        ).astype(jnp.float32),
    )
    spread_scale = jnp.broadcast_to(part_scale[:, :, None], part_scale.shape + (dp_count,))
    conv_grad, head_grad, scale_cols = (
        lax.psum_scatter(
            part_conv.astype(jnp.bfloat16), "dp", scatter_dimension=2, tiled=True
        ).astype(jnp.float32),
        lax.psum_scatter(
            part_head.astype(jnp.bfloat16), "dp", scatter_dimension=2, tiled=True
        ).astype(jnp.float32),
        lax.psum_scatter(
            spread_scale.astype(jnp.bfloat16), "dp", scatter_dimension=2, tiled=True
        ).astype(jnp.float32),
    )
    scale_grad = scale_cols[:, :, 0]
    trunk_out = kept_feature[-1].astype(jnp.bfloat16)
    heads_out = summed.astype(jnp.bfloat16)
    return (trunk_out, heads_out, input_grad, conv_grad, scale_grad, head_grad, rms)


def settle(trunk, heads, image, conv, head, scale, rms, *rest):
    trunk_to, heads_to, image_to, conv_to, head_to, scale_to, rms_to = rest[:7]
    at_trunk, at_heads, at_image, at_conv, at_head, wide, come, go = rest[7:]
    moves = [(conv, at_conv, conv_to)]
    for i in range(3):
        rows = pl.ds(224 * i, 224)
        moves.append((heads.at[rows], at_heads.at[rows], heads_to.at[rows]))
    moves += [(trunk, at_trunk, trunk_to), (image, at_image, image_to), (head, at_head, head_to)]
    fetches = [pltpu.make_async_copy(a, b, come.at[i]) for i, (a, b, _) in enumerate(moves)]
    stores = [pltpu.make_async_copy(b, c, go.at[i]) for i, (_, b, c) in enumerate(moves)]
    stores[0] = pltpu.make_async_copy(wide, conv_to, go.at[0])
    for fetch in fetches:
        fetch.start()
    scale_to[...] = scale[...]
    for i in range(5):
        rms_to[i] = rms[i, 0]
    for i, (fetch, store) in enumerate(zip(fetches, stores)):
        fetch.wait()
        if i == 0:
            wide[...] = at_conv[...].astype(F32)
        store.start()
    for store in stores:
        store.wait()


def settled(results):
    hbm = pl.BlockSpec(memory_space=pl.ANY)
    vmem = pl.BlockSpec(memory_space=pltpu.VMEM)
    smem = pl.BlockSpec(memory_space=pltpu.SMEM)
    shapes = [jax.ShapeDtypeStruct(v.shape, v.dtype) for v in results[:6]]
    shapes[3] = jax.ShapeDtypeStruct(results[3].shape, F32)
    shapes.append(jax.ShapeDtypeStruct((5,), F32))
    return pl.pallas_call(
        settle,
        name="settle",
        out_shape=shapes,
        in_specs=[hbm, hbm, hbm, hbm, hbm, vmem, smem],
        out_specs=[hbm, hbm, hbm, hbm, hbm, vmem, smem],
        scratch_shapes=[pltpu.VMEM(v.shape, v.dtype) for v in results[:5]]
        + [
            pltpu.VMEM(results[3].shape, F32),
            pltpu.SemaphoreType.DMA((7,)),
            pltpu.SemaphoreType.DMA((7,)),
        ],
        compiler_params=pltpu.CompilerParams(vmem_limit_bytes=63 * 2**20),
    )(*results)


def fused(
    inputs,
    heights,
    widths,
    conv_weights,
    affine_scale,
    affine_shift,
    tap_scales,
    head_weights,
    trunk_cot,
    heads_cot,
):
    hbm = pl.BlockSpec(memory_space=pl.ANY)
    vmem = pl.BlockSpec(memory_space=pltpu.VMEM)
    smem = pl.BlockSpec(memory_space=pltpu.SMEM)
    dma = pltpu.SemaphoreType.DMA
    ahead, back = len(ROUTES), len(BACK)

    def flat(v):
        return v[0].transpose(1, 0, 2).reshape(PIX, v.shape[3])

    results = pl.pallas_call(
        partial(kernel, ORDER),
        name="conv_block",
        out_shape=(
            jax.ShapeDtypeStruct((PIX, 512), BF),
            jax.ShapeDtypeStruct((PIX, 1792), BF),
            jax.ShapeDtypeStruct((PIX, 512), BF),
            jax.ShapeDtypeStruct((3, 576, 128), BF),
            jax.ShapeDtypeStruct((3, 64, 448), F32),
            jax.ShapeDtypeStruct((3, 64), F32),
            jax.ShapeDtypeStruct((8, 128), F32),
        ),
        in_specs=[hbm, vmem, vmem, vmem, vmem, smem, smem, hbm, hbm, hbm],
        out_specs=(hbm, hbm, hbm, hbm, vmem, vmem, vmem),
        scratch_shapes=[
            pltpu.VMEM((ROWS, 128), BF),
            pltpu.VMEM((3, 4, 832, 128), BF),
            pltpu.VMEM((3, 512, PAD), BF),
            pltpu.VMEM((3, 512, PAD), BF),
            pltpu.VMEM((2, 6 * 512, 128), BF),
            pltpu.VMEM((3, PIX, 512), BF),
            pltpu.VMEM((3, PIX, 512), BF),
            pltpu.VMEM((3, PIX, 512), BF),
            pltpu.VMEM((PIX, 128), F32),
            pltpu.VMEM((14, PAD, 128), BF),
            pltpu.VMEM((2, 4, PAD, 128), BF),
            pltpu.VMEM((16 + PAD, 512), F32),
            pltpu.VMEM((2, 3, 2, 832, 128), BF),
            pltpu.VMEM((16 * CONV_UNIT, 128), BF),
            pltpu.VMEM((3 * 16 * HEAD_UNIT, 128), BF),
            pltpu.VMEM((LAND[-1], 128), BF),
            pltpu.VMEM((3, 256, 128), BF),
            pltpu.VMEM((3, 2, 8, 64, 128), BF),
            pltpu.VMEM((PIX, 512), F32),
            pltpu.VMEM((8, 512), F32),
            pltpu.VMEM((3, 8, 128), F32),
            pltpu.VMEM((3, 8, 128), F32),
            pltpu.VMEM((4, 8, 128), F32),
            pltpu.VMEM((2, 64, 128), F32),
            pltpu.VMEM((2, 64, 128), F32),
            dma((ahead, 1 + max(PAIR[k] for _, _, _, k in ROUTES))),
            dma((6, 3)),
            dma((3,)),
            dma((back, 12)),
            dma((6, 3)),
            dma((14,)),
            dma((14,)),
            dma((5,)),
            dma((5,)),
            dma((9,)),
            dma((13,)),
        ],
        compiler_params=pltpu.CompilerParams(
            collective_id=0, has_side_effects=True, vmem_limit_bytes=64 * 2**20
        ),
        cost_estimate=pl.CostEstimate(
            flops=45_000_000_000, bytes_accessed=16_000_000, transcendentals=1_200_000
        ),
    )(
        conv_weights,
        head_weights,
        tap_scales,
        affine_scale,
        affine_shift,
        heights,
        widths,
        flat(inputs),
        flat(trunk_cot),
        flat(heads_cot),
    )
    trunk, heads, image, conv_grad, head_grad, scale_grad, rms = settled(results)

    def image_of(v):
        return v.reshape(28, HIGH, v.shape[1]).transpose(1, 0, 2)[None]

    return (
        image_of(trunk),
        image_of(heads),
        image_of(image),
        conv_grad,
        scale_grad,
        head_grad,
        rms,
    )


def solution(mesh):
    in_specs = (
        P(("dp", "fsdp"), None, None, None),
        P(("dp", "fsdp")),
        P(("dp", "fsdp")),
        P(None, "fsdp", "dp"),
        P(),
        P(),
        P(None, "fsdp"),
        P(None, "fsdp", "dp"),
        P(("dp", "fsdp"), None, None, None),
        P(("dp", "fsdp"), None, None, None),
    )
    out_specs = (
        P(("dp", "fsdp"), None, None, None),
        P(("dp", "fsdp"), None, None, None),
        P(("dp", "fsdp"), None, None, None),
        P(None, "fsdp", "dp"),
        P(None, "fsdp"),
        P(None, "fsdp", "dp"),
        P(),
    )
    body = fused if dict(mesh.shape) == {"dp": 4, "fsdp": 8} else general
    return jax.shard_map(body, mesh=mesh, in_specs=in_specs, out_specs=out_specs, check_vma=False)
```

```python
from functools import partial

import jax
import jax.numpy as jnp
from jax import lax
from jax.experimental import pallas as pl
from jax.experimental.pallas import tpu as pltpu
from jax.sharding import PartitionSpec as P

MESH = pl.DeviceIdType.MESH
F32, BF = jnp.float32, jnp.bfloat16

CONV_UNIT, HEAD_UNIT = 576, 224
UNITS = (CONV_UNIT,) * 3 + (HEAD_UNIT,) * 3
BASES = tuple(32 * sum(UNITS[:p]) for p in range(6))
ROWS = 32 * sum(UNITS)
ROUTES = (
    (0, 0, 256, 0),
    (0, 256, 160, 1),
    (0, 416, 160, 2),
    (1, 0, 256, 0),
    (1, 256, 160, 1),
    (1, 416, 160, 2),
    (2, 0, 192, 0),
    (2, 192, 192, 1),
    (2, 384, 192, 2),
    (3, 0, 224, 0),
    (4, 0, 224, 1),
    (5, 0, 224, 2),
)
BACK = (
    (0, 0, 192, 0),
    (0, 192, 192, 1),
    (0, 384, 192, 2),
    (1, 0, 192, 0),
    (1, 192, 192, 1),
    (1, 384, 192, 2),
    (2, 0, 192, 0),
    (2, 192, 192, 1),
    (2, 384, 192, 2),
    (3, 0, 224, 0),
    (4, 0, 224, 1),
    (5, 0, 224, 2),
)
SLOTS = (17, 19, 19, 23, 23)
PAIR = (16, 17, 17, 19, 19)
LAND = tuple(sum(SLOTS[k] * m for _, _, m, k in BACK[:r]) for r in range(len(BACK) + 1))
HIGH, PIX, PAD = 24, 672, 768
ORDER = (
    ("start",),
    ("ld", 0),
    ("e0", 0),
    ("e0", 2),
    ("ld", 1),
    ("ld", 2),
    ("e0", 1),
    ("e0", 4),
    ("e0", 5),
    ("prep_heads",),
    ("zj", 0, 1),
    ("f1", 2),
    ("f1", 1),
    ("f1", 4),
    ("zj", 0, 2),
    ("zj", 2, 1, 1),
    ("yd", 0, 0),
    ("zj", 1, 1, 0),
    ("zj", 0, 3),
    ("e0", 3),
    ("lj", 2, 0),
    ("lj", 1, 0),
    ("zj", 1, 2, 0),
    ("prep_in",),
    ("yd", 0, 1),
    ("zj", 1, 1, 1),
    ("zj", 1, 2, 1),
    ("f1", 5),
    ("xd", 0, 0),
    ("xd", 0, 1),
    ("zj", 1, 3, 0),
    ("zj", 2, 1, 0),
    ("ft", 0),
    ("prep_cot",),
    ("yd", 0, 2),
    ("xd", 0, 2),
    ("xd", 0, 3),
    ("zj", 1, 3, 1),
    ("e0", 7),
    ("zj", 2, 2, 0),
    ("zj", 2, 2, 1),
    ("zj", 2, 3, 1),
    ("yd", 0, 3),
    ("zj", 2, 3, 0),
    ("zj", 3, 1),
    ("zj", 4, 1, 0),
    ("e0", 8),
    ("zj", 5, 1, 0),
    ("yf", 0, 0),
    ("zj", 3, 2),
    ("zj", 3, 3),
    ("xf", 0, 0),
    ("lj", 1, 1),
    ("yd", 3, 0),
    ("zj", 5, 2, 0),
    ("e0", 6),
    ("zj", 4, 1, 1),
    ("lj", 1, 2),
    ("lj", 2, 1),
    ("lj", 2, 2),
    ("xd", 3, 0),
    ("lj", 1, 3),
    ("f1", 7),
    ("yf", 0, 1),
    ("xf", 0, 1),
    ("lj", 2, 3),
    ("yd", 3, 1),
    ("pw", 0),
    ("xd", 3, 1),
    ("pw", 2),
    ("pw", 1),
    ("zj", 4, 2, 1),
    ("zj", 5, 1, 1),
    ("conv", 0, 0),
    ("zj", 4, 2, 0),
    ("conv", 0, 1),
    ("zj", 5, 2, 1),
    ("lj", 4, 0),
    ("conv", 0, 2),
    ("zj", 5, 3, 0),
    ("zj", 5, 3, 1),
    ("yd", 3, 2),
    ("zj", 4, 3, 0),
    ("f1", 8),
    ("act", 0),
    ("yd", 3, 3),
    ("zj", 4, 3, 1),
    ("xd", 3, 2),
    ("yd", 6, 0),
    ("xd", 3, 3),
    ("zj", 6, 1),
    ("zj", 7, 1, 1),
    ("lj", 5, 0),
    ("nt", 0),
    ("yf", 3, 0),
    ("zj", 7, 1, 0),
    ("zj", 6, 2),
    ("lj", 5, 1),
    ("ft", 1),
    ("lj", 4, 1),
    ("zj", 7, 2, 1),
    ("lj", 5, 2),
    ("lj", 5, 3),
    ("zj", 6, 3),
    ("zj", 8, 1, 0),
    ("lj", 7, 0),
    ("xf", 3, 0),
    ("e0", 10),
    ("lj", 4, 2),
    ("xd", 6, 0),
    ("lj", 4, 3),
    ("head_grads", 0, 0),
    ("xf", 3, 1),
    ("yf", 3, 1),
    ("zj", 7, 2, 0),
    ("zj", 8, 1, 1),
    ("head_grads", 0, 1),
    ("pw", 4),
    ("e0", 9),
    ("xd", 6, 1),
    ("zj", 8, 2, 0),
    ("pw", 5),
    ("pw", 3),
    ("lj", 8, 0),
    ("conv", 1, 0),
    ("zj", 8, 2, 1),
    ("conv", 1, 1),
    ("zj", 7, 3, 1),
    ("zj", 7, 3, 0),
    ("yd", 6, 1),
    ("xd", 6, 2),
    ("conv", 1, 2),
    ("yd", 6, 2),
    ("yd", 6, 3),
    ("act", 1),
    ("nt", 1),
    ("lj", 8, 1),
    ("xd", 6, 3),
    ("zj", 8, 3, 0),
    ("zj", 8, 3, 1),
    ("zj", 9, 1),
    ("lj", 7, 1),
    ("e0", 11),
    ("lj", 8, 2),
    ("f1", 10),
    ("ft", 2),
    ("xf", 6, 0),
    ("head_grads", 1, 0),
    ("lj", 7, 2),
    ("zj", 9, 2),
    ("yf", 6, 0),
    ("lj", 7, 3),
    ("zj", 9, 3),
    ("lj", 8, 3),
    ("yf", 6, 1),
    ("xf", 6, 1),
    ("xd", 9, 0),
    ("zj", 10, 1, 0),
    ("head_grads", 1, 1),
    ("pw", 7),
    ("xd", 9, 1),
    ("yd", 9, 0),
    ("yd", 9, 1),
    ("pw", 8),
    ("pw", 6),
    ("conv", 2, 0),
    ("conv", 2, 1),
    ("f1", 11),
    ("xd", 9, 2),
    ("xd", 9, 3),
    ("yd", 9, 2),
    ("conv", 2, 2),
    ("yd", 9, 3),
    ("zj", 10, 1, 1),
    ("s1", 11),
    ("zj", 10, 2, 0),
    ("xf", 9, 0),
    ("zj", 11, 1, 0),
    ("act", 2),
    ("lj", 11, 0),
    ("yf", 9, 0),
    ("zj", 10, 2, 1),
    ("xf", 9, 1),
    ("s1", 10),
    ("yf", 9, 1),
    ("nt", 2),
    ("trunk_cot",),
    ("lj", 10, 0),
    ("zj", 11, 2, 0),
    ("pw", 9),
    ("unpack", 2),
    ("dtap", 2),
    ("lj", 10, 1),
    ("zj", 10, 3, 1),
    ("dlinear", 2),
    ("head_grads", 2, 0),
    ("zj", 10, 3, 0),
    ("head_grads", 2, 1),
    ("conv_back", 2, 0),
    ("s2", 10, 0),
    ("s2", 11, 0),
    ("s1", 9),
    ("conv_back", 2, 1),
    ("lj", 10, 2),
    ("zj", 11, 1, 1),
    ("conv_grads", 2, 0),
    ("zj", 11, 2, 1),
    ("s2", 11, 1),
    ("conv_grads", 2, 1),
    ("conv_grads", 2, 2),
    ("s2", 10, 1),
    ("s1", 7),
    ("lj", 10, 3),
    ("s1", 8),
    ("zj", 11, 3, 1),
    ("conv_back", 2, 2),
    ("zj", 11, 3, 0),
    ("pw", 10),
    ("unpack", 1),
    ("dtap", 1),
    ("dlinear", 1),
    ("s1", 6),
    ("s2", 8, 0),
    ("conv_back", 1, 0),
    ("zd", 10, 0),
    ("s2", 7, 0),
    ("conv_back", 1, 1),
    ("lj", 11, 1),
    ("s2b", 9),
    ("s3a", 9),
    ("zd", 11, 0),
    ("zd", 11, 1),
    ("lj", 11, 2),
    ("conv_grads", 1, 0),
    ("s2", 7, 1),
    ("s2a", 9),
    ("conv_grads", 1, 1),
    ("lj", 11, 3),
    ("conv_grads", 1, 2),
    ("s1", 4),
    ("pw", 11),
    ("s2", 8, 1),
    ("zd", 8, 0),
    ("conv_back", 1, 2),
    ("unpack", 0),
    ("s1", 5),
    ("zd", 7, 0),
    ("zd", 10, 1),
    ("zu", 7, 3),
    ("s3b", 9),
    ("dtap", 0),
    ("s2b", 6),
    ("zu", 8, 3),
    ("dlinear", 0),
    ("zd", 8, 1),
    ("s2", 4, 0),
    ("s2a", 6),
    ("zd", 7, 1),
    ("zu", 10, 3),
    ("s3a", 6),
    ("s2", 5, 0),
    ("s1", 3),
    ("conv_back", 0, 0),
    ("s2", 4, 1),
    ("zu", 11, 3),
    ("conv_grads", 0, 0),
    ("s2", 5, 1),
    ("zu", 9, 3),
    ("conv_grads", 0, 1),
    ("zu", 4, 3),
    ("conv_grads", 0, 2),
    ("s1", 2),
    ("s1", 1),
    ("zu", 5, 3),
    ("zu", 7, 2),
    ("zu", 10, 2),
    ("zu", 8, 2),
    ("zu", 11, 2),
    ("zu", 4, 2),
    ("zu", 5, 2),
    ("zd", 5, 0),
    ("s1", 0),
    ("joined", 0),
    ("s3b", 6),
    ("zd", 4, 0),
    ("joined", 1),
    ("zd", 6, 0),
    ("zu", 9, 2),
    ("zf", 7),
    ("m0",),
    ("s2", 2, 0),
    ("zd", 9, 0),
    ("zf", 10),
    ("s2", 1, 0),
    ("zf", 8),
    ("s2a", 3),
    ("zd", 2, 0),
    ("s3a", 3),
    ("conv_back", 0, 1),
    ("zf", 11),
    ("zd", 1, 0),
    ("m1", 0),
    ("s2b", 3),
    ("zd", 9, 1),
    ("zd", 5, 1),
    ("zd", 4, 1),
    ("zu", 6, 3),
    ("s2", 2, 1),
    ("s2", 1, 1),
    ("zd", 6, 1),
    ("s2b", 0),
    ("zd", 2, 1),
    ("zd", 1, 1),
    ("zu", 2, 3),
    ("s2a", 0),
    ("conv_back", 0, 2),
    ("zf", 5),
    ("ff", 10),
    ("zu", 1, 3),
    ("ff", 7),
    ("pf", 4),
    ("zu", 6, 2),
    ("s3a", 0),
    ("m1", 1),
    ("zf", 9),
    ("s3b", 3),
    ("pf", 3),
    ("ff", 11),
    ("pf", 5),
    ("zf", 4),
    ("zu", 3, 3),
    ("s3b", 0),
    ("t0",),
    ("zu", 0, 3),
    ("zu", 2, 2),
    ("m1", 2),
    ("zu", 1, 2),
    ("zu", 3, 2),
    ("zd", 3, 0),
    ("m2", 1),
    ("image_grad",),
    ("zu", 0, 2),
    ("zf", 6),
    ("t1",),
    ("zd", 0, 0),
    ("zf", 2),
    ("zd", 3, 1),
    ("ff", 4),
    ("ff", 5),
    ("zf", 1),
    ("zd", 0, 1),
    ("ff", 8),
    ("m2", 2),
    ("pf", 2),
    ("m2", 3),
    ("zf", 3),
    ("pf", 1),
    ("m3",),
    ("zf", 0),
    ("ff", 2),
    ("ff", 1),
    ("pf", 0),
    ("t2",),
    ("finish",),
)


def kernel(
    order,
    conv_in,
    head_in,
    tap_in,
    gain_in,
    offset_in,
    height_in,
    width_in,
    image_in,
    trunk_in,
    cot_in,
    trunk_out,
    heads_out,
    image_out,
    conv_out,
    head_out,
    scale_out,
    rms_out,
    W,
    F3,
    FT,
    FTP,
    NTP,
    N,
    GP,
    DT,
    RN,
    COT,
    COTP,
    ACC,
    D3P,
    GC2,
    GH,
    RL,
    RAW,
    HB,
    SQ,
    LB,
    MR,
    ZB,
    SB,
    SR,
    ag_recv,
    ag_send,
    load_sem,
    rs_recv,
    rs_send,
    pair_recv,
    pair_send,
    in_sem,
    out_sem,
    small_recv,
    small_send,
):
    dpi, fsi = lax.axis_index("dp"), lax.axis_index("fsdp")
    y, c, z, x = dpi // 2, dpi % 2, fsi // 2, fsi % 2

    def dev(yy, cc, zz, xx):
        return (yy * 2 + cc, zz * 2 + xx)

    xn, yn, pn = dev(y, c, z, 1 - x), dev(1 - y, c, z, x), dev(y, 1 - c, z, x)
    up, dn = dev(y, c, jnp.minimum(z + 1, 3), x), dev(y, c, jnp.maximum(z - 1, 0), x)
    sig = [z, z + 1 - 2 * (z % 2), jnp.where(z < 2, 2, 1), jnp.where(z < 2, 3, 0)]
    height, width = height_in[0], width_in[0]

    def when(cond, fn):
        pl.when(cond)(fn)

    def remote(src, dst, send, recv, t):
        return pltpu.make_async_remote_copy(
            src_ref=src, dst_ref=dst, send_sem=send, recv_sem=recv, device_id=t, device_id_type=MESH
        )

    def row(p, yy, cc, s, xx, off=0):
        return pl.multiple_of(BASES[p] + ((2 * yy + cc) * 8 + 2 * s + xx) * UNITS[p] + off, 32)

    def x_first(kind):
        return kind not in (2, 4)

    def shard(r, first, s, last):
        p, off, _, kind = ROUTES[r]
        yy, xx = (last, first) if x_first(kind) else (first, last)
        return row(p, yy, c, s, xx, off)

    def ends(r, routes=ROUTES):
        return (x, y, xn, yn) if x_first(routes[r][3]) else (y, x, yn, xn)

    def place(r, line):
        first, last, _, _ = ends(r)
        return (1 - first if line % 2 else first), (1 - last if line // 2 else last)

    def ag(r, at, si, ri, t, n=1):
        part = W.at[pl.ds(at, ROUTES[r][2] * n)]
        return remote(part, part, ag_send.at[ROUTES[r][0], si], ag_recv.at[r, ri], t)

    def ag_start(r, at, si, ri, t, own=False):
        copy = ag(r, at, si, ri, t)
        p, off, m, _ = ROUTES[r]
        if own and p < 3:
            copy = remote(
                conv_in.at[p, pl.ds(off, m)],
                W.at[pl.ds(at, m)],
                ag_send.at[p, si],
                ag_recv.at[r, ri],
                t,
            )
        copy.start()

    def ag_wait(r, ri, n=1):
        ag(r, BASES[ROUTES[r][0]], 0, ri, xn, n).wait_recv()

    def pair(r, at, own=False):
        ag_start(r, at, 0, PAIR[ROUTES[r][3]], pn, own)

    def load(p):
        return pltpu.make_async_copy(
            conv_in.at[p], W.at[pl.ds(row(p, y, c, z, x), CONV_UNIT)], load_sem.at[p]
        )

    def ld(p):
        load(p).wait()

    def along(r, s, at, line, passed=True):
        climbs = (s < z) & (z < 3) if passed else z < 3
        sinks = (s > z) & (z > 0) if passed else z > 0
        when(climbs, lambda: ag_start(r, at, 1, 4 * line + s, up, not passed and line == 0))
        when(sinks, lambda: ag_start(r, at, 2, 4 * line + s, dn, not passed and line == 0))

    def fan(r, s, at, line, own=False):
        kind = ROUTES[r][3]
        if kind == 0:
            ag_start(r, at, 0, 4 + s, xn, own)
            ag_start(r, at, 0, 8 + s, yn, own)
        elif kind < 3:
            ag_start(r, at, 0, 8 + 4 * line + s, ends(r)[3], own)
        pair(r, at, own)

    def e0(r):
        first, last, fn, ln = ends(r)
        at = shard(r, first, z, last)
        if ROUTES[r][3]:
            ag_start(r, at, 0, 16, fn, True)
        if ROUTES[r][3] > 2:
            ag_start(r, at, 0, 17, ln, True)
        along(r, z, at, 0, False)
        fan(r, z, at, 0, True)

    def f1(r):
        first, last, _, ln = ends(r)
        at = shard(r, 1 - first, z, last)
        ag_wait(r, 16)
        if ROUTES[r][3] > 2:
            ag_start(r, at, 0, 18, ln)
        along(r, z, at, 1, False)
        fan(r, z, at, 1)

    def g1(r, i):
        f, l = place(r, 2 + i)
        at = shard(r, f, z, l)
        ag_wait(r, 17 + i)
        along(r, z, at, 2 + i, False)
        fan(r, z, at, 2 + i)

    def zj(r, j, only=0):
        s = sig[j]
        for line in range(4) if ROUTES[r][3] > 2 else (only,):
            f, l = place(r, line)
            at = shard(r, f, s, l)
            ag_wait(r, 4 * line + s)
            along(r, s, at, line)
            fan(r, s, at, line)

    def lj(r, j):
        first, last, _, _ = ends(r)
        s = sig[j]
        for line in range(2):
            ag_wait(r, 8 + 4 * line + s)
            pair(r, shard(r, place(r, line)[0], s, 1 - last))

    def xd(r, j):
        s = sig[j]
        at = shard(r, 1 - x, s, y)
        ag_wait(r, 4 + s)
        when(s % 2 == 0, lambda: ag_start(r, at, 0, 12 + s, yn))
        pair(r, at)

    def yd(r, j):
        s = sig[j]
        at = shard(r, x, s, 1 - y)
        ag_wait(r, 8 + s)
        when(s % 2 == 1, lambda: ag_start(r, at, 0, 12 + s, xn))
        pair(r, at)

    def yf(r, k):
        s = jnp.where(z < 2, 2 * k, 2 - 2 * k)
        ag_wait(r, 12 + s)
        pair(r, shard(r, 1 - x, s, 1 - y))

    def xf(r, k):
        s = jnp.where(z < 2, 1 + 2 * k, 3 - 2 * k)
        ag_wait(r, 12 + s)
        pair(r, shard(r, 1 - x, s, 1 - y))

    def pw(r):
        ag_wait(r, PAIR[ROUTES[r][3]], 16)

    def sent(copy_of, sems, main, line, climbs, sinks):
        copy_of(main, sems.at[0]).wait_send()
        for k in range(4):
            if climbs(k):
                when(z == k, lambda: copy_of(line * climbs(k), sems.at[1]).wait_send())
            if sinks(k):
                when(z == k, lambda: copy_of(line * sinks(k), sems.at[2]).wait_send())

    def ag_end(p):
        mine = [(m, kind) for q, _, m, kind in ROUTES if q == p]

        def copy_of(rows, sem):
            return remote(W.at[pl.ds(0, rows)], W.at[pl.ds(0, rows)], sem, ag_recv.at[0, 0], xn)

        sent(
            copy_of,
            ag_send.at[p],
            sum(m * (28, 25, 25, 19, 19)[kind] for m, kind in mine),
            sum(m * (1, 2, 2, 4, 4)[kind] for m, kind in mine),
            lambda k: k + 1 if k < 3 else 0,
            lambda k: 4 - k if k > 0 else 0,
        )

    def grads(p):
        if p == 2:
            return GC2, 0
        if p < 2:
            return W, BASES[2] + (1 - p) * 16 * CONV_UNIT
        return GH, (p - 3) * 16 * HEAD_UNIT

    def grow(r, first, s, last):
        p, off, _, kind = BACK[r]
        yy, xx = (last, first) if x_first(kind) else (first, last)
        return pl.multiple_of(grads(p)[1] + (yy * 8 + 2 * s + xx) * UNITS[p] + off, 32)

    def slot(r, k):
        return pl.multiple_of(LAND[r] + k * BACK[r][2], 32)

    def rs(r, at, k, si, ri, t, n=1):
        m = BACK[r][2] * n
        return remote(
            grads(BACK[r][0])[0].at[pl.ds(at, m)],
            RL.at[pl.ds(slot(r, k), m)],
            rs_send.at[BACK[r][0], si],
            rs_recv.at[r, ri],
            t,
        )

    def rs_start(r, at, k, i, t):
        rs(r, at, k, 0 if i < 6 else 1 if i < 9 else 2, i, t).start()

    def rs_wait(r, ri, n=1):
        rs(r, grads(BACK[r][0])[1], 0, 0, ri, xn, n).wait_recv()

    def add(r, at, *ks):
        ref, rows = grads(BACK[r][0])[0], pl.ds(at, BACK[r][2])
        total = ref[rows, :].astype(F32)
        for k in ks:
            total = total + RL[pl.ds(slot(r, k), BACK[r][2]), :].astype(F32)
        ref[rows, :] = total.astype(BF)

    def s1(r):
        if BACK[r][3] == 0:
            for s in (0, 2):
                rs_start(r, grow(r, 1 - x, s, 1 - y), s // 2, 0, yn)
            for s in (1, 3):
                rs_start(r, grow(r, 1 - x, s, 1 - y), 2 + s // 2, 1, xn)
            for s in (1, 3):
                rs_start(r, grow(r, 1 - x, s, y), 4 + s, 2, xn)
            for s in (0, 2):
                rs_start(r, grow(r, x, s, 1 - y), 8 + s, 4, yn)
            return
        if BACK[r][3] > 2:
            far(r)
            return
        _, last, _, ln = ends(r, BACK)
        for i, group in enumerate(((0, 3), (1, 2))):
            for s in group:
                for f in range(2):
                    rs_start(r, grow(r, f, s, 1 - last), 2 * s + f, i, ln)

    def s2a(r):
        rs_wait(r, 0, 2)
        for s in (0, 2):
            at = grow(r, 1 - x, s, y)
            add(r, at, s // 2)
            rs_start(r, at, 4 + s, 3, xn)

    def s2b(r):
        rs_wait(r, 1, 2)
        for s in (1, 3):
            at = grow(r, x, s, 1 - y)
            add(r, at, 2 + s // 2)
            rs_start(r, at, 8 + s, 5, yn)

    def s3a(r):
        rs_wait(r, 2, 2)
        rs_wait(r, 4, 2)
        for s in range(4):
            add(r, grow(r, x, s, y), 4 + s if s % 2 else 8 + s)

    def line_of(r):
        kind, last = BACK[r][3], ends(r, BACK)[1]
        if kind == 0:
            return ((x, y),), 12, 1
        if kind < 3:
            return ((0, last), (1, last)), 8, 2
        return ((0, 0), (1, 0), (0, 1), (1, 1)), 0, 4

    def rs_up(r, t):
        places, base, n = line_of(r)
        for i, (f, l) in enumerate(places):
            rs_start(r, grow(r, f, t, l), base + n * t + i, 5 + t, up)

    def rs_down(r, t):
        places, base, n = line_of(r)
        for i, (f, l) in enumerate(places):
            k = jnp.where(t == z - 1, 4, t)
            rs_start(r, grow(r, f, t, l), base + n * k + i, 9 + t, dn)

    def far(r):
        @pl.when(z == 0)
        def _():
            for t in (3, 2, 1):
                rs_up(r, t)

        @pl.when(z == 3)
        def _():
            for t in (0, 1, 2):
                rs_down(r, t)

    def s3b(r):
        rs_wait(r, 3, 2)
        rs_wait(r, 5, 2)
        for s in range(4):
            add(r, grow(r, x, s, y), 8 + s if s % 2 else 4 + s)
        far(r)

    def s2(r, i):
        rs_wait(r, i, 4)
        for s in ((0, 3), (1, 2))[i]:
            for f in range(2):
                add(r, grow(r, f, s, ends(r, BACK)[1]), 2 * s + f)

        @pl.when(z == 0)
        def _():
            for t in ((3,), (2, 1))[i]:
                rs_up(r, t)

        @pl.when(z == 3)
        def _():
            for t in ((0,), (1, 2))[i]:
                rs_down(r, t)

    def zu(r, t):
        @pl.when((z > 0) & (z < t))
        def _():
            places, base, n = line_of(r)
            rs_wait(r, 5 + t, n)
            for i, (f, l) in enumerate(places):
                add(r, grow(r, f, t, l), base + n * t + i)
            rs_up(r, t)

    def zd(r, t):
        @pl.when((z < 3) & (z > t))
        def _():
            places, base, n = line_of(r)
            rs_wait(r, 9 + t, n)
            for i, (f, l) in enumerate(places):
                add(r, grow(r, f, t, l), base + n * t + i)
            rs_down(r, t)

    def zf(r):
        places, base, n = line_of(r)
        first, last, fn, ln = ends(r, BACK)
        when(z > 0, lambda: rs_wait(r, 5 + z, n))
        when(z < 3, lambda: rs_wait(r, 9 + z, n))

        def both(*ks):
            for i, (f, l) in enumerate(places):
                add(r, grow(r, f, z, l), *[base + n * k + i for k in ks])

        when(z == 0, lambda: both(4))
        when(z == 3, lambda: both(3))
        when((z > 0) & (z < 3), lambda: both(z, 4))
        if n == 2:
            rs_start(r, grow(r, 1 - first, z, last), 18, 2, fn)
        if n == 4:
            for f in range(2):
                rs_start(r, grow(r, f, z, 1 - last), 20 + f, 0, ln)

    def gg(r):
        first, last, fn, _ = ends(r, BACK)
        rs_wait(r, 0, 2)
        for f in range(2):
            add(r, grow(r, f, z, last), 20 + f)
        rs_start(r, grow(r, 1 - first, z, last), 22, 2, fn)

    def ff(r):
        first, last, _, _ = ends(r, BACK)
        rs_wait(r, 2)
        add(r, grow(r, first, z, last), 22 if BACK[r][3] > 2 else 18)

    def conv_store(p):
        ref, base = grads(p)
        at = pl.multiple_of(base + (y * 8 + 2 * z + x) * CONV_UNIT, 32)
        return pltpu.make_async_copy(ref.at[pl.ds(at, CONV_UNIT)], conv_out.at[p], out_sem.at[p])

    def diagonal():
        shape = (64, 64)
        return lax.broadcasted_iota(jnp.int32, shape, 0) == lax.broadcasted_iota(jnp.int32, shape, 1)

    def tap_column(layer):
        wide = jnp.broadcast_to(tap_in[layer : layer + 1, :].astype(F32), (64, 64))
        return jnp.sum(jnp.where(diagonal(), wide, 0.0), axis=1, keepdims=True)

    def left_lanes(count):
        return lax.broadcasted_iota(jnp.int32, (count, 128), 1) < 64

    def unfold(v, upper):
        turned = pltpu.roll(v, 64, 1)
        return jnp.concatenate([jnp.where(upper, v, 0.0), jnp.where(upper, turned, 0.0)], axis=0)

    def pf(p):
        if p < 3:
            conv_store(p).start()
            return
        layer = 5 - p
        base = pl.multiple_of(grads(p)[1] + (y * 8 + 2 * z + x) * HEAD_UNIT, 32)
        full = [GH[pl.ds(base + 64 * t, 64), :].astype(F32) for t in range(3)]
        half = unfold(GH[pl.ds(base + 192, 32), :].astype(F32), (left_lanes(32) == (c == 0)))
        tiles = [jnp.where(c == 0, a, b) for a, b in zip(full + [half], [half] + full)]
        total = jnp.zeros((64, 1), F32)
        for t in range(4):
            raw = RAW[layer, 64 * t : 64 * t + 64, :].astype(F32)
            total = total + jnp.sum(tiles[t] * raw, axis=1, keepdims=True)
        SB[0, :, layer : layer + 1] = total
        tap = tap_column(layer)
        tiles = [v * tap for v in tiles]
        rolled = [pltpu.roll(v, 64, 1) for v in tiles]
        left = left_lanes(64)
        for t in range(4):
            later = rolled[t + 1] if t < 3 else rolled[t]
            v = jnp.where(c == 0, tiles[t], jnp.where(left, rolled[t], later))
            if t < 3:
                head_out[layer, :, 128 * t : 128 * t + 128] = v
            else:
                head_out[layer, :, 384:448] = v[:, 0:64]

    def rs_end(p):
        mine = [(m, kind) for q, _, m, kind in BACK if q == p]
        ref, base = grads(p)

        def copy_of(rows, sem):
            return remote(ref.at[pl.ds(base, rows)], RL.at[pl.ds(0, rows)], sem, rs_recv.at[0, 0], xn)

        sent(
            copy_of,
            rs_send.at[p],
            sum(m * (12, 9, 9, 3, 3)[kind] for m, kind in mine),
            sum(m * (1, 2, 2, 4, 4)[kind] for m, kind in mine),
            lambda k: 3 - k,
            lambda k: k,
        )

    def share_ft(layer):
        return remote(FT.at[layer], FTP.at[layer], pair_send.at[layer], pair_recv.at[layer], pn)

    def share_nt(layer):
        i = 3 + layer
        src = GC2.at[pl.ds(0, 6 * 512)]
        return remote(src, NTP.at[layer % 2], pair_send.at[i], pair_recv.at[i], pn)

    def share_cot(k):
        src = COT.at[pl.ds(7 * k + 3 * (1 - c), 4)]
        return remote(src, COTP.at[k], pair_send.at[6 + k], pair_recv.at[6 + k], pn)

    def share_d(layer, k):
        i = 8 + 2 * layer + k
        src = F3.at[:, 2 * k + 1 - c]
        return remote(src, D3P.at[layer % 2, :, k], pair_send.at[i], pair_recv.at[i], pn)

    def blocks(count, fn):
        def step(m, carry):
            fn(m)
            return carry

        lax.fori_loop(0, count, step, 0)

    one_time = jnp.where(dpi >= 0, 1, 2)

    def apart(fn):
        def wrapped(*args):
            def step(m, carry):
                fn(*args)
                return carry

            lax.fori_loop(0, one_time, step, 0)

        return wrapped

    def at48(m, base=0):
        return pl.ds(pl.multiple_of(base + 48 * m, 8 if base == 8 else 16), 48)

    def place48():
        i = lax.broadcasted_iota(jnp.int32, (48, 1), 0)
        second = i >= HIGH
        return jnp.where(second, i - HIGH, i), jnp.where(second, 1, 0)

    def mask_of(m):
        r, second = place48()
        return jnp.where((r < height) & (2 * m + second < width), 1.0, 0.0).astype(F32)

    def image_part(i):
        src = (image_in, trunk_in)[i // 4].at[:, pl.ds(128 * (i % 4), 128)]
        return pltpu.make_async_copy(src, GC2.at[pl.ds(3072 + PIX * i, PIX)], in_sem.at[i // 4])

    def image_wait(i):
        part = GC2.at[pl.ds(3072 + 4 * PIX * i, 4 * PIX)]
        pltpu.make_async_copy(part, part, in_sem.at[i]).wait()

    def cot_part(t):
        return pltpu.make_async_copy(
            cot_in.at[:, pl.ds(128 * t, 128)], COT.at[t, pl.ds(0, PIX)], in_sem.at[2]
        )

    def cot_wait(first, count, sem):
        part = COT.at[pl.ds(first, count), pl.ds(0, PIX)]
        pltpu.make_async_copy(part, part, sem).wait()

    def expand(first, masked):
        def one(m):
            at = at48(m, 8)
            for k in range(4):
                rows = pl.ds(pl.multiple_of(3072 + PIX * (first + k) + 48 * m, 16), 48)
                v = GC2[rows, :].astype(F32)
                if masked:
                    v = v * mask_of(m)
                    SQ[0:1, 128 * k : 128 * k + 128] += jnp.sum(v * v, axis=0, keepdims=True)
                ACC[at, 128 * k : 128 * k + 128] = v

        blocks(14, one)

    def start():
        for p in range(3):
            load(p).start()
        for i in range(8):
            image_part(i).start()
        for t in range(14):
            cot_part(t).start()
        barrier = pltpu.get_barrier_semaphore()
        for t in (xn, yn, pn):
            pl.semaphore_signal(barrier, inc=1, device_id=t, device_id_type=MESH)
        when(
            z < 3, lambda: pl.semaphore_signal(barrier, inc=1, device_id=up, device_id_type=MESH)
        )
        when(
            z > 0, lambda: pl.semaphore_signal(barrier, inc=1, device_id=dn, device_id_type=MESH)
        )
        pl.semaphore_wait(barrier, jnp.where((z == 0) | (z == 3), 4, 5))

    def prep_heads():
        left = left_lanes(64)
        ACC[0:64, :] = jnp.zeros((64, 512), F32)
        for layer in range(3):
            ACC[0:64, 0:448] = head_in[layer].astype(F32)
            tap = tap_column(layer)
            base = row(5 - layer, y, c, z, x)
            tiles = [ACC[0:64, 128 * t : 128 * t + 128] for t in range(4)]
            rolled = [pltpu.roll(v, 64, 1) for v in tiles]
            moved = [
                jnp.where(left, rolled[t - 1] if t else 0.0, rolled[t]) for t in range(4)
            ]
            for t in range(4):
                v = jnp.where(c == 0, tiles[t], moved[t])
                RAW[layer, 64 * t : 64 * t + 64, :] = v.astype(BF)
            for t in range(3):
                v = jnp.where(c == 0, tiles[t], moved[t + 1])
                W[pl.ds(base + 64 * t, 64), :] = (v * tap).astype(BF)
            v = jnp.where(c == 0, tiles[3], moved[0]) * tap
            W[pl.ds(base + 192, 32), :] = (v[0:32] + pltpu.roll(v[32:64], 64, 1)).astype(BF)

    def prep_in():
        ACC[...] = jnp.zeros_like(ACC)
        SQ[...] = jnp.zeros_like(SQ)
        SB[0] = jnp.zeros((64, 128), F32)
        for b in range(3):
            for k in range(4):
                F3[b, k, 0:32, :] = jnp.zeros((32, 128), BF)
                F3[b, k, 704:832, :] = jnp.zeros((128, 128), BF)
        image_wait(0)
        expand(0, True)
        pixels = (height * width).astype(F32) * (1.0 / 512.0)
        SQ[5:6, :] = jnp.full((1, 512), pixels, F32)

    def shifts():
        r, _ = place48()

        def one(m):
            v64 = ACC[pl.ds(pl.multiple_of(48 * m, 8), 64), :]
            for b in range(3):
                v = v64[7 + b : 55 + b, :]
                if b != 1:
                    v = jnp.where(r == (0 if b == 0 else HIGH - 1), 0.0, v)
                v = v.astype(BF)
                for k in range(4):
                    F3[b, k, at48(m, 32), :] = v[:, 128 * k : 128 * k + 128]

        blocks(14, one)

    def ft(layer):
        shifts()

        def one(m):
            v = ACC[pl.ds(pl.multiple_of(8 + 128 * m, 8), 128), :]
            FT[layer, :, pl.ds(pl.multiple_of(128 * m, 128), 128)] = v.T.astype(BF)

        blocks(6, one)
        share_ft(layer).start()

    def prep_cot():
        def clear(t):
            COT[t, PIX:PAD, :] = jnp.zeros((PAD - PIX, 128), BF)

        blocks(14, clear)
        cot_wait(0, 14, in_sem.at[2])
        for k in range(2):
            share_cot(k).start()

    def taps(a, transposed):
        first = 8 + HIGH * a if not transposed else 8 + HIGH * (2 - a)
        order = (0, 1, 2) if not transposed else (2, 1, 0)
        return [
            jnp.concatenate([F3[b, k, first : first + PIX, :] for k in range(4)], axis=1)
            for b in order
        ]

    def weights(layer, a, b):
        first = BASES[layer] + 512 * (3 * b + a)
        return jnp.concatenate(
            [W[first + 4608 * k : first + 4608 * k + 512, :] for k in range(4)], axis=1
        )

    @apart
    def conv(layer, a):
        v = jnp.dot(
            jnp.concatenate(taps(a, False), axis=1),
            jnp.concatenate([weights(layer, a, b) for b in range(3)], axis=0),
            preferred_element_type=F32,
        )
        if a == 0:
            ACC[8 : 8 + PIX, :] = v
        else:
            ACC[8 : 8 + PIX, :] += v

    def act(layer):
        gain, offset = gain_in[layer : layer + 1, :], offset_in[layer : layer + 1, :]
        k = 0.7978845608028654

        def one(m):
            rows, at = at48(m, 8), at48(m)
            u = ACC[rows, :] * gain + offset
            mask = mask_of(m)
            u2 = u * u
            t = jnp.tanh(k * u * (1.0 + 0.044715 * u2))
            half = 0.5 * (1.0 + t) * mask
            f = u * half
            slope = half + (0.5 * k) * mask * u * (1.0 - t * t) * (1.0 + 0.134145 * u2)
            squares = f * f
            rn = lax.rsqrt(jnp.mean(squares, axis=-1, keepdims=True) + 1e-5)
            GP[layer, at, :] = (slope * gain).astype(BF)
            N[layer, at, :] = (f * rn).astype(BF)
            RN[at, layer : layer + 1] = rn
            SQ[layer + 1 : layer + 2, :] += jnp.sum(squares, axis=0, keepdims=True)
            if layer < 2:
                ACC[rows, :] = f
            else:
                v = f.astype(BF)
                for b in range(4):
                    F3[1, b, at48(m, 32), :] = v[:, 128 * b : 128 * b + 128]

        blocks(14, one)
        if layer == 2:
            for b in range(4):
                trunk_store(b).start()

    def trunk_store(b):
        return pltpu.make_async_copy(
            F3.at[1, b, pl.ds(32, PIX)], trunk_out.at[:, pl.ds(128 * b, 128)], out_sem.at[3]
        )

    def nt(layer):
        if layer > 0:
            share_nt(layer - 1).wait_send()

        turn(layer)
        share_nt(layer).start()

    @apart
    def turn(layer):
        for m in range(6):
            v = N[layer, 128 * m : min(128 * m + 128, PIX), :].astype(F32)
            if m == 5:
                v = jnp.concatenate([v, jnp.zeros((PAD - PIX, 512), F32)], axis=0)
            GC2[512 * m : 512 * m + 512, :] = v.T.astype(BF)

    def head_grads(layer, k):
        if k == 0:
            share_nt(layer).wait_recv()
        if layer == 0:
            share_cot(k).wait_recv()
        head_grads_of(layer, k)

    @apart
    def head_grads_of(layer, k):
        mine = [GC2[512 * m : 512 * m + 512, :] for m in range(6)]
        theirs = [NTP[layer % 2, 512 * m : 512 * m + 512, :] for m in range(6)]
        own = [COT[7 * k + 4 * c + i] for i in range(3)] + [COT[7 * k + 3]]
        other = [COTP[k, c + i] for i in range(3)] + [COTP[k, 3 * (1 - c)]]
        v = jnp.dot(
            jnp.concatenate(mine + theirs, axis=1),
            jnp.concatenate(
                [jnp.concatenate(own, axis=1), jnp.concatenate(other, axis=1)], axis=0
            ),
            preferred_element_type=F32,
        )
        base = grads(5 - layer)[1] + k * 8 * HEAD_UNIT
        valid = left_lanes(32) == (c == 0)
        for f in range(8):
            first = base + f * HEAD_UNIT
            for t in range(3):
                part = v[64 * f : 64 * f + 64, 128 * t : 128 * t + 128]
                GH[first + 64 * t : first + 64 * t + 64, :] = part.astype(BF)
            half = v[64 * f : 64 * f + 64, 384:512]
            lower = pltpu.roll(half[32:64], 64, 1)
            GH[first + 192 : first + 224, :] = jnp.where(valid, half[0:32], lower).astype(BF)

    def unpack(layer):
        left = left_lanes(32)

        def one(f):
            for k in range(2):
                base = BASES[5 - layer] + 16 * k * HEAD_UNIT + 192
                low, high = [
                    W[pl.ds(pl.multiple_of(base + (8 * i + f) * HEAD_UNIT, 32), 32), :].astype(F32)
                    for i in range(2)
                ]
                HB[layer, k, f, 0:32, :] = jnp.where(left, low, high).astype(BF)
                v = jnp.where(left, pltpu.roll(low, 64, 1), pltpu.roll(high, 64, 1))
                HB[layer, k, f, 32:64, :] = v.astype(BF)

        blocks(8, one)

    def head_pair(layer, k, low=0, high=7):
        def tile(f, t):
            if t == 3:
                return HB[layer, k, f]
            i, t = (0, t) if t < 3 else (1, t - 4)
            first = BASES[5 - layer] + (16 * k + 8 * i + f) * HEAD_UNIT + 64 * t
            return W[first : first + 64, :]

        return jnp.concatenate(
            [jnp.concatenate([tile(f, t) for f in range(8)], axis=0) for t in range(low, high)], axis=1
        )

    def at224(m):
        return pl.ds(pl.multiple_of(224 * m, 32), 224)

    def dtap(layer):
        def one(m):
            at = at224(m)
            h = jnp.zeros((224, 512), F32)
            for k in range(2):
                left = jnp.concatenate([COT[7 * k + i, at, :] for i in range(7)], axis=1)
                h = h + lax.dot_general(
                    left, head_pair(layer, k), (((1,), (1,)), ((), ())), preferred_element_type=F32
                )
            n = N[layer, at, :].astype(F32)
            mean = jnp.mean(h * n, axis=-1, keepdims=True)
            DT[layer, at, :] = ((h - n * mean) * RN[at, layer : layer + 1]).astype(BF)

        blocks(3, one)

    def joined(k):
        if k == 0:
            for i in range(2):
                share_cot(i).wait_send()
        joined_of(k, 0, 4)
        joined_of(k, 4, 7)
        for i in range(7):
            heads_store(7 * k + i).start()

    @apart
    def joined_of(k, first, last):
        v = jnp.dot(
            jnp.concatenate([N[i] for i in range(3)], axis=1),
            jnp.concatenate([head_pair(i, k, first, last) for i in range(3)], axis=0),
            preferred_element_type=F32,
        )
        squares = jnp.sum(v * v, axis=0, keepdims=True)
        for i in range(last - first):
            SQ[4:5, 0:128] += squares[:, 128 * i : 128 * i + 128]
            COT[7 * k + first + i, 0:PIX, :] = v[:, 128 * i : 128 * i + 128].astype(BF)

    def heads_store(t):
        return pltpu.make_async_copy(
            COT.at[t, pl.ds(0, PIX)], heads_out.at[:, pl.ds(128 * t, 128)], in_sem.at[3 + t // 7]
        )

    def trunk_cot():
        image_wait(1)
        expand(4, False)

    def dlinear(layer):
        def one(m):
            rows, at = at48(m, 8), at48(m)
            g = ACC[rows, :] + DT[layer, at, :].astype(F32)
            ACC[rows, :] = g * GP[layer, at, :].astype(F32)

        blocks(14, one)
        if layer == 2:
            part = F3.at[1, :, pl.ds(32, PIX)]
            pltpu.make_async_copy(part, part, out_sem.at[3]).wait()
        else:
            for k in range(2):
                share_d(layer + 1, k).wait_send()
        shifts()
        for k in range(2):
            share_d(layer, k).start()

    @apart
    def conv_back(layer, a):
        v = lax.dot_general(
            jnp.concatenate(taps(a, True), axis=1),
            jnp.concatenate([weights(layer, a, b) for b in range(3)], axis=1),
            (((1,), (1,)), ((), ())),
            preferred_element_type=F32,
        )
        if a == 0:
            ACC[8 : 8 + PIX, :] = v
        else:
            ACC[8 : 8 + PIX, :] += v

    def conv_grads(layer, a):
        if a == 0:
            share_ft(layer).wait_recv()
            for k in range(2):
                share_d(layer, k).wait_recv()
            if layer == 2:
                share_nt(2).wait_send()
            if layer == 1:
                ag_end(2)
        conv_grads_of(layer, a)

    @apart
    def conv_grads_of(layer, a):
        first = 8 + HIGH * (2 - a)
        rows = slice(first, first + PAD)
        own = [F3[2 - b, 2 * k + c, rows, :] for b in range(3) for k in range(2)]
        other = [D3P[layer % 2, 2 - b, k, rows, :] for b in range(3) for k in range(2)]
        v = jnp.dot(
            jnp.concatenate([FT[layer], FTP[layer]], axis=1),
            jnp.concatenate(
                [jnp.concatenate(own, axis=1), jnp.concatenate(other, axis=1)], axis=0
            ),
            preferred_element_type=F32,
        ).astype(BF)
        ref, base = grads(layer)
        for b in range(3):
            for k in range(2):
                r = base + 4608 * k + 512 * (3 * b + a)
                at = 256 * b + 128 * k
                ref[r : r + 512, :] = v[:, at : at + 128]

    def image_store():
        return pltpu.make_async_copy(DT.at[2], image_out, out_sem.at[4])

    def image_grad():
        def one(m):
            DT[2, at48(m), :] = (ACC[at48(m, 8), :] * mask_of(m)).astype(BF)

        blocks(14, one)
        image_store().start()

    def small(i):
        return remote(LB.at[i], MR.at[i], small_send.at[i], small_recv.at[i], (pn, xn, yn)[i])

    def line(s, i, t):
        return remote(ZB.at[s], ZB.at[s], small_send.at[i], small_recv.at[5 + s], t)

    def m0():
        v = SQ[:, 0:128]
        for i in range(1, 4):
            v = v + SQ[:, 128 * i : 128 * i + 128]
        LB[0] = v
        small(0).start()

    def m1(i):
        small(i).wait_recv()
        v = LB[i] + MR[i]
        if i < 2:
            LB[i + 1] = v
            small(i + 1).start()
            return
        ZB[z] = v
        when(z < 3, lambda: line(z, 5 + z, up).start())
        when(z > 0, lambda: line(z, 9 + z, dn).start())

    def m2(j):
        s = sig[j]
        line(s, 5, up).wait_recv()
        when((s < z) & (z < 3), lambda: line(s, 5 + s, up).start())
        when((s > z) & (z > 0), lambda: line(s, 9 + s, dn).start())

    def m3():
        total = ZB[0] + ZB[1] + ZB[2] + ZB[3]
        v = jnp.sum(total, axis=1, keepdims=True)
        which = lax.broadcasted_iota(jnp.int32, (8, 1), 0)
        wide = jnp.where(which == 4, 1792.0, 512.0).astype(F32)
        rms_out[...] = jnp.broadcast_to(jnp.sqrt(v / (v[5:6] * wide)), (8, 128))

    def scale_sum(i):
        return remote(SB.at[i], SR.at[i], small_send.at[3 + i], small_recv.at[3 + i], (pn, yn)[i])

    def t0():
        scale_sum(0).start()

    def t1():
        scale_sum(0).wait_recv()
        SB[1] = SB[0] + SR[0]
        scale_sum(1).start()

    def t2():
        scale_sum(1).wait_recv()
        total = SB[1] + SR[1]
        for layer in range(3):
            v = jnp.where(diagonal(), total[:, layer : layer + 1], 0.0)
            scale_out[layer : layer + 1, :] = jnp.sum(v, axis=0, keepdims=True)

    def finish():
        for p in range(6):
            if p != 2:
                ag_end(p)
            rs_end(p)
        for i in range(3):
            share_ft(i).wait_send()
            small(i).wait_send()
            conv_store(i).wait()
        for k in range(2):
            share_d(0, k).wait_send()
            scale_sum(k).wait_send()
        for s in range(4):
            when((z < 3) & (s <= z), lambda s=s: line(s, 5 + s, up).wait_send())
            when((z > 0) & (s >= z), lambda s=s: line(s, 9 + s, dn).wait_send())
        for k in range(2):
            cot_wait(7 * k, 7, in_sem.at[3 + k])
        image_store().wait()

    fns = dict(
        start=start, ld=ld, e0=e0, f1=f1, g1=g1, gg=gg, zj=zj, lj=lj, xd=xd, yd=yd, xf=xf, yf=yf, pw=pw,
        s1=s1, s2a=s2a, s2b=s2b, s3a=s3a, s3b=s3b, s2=s2, zu=zu, zd=zd, zf=zf, ff=ff, pf=pf,
        prep_heads=prep_heads, prep_in=prep_in, prep_cot=prep_cot, ft=ft, conv=conv, act=act, nt=nt,
        head_grads=head_grads, unpack=unpack, dtap=dtap, joined=joined, trunk_cot=trunk_cot,
        dlinear=dlinear, conv_back=conv_back, conv_grads=conv_grads, image_grad=image_grad,
        m0=m0, m1=m1, m2=m2, m3=m3, t0=t0, t1=t1, t2=t2, finish=finish,
    )
    for name, *args in order:
        fns[name](*args)


def patches(feature):
    height = feature.shape[1]
    breadth = feature.shape[2]
    padded = jnp.pad(feature, ((0, 0), (1, 1), (1, 1), (0, 0)))
    pieces = [
        padded[:, down_step : down_step + height, side_step : side_step + breadth, :]
        for down_step in range(3)
        for side_step in range(3)
    ]
    return jnp.concatenate(pieces, axis=-1)


def unpatch(stacked, channels):
    images, height, breadth, _ = stacked.shape
    padded = jnp.zeros((images, height + 2, breadth + 2, channels), jnp.float32)
    for down_step in range(3):
        for side_step in range(3):
            tap_index = 3 * down_step + side_step
            padded = padded.at[
                :, down_step : down_step + height, side_step : side_step + breadth, :
            ].add(stacked[..., tap_index * channels : (tap_index + 1) * channels])
    return padded[:, 1:-1, 1:-1, :]


def activate(linear, gain_vec, offsets, valid_mask):
    return valid_mask * jax.nn.gelu(linear * gain_vec + offsets)


def tap_piece(feature, scale_vec):
    return (
        feature * lax.rsqrt(jnp.mean(feature * feature, axis=-1, keepdims=True) + 1e-05) * scale_vec
    )


def general(
    inputs,
    heights,
    widths,
    conv_weights,
    affine_scale,
    affine_shift,
    tap_scales,
    head_weights,
    trunk_cot,
    heads_cot,
):
    images, height, breadth, channels = inputs.shape
    layer_count = conv_weights.shape[0]
    row_ids = jnp.arange(height, dtype=jnp.int32)
    col_ids = jnp.arange(breadth, dtype=jnp.int32)
    valid = (row_ids[None, :, None] < heights[:, None, None]) & (
        col_ids[None, None, :] < widths[:, None, None]
    )
    valid_mask = jnp.where(valid, 1.0, 0.0).astype(jnp.float32)[..., None]
    conv_cols, head_cols = (
        lax.all_gather(conv_weights, "dp", axis=2, tiled=True),
        lax.all_gather(head_weights, "dp", axis=2, tiled=True),
    )
    conv_full, head_full, scale_full = (
        lax.all_gather(conv_cols, "fsdp", axis=1, tiled=True),
        lax.all_gather(head_cols, "fsdp", axis=1, tiled=True),
        lax.all_gather(tap_scales, "fsdp", axis=1, tiled=True),
    )
    outputs_wide = head_full.shape[2]
    feature = inputs.astype(jnp.float32) * valid_mask
    squares = [jnp.sum(feature * feature)]
    entering = inputs * valid_mask.astype(jnp.bfloat16)
    kept_in, kept_linear, kept_feature, kept_tap = ([], [], [], [])
    summed = jnp.zeros((images, height, breadth, outputs_wide), jnp.float32)
    for layer_index in range(layer_count):
        stacked = patches(entering)
        linear = jnp.einsum(
            "ghwk,kc->ghwc", stacked, conv_full[layer_index], preferred_element_type=jnp.float32
        )
        feature = activate(linear, affine_scale[layer_index], affine_shift[layer_index], valid_mask)
        tapped = tap_piece(feature, scale_full[layer_index].astype(jnp.float32)).astype(
            jnp.bfloat16
        )
        summed = summed + jnp.einsum(
            "ghwc,co->ghwo", tapped, head_full[layer_index], preferred_element_type=jnp.float32
        )
        kept_in.append(entering)
        kept_linear.append(linear)
        kept_feature.append(feature)
        kept_tap.append(tapped)
        squares.append(jnp.sum(feature * feature))
        entering = feature.astype(jnp.bfloat16)
    squares.append(jnp.sum(summed * summed))
    square_total, pixels = lax.psum((jnp.stack(squares), jnp.sum(valid_mask)), ("dp", "fsdp"))
    divisors = jnp.array([channels] * (layer_count + 1) + [outputs_wide], jnp.float32)
    rms = jnp.sqrt(square_total / (pixels * divisors))
    conv_back, head_back, scale_back = conv_full, head_full, scale_full
    grad_conv = [None] * layer_count
    grad_scale = [None] * layer_count
    grad_head = [None] * layer_count
    grad_feature = trunk_cot.astype(jnp.float32)
    for layer_index in reversed(range(layer_count)):
        grad_head[layer_index] = jnp.einsum(
            "ghwc,ghwo->co", kept_tap[layer_index], heads_cot, preferred_element_type=jnp.float32
        )
        grad_tapped = jnp.einsum(
            "ghwo,co->ghwc", heads_cot, head_back[layer_index], preferred_element_type=jnp.float32
        )
        _, pullback = jax.vjp(
            tap_piece, kept_feature[layer_index], scale_back[layer_index].astype(jnp.float32)
        )
        feature_part, scale_part = pullback(grad_tapped)
        grad_scale[layer_index] = scale_part
        grad_feature = grad_feature + feature_part
        local_act = partial(
            activate,
            gain_vec=affine_scale[layer_index],
            offsets=affine_shift[layer_index],
            valid_mask=valid_mask,
        )
        _, pullback = jax.vjp(local_act, kept_linear[layer_index])
        (grad_linear,) = pullback(grad_feature)
        low_linear = grad_linear.astype(jnp.bfloat16)
        grad_conv[layer_index] = jnp.einsum(
            "ghwk,ghwc->kc",
            patches(kept_in[layer_index]),
            low_linear,
            preferred_element_type=jnp.float32,
        )
        spread = jnp.einsum(
            "ghwc,kc->ghwk", low_linear, conv_back[layer_index], preferred_element_type=jnp.float32
        )
        grad_feature = unpatch(spread, channels)
    input_grad = (grad_feature * valid_mask).astype(jnp.bfloat16)
    stacked_conv = jnp.stack(grad_conv)
    stacked_head = jnp.stack(grad_head)
    stacked_scale = jnp.stack(grad_scale)
    dp_count = lax.axis_size("dp")
    part_conv, part_head, part_scale = (
        lax.psum_scatter(
            stacked_conv.astype(jnp.bfloat16), "fsdp", scatter_dimension=1, tiled=True
        ).astype(jnp.float32),
        lax.psum_scatter(
            stacked_head.astype(jnp.bfloat16), "fsdp", scatter_dimension=1, tiled=True
        ).astype(jnp.float32),
        lax.psum_scatter(
            stacked_scale.astype(jnp.bfloat16), "fsdp", scatter_dimension=1, tiled=True
        ).astype(jnp.float32),
    )
    spread_scale = jnp.broadcast_to(part_scale[:, :, None], part_scale.shape + (dp_count,))
    conv_grad, head_grad, scale_cols = (
        lax.psum_scatter(
            part_conv.astype(jnp.bfloat16), "dp", scatter_dimension=2, tiled=True
        ).astype(jnp.float32),
        lax.psum_scatter(
            part_head.astype(jnp.bfloat16), "dp", scatter_dimension=2, tiled=True
        ).astype(jnp.float32),
        lax.psum_scatter(
            spread_scale.astype(jnp.bfloat16), "dp", scatter_dimension=2, tiled=True
        ).astype(jnp.float32),
    )
    scale_grad = scale_cols[:, :, 0]
    trunk_out = kept_feature[-1].astype(jnp.bfloat16)
    heads_out = summed.astype(jnp.bfloat16)
    return (trunk_out, heads_out, input_grad, conv_grad, scale_grad, head_grad, rms)


def settle(trunk, heads, image, conv, head, scale, rms, *rest):
    trunk_to, heads_to, image_to, conv_to, head_to, scale_to, rms_to = rest[:7]
    at_trunk, at_heads, at_image, at_conv, at_head, wide, come, go = rest[7:]
    moves = [(conv, at_conv, conv_to)]
    for i in range(3):
        rows = pl.ds(224 * i, 224)
        moves.append((heads.at[rows], at_heads.at[rows], heads_to.at[rows]))
    moves += [(trunk, at_trunk, trunk_to), (image, at_image, image_to), (head, at_head, head_to)]
    fetches = [pltpu.make_async_copy(a, b, come.at[i]) for i, (a, b, _) in enumerate(moves)]
    stores = [pltpu.make_async_copy(b, c, go.at[i]) for i, (_, b, c) in enumerate(moves)]
    stores[0] = pltpu.make_async_copy(wide, conv_to, go.at[0])
    for fetch in fetches:
        fetch.start()
    scale_to[...] = scale[...]
    for i in range(5):
        rms_to[i] = rms[i, 0]
    for i, (fetch, store) in enumerate(zip(fetches, stores)):
        fetch.wait()
        if i == 0:
            wide[...] = at_conv[...].astype(F32)
        store.start()
    for store in stores:
        store.wait()


def settled(results):
    hbm = pl.BlockSpec(memory_space=pl.ANY)
    vmem = pl.BlockSpec(memory_space=pltpu.VMEM)
    smem = pl.BlockSpec(memory_space=pltpu.SMEM)
    shapes = [jax.ShapeDtypeStruct(v.shape, v.dtype) for v in results[:6]]
    shapes[3] = jax.ShapeDtypeStruct(results[3].shape, F32)
    shapes.append(jax.ShapeDtypeStruct((5,), F32))
    return pl.pallas_call(
        settle,
        name="settle",
        out_shape=shapes,
        in_specs=[hbm, hbm, hbm, hbm, hbm, vmem, smem],
        out_specs=[hbm, hbm, hbm, hbm, hbm, vmem, smem],
        scratch_shapes=[pltpu.VMEM(v.shape, v.dtype) for v in results[:5]]
        + [
            pltpu.VMEM(results[3].shape, F32),
            pltpu.SemaphoreType.DMA((7,)),
            pltpu.SemaphoreType.DMA((7,)),
        ],
        compiler_params=pltpu.CompilerParams(vmem_limit_bytes=63 * 2**20),
    )(*results)


def fused(
    inputs,
    heights,
    widths,
    conv_weights,
    affine_scale,
    affine_shift,
    tap_scales,
    head_weights,
    trunk_cot,
    heads_cot,
):
    hbm = pl.BlockSpec(memory_space=pl.ANY)
    vmem = pl.BlockSpec(memory_space=pltpu.VMEM)
    smem = pl.BlockSpec(memory_space=pltpu.SMEM)
    dma = pltpu.SemaphoreType.DMA
    ahead, back = len(ROUTES), len(BACK)

    def flat(v):
        return v[0].transpose(1, 0, 2).reshape(PIX, v.shape[3])

    results = pl.pallas_call(
        partial(kernel, ORDER),
        name="conv_block",
        out_shape=(
            jax.ShapeDtypeStruct((PIX, 512), BF),
            jax.ShapeDtypeStruct((PIX, 1792), BF),
            jax.ShapeDtypeStruct((PIX, 512), BF),
            jax.ShapeDtypeStruct((3, 576, 128), BF),
            jax.ShapeDtypeStruct((3, 64, 448), F32),
            jax.ShapeDtypeStruct((3, 64), F32),
            jax.ShapeDtypeStruct((8, 128), F32),
        ),
        in_specs=[hbm, vmem, vmem, vmem, vmem, smem, smem, hbm, hbm, hbm],
        out_specs=(hbm, hbm, hbm, hbm, vmem, vmem, vmem),
        scratch_shapes=[
            pltpu.VMEM((ROWS, 128), BF),
            pltpu.VMEM((3, 4, 832, 128), BF),
            pltpu.VMEM((3, 512, PAD), BF),
            pltpu.VMEM((3, 512, PAD), BF),
            pltpu.VMEM((2, 6 * 512, 128), BF),
            pltpu.VMEM((3, PIX, 512), BF),
            pltpu.VMEM((3, PIX, 512), BF),
            pltpu.VMEM((3, PIX, 512), BF),
            pltpu.VMEM((PIX, 128), F32),
            pltpu.VMEM((14, PAD, 128), BF),
            pltpu.VMEM((2, 4, PAD, 128), BF),
            pltpu.VMEM((16 + PAD, 512), F32),
            pltpu.VMEM((2, 3, 2, 832, 128), BF),
            pltpu.VMEM((16 * CONV_UNIT, 128), BF),
            pltpu.VMEM((3 * 16 * HEAD_UNIT, 128), BF),
            pltpu.VMEM((LAND[-1], 128), BF),
            pltpu.VMEM((3, 256, 128), BF),
            pltpu.VMEM((3, 2, 8, 64, 128), BF),
            pltpu.VMEM((8, 512), F32),
            pltpu.VMEM((3, 8, 128), F32),
            pltpu.VMEM((3, 8, 128), F32),
            pltpu.VMEM((4, 8, 128), F32),
            pltpu.VMEM((2, 64, 128), F32),
            pltpu.VMEM((2, 64, 128), F32),
            dma((ahead, 1 + max(PAIR[k] for _, _, _, k in ROUTES))),
            dma((6, 3)),
            dma((3,)),
            dma((back, 12)),
            dma((6, 3)),
            dma((14,)),
            dma((14,)),
            dma((5,)),
            dma((5,)),
            dma((9,)),
            dma((13,)),
        ],
        compiler_params=pltpu.CompilerParams(
            collective_id=0, has_side_effects=True, vmem_limit_bytes=64 * 2**20
        ),
        cost_estimate=pl.CostEstimate(
            flops=45_000_000_000, bytes_accessed=16_000_000, transcendentals=1_200_000
        ),
    )(
        conv_weights,
        head_weights,
        tap_scales,
        affine_scale,
        affine_shift,
        heights,
        widths,
        flat(inputs),
        flat(trunk_cot),
        flat(heads_cot),
    )
    trunk, heads, image, conv_grad, head_grad, scale_grad, rms = settled(results)

    def image_of(v):
        return v.reshape(28, HIGH, v.shape[1]).transpose(1, 0, 2)[None]

    return (
        image_of(trunk),
        image_of(heads),
        image_of(image),
        conv_grad,
        scale_grad,
        head_grad,
        rms,
    )


def solution(mesh):
    in_specs = (
        P(("dp", "fsdp"), None, None, None),
        P(("dp", "fsdp")),
        P(("dp", "fsdp")),
        P(None, "fsdp", "dp"),
        P(),
        P(),
        P(None, "fsdp"),
        P(None, "fsdp", "dp"),
        P(("dp", "fsdp"), None, None, None),
        P(("dp", "fsdp"), None, None, None),
    )
    out_specs = (
        P(("dp", "fsdp"), None, None, None),
        P(("dp", "fsdp"), None, None, None),
        P(("dp", "fsdp"), None, None, None),
        P(None, "fsdp", "dp"),
        P(None, "fsdp"),
        P(None, "fsdp", "dp"),
        P(),
    )
    body = fused if dict(mesh.shape) == {"dp": 4, "fsdp": 8} else general
    return jax.shard_map(body, mesh=mesh, in_specs=in_specs, out_specs=out_specs, check_vma=False)
```
